32 devices in a mesh: batch: 4 (over z), lon: 8 (over y, x, core).
Axes of the slice: x: 2, y: 2, z: 4, core: 2. Of those that a mesh axis runs over, the one named last changes fastest.
Arguments:
- fields: bfloat16 [8, 48, 64, 64], P('batch', None, 'lon'), may hold values from -6 to 6
- variable_ids: int32 [8, 48], P('batch'), may hold values from 0 to 47, each once within a row
- variable_mask: int32 [8, 48], P('batch'), may hold values from 0 to 1, as said below
- position: bfloat16 [32, 32, 1024], P('lon'), may hold values from -3 to 3
- patching: bfloat16 [1024, 192], replicated, may hold values from -3 to 3
- tagging: bfloat16 [1024, 48], replicated, may hold values from -6 to 6
- beacon: bfloat16 [1024], replicated, may hold values from -6 to 6
- keying: bfloat16 [1024, 1024], replicated, may hold values from -0.1875 to 0.1875
- valuing: bfloat16 [1024, 1024], replicated, may hold values from -0.1875 to 0.1875
- lifting: bfloat16 [1024], replicated, may hold values from -1.75 to 1.75
- merging: bfloat16 [1024, 1024], replicated, may hold values from -0.5 to 0.5
- offset: bfloat16 [1024], replicated, may hold values from -1.75 to 1.75
- scaling: bfloat16 [1024], replicated, may hold values from 0.25 to 1.75
- centre: bfloat16 [1024], replicated, may hold values from -1.75 to 1.75
- projecting: bfloat16 [1024, 3072], replicated, may hold values from -0.1875 to 0.1875
- biasing: bfloat16 [2048], replicated, may hold values from -1.75 to 1.75
- mixing: bfloat16 [1024, 1024], replicated, may hold values from -4 to 4
- nudging: bfloat16 [1024], replicated, may hold values from -1.75 to 1.75
- rescaling: bfloat16 [1024], replicated, may hold values from 0.25 to 1.75
- recentre: bfloat16 [1024], replicated, may hold values from -1.75 to 1.75
- widening: bfloat16 [1024, 4096], replicated, may hold values from -0.1875 to 0.1875
- uplift: bfloat16 [4096], replicated, may hold values from -1.75 to 1.75
- narrowing: bfloat16 [4096, 1024], replicated, may hold values from -0.09375 to 0.09375
- settle: bfloat16 [1024], replicated, may hold values from -1.75 to 1.75
- reading: bfloat16 [1024, 192], replicated, may hold values from -0.1875 to 0.1875
- baseline: bfloat16 [192], replicated, may hold values from -3 to 3
- cotangent: bfloat16 [8, 48, 64, 64], P('batch', None, 'lon'), may hold values from -6 to 6
Outputs:
- prediction: bfloat16 [8, 48, 64, 64], P('batch', None, 'lon')
- fields_gradient: float32 [8, 48, 64, 64], P('batch', None, 'lon')
- position_gradient: float32 [32, 32, 1024], P('lon')
- patching_gradient: float32 [1024, 192], P(('batch', 'lon'))
- tagging_gradient: float32 [1024, 48], P(('batch', 'lon'))
- beacon_gradient: float32 [1024], P(('batch', 'lon'))
- keying_gradient: float32 [1024, 1024], P(('batch', 'lon'))
- valuing_gradient: float32 [1024, 1024], P(('batch', 'lon'))
- lifting_gradient: float32 [1024], P(('batch', 'lon'))
- merging_gradient: float32 [1024, 1024], P(('batch', 'lon'))
- offset_gradient: float32 [1024], P(('batch', 'lon'))
- scaling_gradient: float32 [1024], P(('batch', 'lon'))
- centre_gradient: float32 [1024], P(('batch', 'lon'))
- projecting_gradient: float32 [1024, 3072], P(('batch', 'lon'))
- biasing_gradient: float32 [2048], P(('batch', 'lon'))
- mixing_gradient: float32 [1024, 1024], P(('batch', 'lon'))
- nudging_gradient: float32 [1024], P(('batch', 'lon'))
- rescaling_gradient: float32 [1024], P(('batch', 'lon'))
- recentre_gradient: float32 [1024], P(('batch', 'lon'))
- widening_gradient: float32 [1024, 4096], P(('batch', 'lon'))
- uplift_gradient: float32 [4096], P(('batch', 'lon'))
- narrowing_gradient: float32 [4096, 1024], P(('batch', 'lon'))
- settle_gradient: float32 [1024], P(('batch', 'lon'))
- reading_gradient: float32 [1024, 192], P(('batch', 'lon'))
- baseline_gradient: float32 [192], replicated
The draws below stay inside these ranges and needn't reach their ends.
Inputs may be any that keep to these rules, and one draw needn't show every extreme that they name: `variable_mask`: each item keeps between 30 and 48 of its variables; some item keeps exactly 30 and another all 48. `variable_ids`: each item's slots name every variable once.
All inputs are finite; a program needn't handle non-finite values.
Results may differ from the reference program's by a relative error of at most 0.017.
Values may be sent and summed in bfloat16 or wider, within the bound.
A program may use at most 320 MiB of HBM per device.

```python
import math
from functools import partial
import jax
import jax.numpy as jnp
from jax import lax

D = 1024
HEADS = 16
HDIM = 64
FF = 4096
NVAR = 48
NOUT = 48
MINVAR = 30
LATP = 32
ITEMS = 8
LONP = 32
SEQ = 1024
LONPIX = 64
LATPIX = 64


def mask_order(order_key):
    return jax.random.permutation(order_key, NVAR)


def draw_variable_mask(key, part):
    key = jax.random.fold_in(key, 7)
    count_key, lowest_key, highest_key, order_key = jax.random.split(key, 4)
    counts = jax.random.randint(count_key, (ITEMS,), MINVAR, NVAR + 1)
    lowest = jax.random.randint(lowest_key, (), 0, ITEMS)
    highest = (lowest + 1 + jax.random.randint(highest_key, (), 0, ITEMS - 1)) % ITEMS
    places = jnp.arange(ITEMS, dtype=jnp.int32)
    counts = jnp.where(places == lowest, MINVAR, counts)
    counts = jnp.where(places == highest, NVAR, counts)
    orders = jax.vmap(mask_order)(jax.random.split(order_key, ITEMS))
    return (orders < counts[:, None]).astype(jnp.int32)


def levels(key, shape, cuts, least, largest):
    factor_of, own = 1.0, jax.random.fold_in(key, 6)
    for axis_at, shards_of in cuts:
        draws = jnp.exp(jax.random.uniform(jax.random.fold_in(own, axis_at), (shards_of,), jnp.float32, least / len(cuts), largest / len(cuts)))
        factor_of = factor_of * jnp.repeat(draws, shape[axis_at] // shards_of).reshape([-1 if axis == axis_at else 1 for axis in range(len(shape))])
    return factor_of


def scatter_about(own_key, shape, deviation, reach, pieces=(), kind=jnp.bfloat16):
    result = deviation * jax.random.normal(own_key, shape, jnp.float32)
    if pieces:
        result = result * levels(own_key, shape, pieces, -0.22, 0.18)
    return jnp.clip(result, -reach, reach).astype(kind)


def setup_inputs(seed: int = 0) -> dict:
    arg_keys = jax.random.split(jax.random.key(seed), 28)
    return {
        "fields": scatter_about(arg_keys[0], (ITEMS, NVAR, LONPIX, LATPIX), 1.0, 6.0, ((0, 4), (2, 8))),
        "variable_ids": jax.vmap(lambda own: jax.random.permutation(own, NVAR))(jax.random.split(arg_keys[1], ITEMS)).reshape((ITEMS, NVAR)).astype(jnp.int32),
        "variable_mask": draw_variable_mask(jax.random.fold_in(arg_keys[27], 71), 0),
        "position": scatter_about(arg_keys[3], (LONP, LATP, D), 0.5, 3.0, ((0, 8),)),
        "patching": scatter_about(arg_keys[4], (D, NVAR * 4), 4 ** -0.5, 3.0),
        "tagging": scatter_about(arg_keys[5], (D, NVAR), 1.0, 6.0),
        "beacon": scatter_about(arg_keys[6], (D,), 1.0, 6.0),
        "keying": scatter_about(arg_keys[7], (D, D), D ** -0.5, 0.1875),
        "valuing": scatter_about(arg_keys[8], (D, D), D ** -0.5, 0.1875),
        "lifting": scatter_about(arg_keys[9], (D,), 0.3, 1.75),
        "merging": scatter_about(arg_keys[10], (D, D), (D // 8) ** -0.5, 0.5),
        "offset": scatter_about(arg_keys[11], (D,), 0.3, 1.75),
        "scaling": jnp.clip(1.0 + 0.15 * jax.random.normal(arg_keys[12], (D,), jnp.float32), 0.25, 1.75).astype(jnp.bfloat16),
        "centre": scatter_about(arg_keys[13], (D,), 0.3, 1.75),
        "projecting": scatter_about(arg_keys[14], (D, 3 * D), D ** -0.5, 0.1875),
        "biasing": scatter_about(arg_keys[15], (2 * D,), 0.3, 1.75),
        "mixing": scatter_about(arg_keys[16], (D, D), 2 ** -0.5, 4.0),
        "nudging": scatter_about(arg_keys[17], (D,), 0.3, 1.75),
        "rescaling": jnp.clip(1.0 + 0.15 * jax.random.normal(arg_keys[18], (D,), jnp.float32), 0.25, 1.75).astype(jnp.bfloat16),
        "recentre": scatter_about(arg_keys[19], (D,), 0.3, 1.75),
        "widening": scatter_about(arg_keys[20], (D, FF), D ** -0.5, 0.1875),
        "uplift": scatter_about(arg_keys[21], (FF,), 0.3, 1.75),
        "narrowing": scatter_about(arg_keys[22], (FF, D), FF ** -0.5, 0.09375),
        "settle": scatter_about(arg_keys[23], (D,), 0.3, 1.75),
        "reading": scatter_about(arg_keys[24], (D, NOUT * 4), D ** -0.5, 0.1875),
        "baseline": scatter_about(arg_keys[25], (NOUT * 4,), 0.5, 3.0),
        "cotangent": scatter_about(arg_keys[26], (ITEMS, NOUT, LONPIX, LATPIX), 1.0, 6.0, ((0, 4), (2, 8))),
    }


HIGH = lax.Precision.HIGHEST
EPSILON = 1e-06

@jax.custom_vjp
def low(v):
    return lax.optimization_barrier(v.astype(jnp.bfloat16)).astype(jnp.float32)

@jax.custom_vjp
def low_back(v):
    return v

def low_keep(v):
    return (low(v), None)

def low_pass(kept, grad):
    return (grad,)

def back_keep(v):
    return (v, None)

def back_low(kept, grad):
    return (low(grad),)
low.defvjp(low_keep, low_pass)
low_back.defvjp(back_keep, back_low)

def matmul(left, right):
    return jnp.dot(left, right, precision=HIGH)

def as_float(tensor):
    return tensor.astype(jnp.float32)

def layer_norm(values, scaler, shifter):
    centred = values - lax.optimization_barrier(jnp.mean(values, axis=-1, keepdims=True))
    spread = lax.optimization_barrier(jnp.mean(centred * centred, axis=-1, keepdims=True))
    return centred * lax.rsqrt(spread + EPSILON) * scaler + shifter

def to_tokens(canvas):
    shaped = canvas.reshape(canvas.shape[0], LONP, 2, LATP, 2)
    return shaped.transpose(1, 3, 0, 2, 4).reshape(SEQ, canvas.shape[0] * 4)

def from_tokens(token_rows, channels):
    shaped = token_rows.reshape(LONP, LATP, channels, 2, 2)
    return shaped.transpose(2, 0, 3, 1, 4).reshape(channels, LONPIX, LATPIX)

def to_variables(slots, order):
    return jnp.zeros_like(slots).at[order].set(slots)

def to_slots(canvas, order):
    return canvas[order]

def item_forward(params, patches, present):
    position, patching, tagging, beacon, keying, valuing, lifting, merging, offset, scaling, centre, projecting, biasing, mixing, nudging, rescaling, recentre, widening, uplift, narrowing, settle, reading, baseline = params
    factor = HDIM ** (-0.5)
    keymap = jnp.einsum('dhe,he->dh', keying.reshape(D, HEADS, HDIM), beacon.reshape(HEADS, HDIM), precision=HIGH)
    patch_map = matmul(patching.T, keymap).reshape(NVAR, 4, HEADS)
    tag_map = matmul(tagging.T, keymap)
    pixels = patches.reshape(SEQ, NVAR, 4)
    logits = (jnp.einsum('tvk,vkh->thv', pixels, patch_map, precision=HIGH) + tag_map.T[None]) * factor
    logits = jnp.where(present[None, None, :], logits, -1e+30)
    weights = jax.nn.softmax(logits, axis=-1)
    blended = (weights[:, :, :, None] * pixels[:, None]).reshape(SEQ, HEADS, NVAR * 4)
    mixture = jnp.einsum('thj,dj->thd', blended, patching, precision=HIGH) + jnp.einsum('thv,dv->thd', weights, tagging, precision=HIGH)
    pooled = jnp.einsum('thd,dhe->the', low(mixture), valuing.reshape(D, HEADS, HDIM), precision=HIGH).reshape(SEQ, D) + lifting
    embedded = low_back(matmul(low(low_back(pooled)), merging) + offset) + position.reshape(SEQ, D)
    normed = low(layer_norm(embedded, scaling, centre))
    joint_bias = jnp.concatenate([biasing[:D], jnp.zeros((D,), biasing.dtype), biasing[D:]])
    joint_rows = low(low_back(matmul(normed, projecting) + joint_bias))
    queries = joint_rows[:, :D].reshape(SEQ, HEADS, HDIM)
    key_rows = joint_rows[:, D:2 * D].reshape(SEQ, HEADS, HDIM)
    value_rows = joint_rows[:, 2 * D:].reshape(SEQ, HEADS, HDIM)
    scores = low_back(jnp.einsum('qhe,khe->hqk', queries, key_rows, precision=HIGH) * factor)
    probability = jax.nn.softmax(scores, axis=-1)
    attended = jnp.einsum('hqk,khe->qhe', low(probability), value_rows, precision=HIGH).reshape(SEQ, D)
    middle = embedded + low_back(matmul(low(low_back(attended)), mixing) + nudging)
    second = low(layer_norm(middle, rescaling, recentre))
    hidden = low_back(matmul(second, widening) + uplift)
    final_rows = middle + low_back(matmul(low(jax.nn.gelu(hidden, approximate=True)), narrowing) + settle)
    return matmul(low(final_rows), reading) + baseline

def reference(fields, variable_ids, variable_mask, position, patching, tagging, beacon, keying, valuing, lifting, merging, offset, scaling, centre, projecting, biasing, mixing, nudging, rescaling, recentre, widening, uplift, narrowing, settle, reading, baseline, cotangent):
    params = tuple(map(as_float, (position, patching, tagging, beacon, keying, valuing, lifting, merging, offset, scaling, centre, projecting, biasing, mixing, nudging, rescaling, recentre, widening, uplift, narrowing, settle, reading, baseline)))
    ordered = jax.vmap(to_variables)(fields.astype(jnp.float32), variable_ids)
    present = jax.vmap(to_variables)(variable_mask, variable_ids) > 0
    patches = jax.vmap(to_tokens)(jnp.roll(ordered, 1, axis=2))
    targets = jax.vmap(to_tokens)(jnp.roll(cotangent.astype(jnp.float32), 1, axis=2))
    group_size = math.gcd(ITEMS, max(1, 2048 // SEQ))
    groups = ITEMS // group_size

    def group_step(totals, stacked):
        patch_group, live_group, target_group = stacked

        def forward_group(weights_all, patch_rows):
            return jax.vmap(item_forward, in_axes=(None, 0, 0))(weights_all, patch_rows, live_group)
        outputs, pullback = jax.vjp(forward_group, params, patch_group)
        weight_grads, patch_grads = pullback(target_group)
        return (jax.tree.map(jnp.add, totals, weight_grads), (outputs, patch_grads))
    initial = jax.tree.map(jnp.zeros_like, params)
    shaped = (patches.reshape(groups, group_size, SEQ, NVAR * 4), present.reshape(groups, group_size, NVAR), targets.reshape(groups, group_size, SEQ, NOUT * 4))
    totals, (outputs, patch_grads) = lax.scan(group_step, initial, shaped)
    canvas = jax.vmap(partial(from_tokens, channels=NOUT))(outputs.reshape(ITEMS, SEQ, NOUT * 4))
    prediction = jnp.roll(canvas, -1, axis=2).astype(jnp.bfloat16)
    grad_canvas = jax.vmap(partial(from_tokens, channels=NVAR))(patch_grads.reshape(ITEMS, SEQ, NVAR * 4))
    fields_gradient = jax.vmap(to_slots)(jnp.roll(grad_canvas, -1, axis=2), variable_ids)
    g_position, g_patching, g_tagging, g_beacon, g_keying, g_valuing, g_lifting, g_merging, g_offset, g_scaling, g_centre, g_projecting, g_biasing, g_mixing, g_nudging, g_rescaling, g_recentre, g_widening, g_uplift, g_narrowing, g_settle, g_reading, g_baseline = totals
    return (prediction, fields_gradient, g_position, g_patching, g_tagging, g_beacon, g_keying, g_valuing, g_lifting, g_merging, g_offset, g_scaling, g_centre, g_projecting, g_biasing, g_mixing, g_nudging, g_rescaling, g_recentre, g_widening, g_uplift, g_narrowing, g_settle, g_reading, g_baseline)
```

```python
import functools

import jax
import jax.numpy as jnp
from jax import lax
from jax.experimental import pallas as pl
from jax.experimental.pallas import tpu as pltpu
from jax.sharding import PartitionSpec as P

D = 1024
HEADS = 16
HDIM = 64
FF = 4096
NVAR = 48
NOUT = 48
LATP = 32
VPAD = 64
JPAD = 5 * VPAD

HIGH = lax.Precision.HIGHEST
EPSILON = 1e-06
F32 = jnp.float32
BF16 = jnp.bfloat16
FACTOR = HDIM ** (-0.5)
MIB = 2**20


def product(left, right):
    return jnp.dot(left, right, preferred_element_type=F32)


def contract(left, right, dims):
    return lax.dot_general(left, right, (dims, ((), ())), preferred_element_type=F32)


def normalize(values):
    centred = values - jnp.mean(values, axis=-1, keepdims=True)
    inverse = lax.rsqrt(jnp.mean(centred * centred, axis=-1, keepdims=True) + EPSILON)
    return centred * inverse, inverse


def norm_back(upstream, normal, inverse, scaler):
    weighted = upstream * scaler
    return inverse * (
        weighted
        - jnp.mean(weighted, axis=-1, keepdims=True)
        - normal * jnp.mean(weighted * normal, axis=-1, keepdims=True)
    )


def gelu_parts(x):
    c = 0.7978845608028654
    t = jnp.tanh(c * (x + 0.044715 * (x * x * x)))
    value = 0.5 * x * (1.0 + t)
    slope = 0.5 * (1.0 + t) + 0.5 * x * (1.0 - t * t) * (c * (1.0 + 3 * 0.044715 * x * x))
    return value, slope


def pool_weights(patches_ref, logit_map_ref, tag_row_ref, mask_ref, weights):
    logits = jnp.dot(
        patches_ref[...].astype(F32)[:, : 4 * VPAD],
        logit_map_ref[...],
        precision=HIGH,
        preferred_element_type=F32,
    ) + tag_row_ref[...]
    mask = mask_ref[...]
    for h in range(HEADS):
        part = jnp.where(mask == 0.0, logits[:, h * VPAD : (h + 1) * VPAD], mask)
        top = jnp.max(part, axis=-1, keepdims=True)
        grown = jnp.exp(part - top)
        weights[h] = grown / jnp.sum(grown, axis=-1, keepdims=True)


def pool_fwd_kernel(patches_ref, logit_map_ref, tag_row_ref, mask_ref, pv_ref, lift_ref, out_ref, w_ref):
    pool_weights(patches_ref, logit_map_ref, tag_row_ref, mask_ref, w_ref)
    patches = patches_ref[...].astype(F32)
    for pair in range(HEADS // 2):
        halves = []
        for h in (2 * pair, 2 * pair + 1):
            w = w_ref[h]
            blended = (jnp.concatenate([w] * 5, axis=1) * patches).astype(BF16)
            halves.append(product(blended, pv_ref[:, h * HDIM : (h + 1) * HDIM]))
        cols = slice(pair * 128, pair * 128 + 128)
        out_ref[:, cols] = (jnp.concatenate(halves, axis=1) + lift_ref[:, cols]).astype(BF16)


def pool_forward(patches, logit_map, tag_row, mask, pv, lifting):
    rows = patches.shape[0]
    return pl.pallas_call(
        pool_fwd_kernel,
        out_shape=(
            jax.ShapeDtypeStruct((rows, D), BF16),
            jax.ShapeDtypeStruct((HEADS, rows, VPAD), F32),
        ),
        compiler_params=pltpu.CompilerParams(vmem_limit_bytes=48 * MIB),
        name="pool_fwd",
    )(patches, logit_map, tag_row, mask, pv, lifting)


def pool_bwd_kernel(patches_ref, w_ref, qrow_ref, pv_ref, du_ref, dpatch_ref, dpv_ref, dqz_ref):
    patches = patches_ref[...].astype(F32)
    total = jnp.zeros((patches.shape[0], 4 * VPAD), F32)
    for pair in range(HEADS // 2):
        halves = []
        for h in (2 * pair, 2 * pair + 1):
            w = w_ref[h]
            wide = jnp.concatenate([w] * 5, axis=1)
            blended = (wide * patches).astype(BF16)
            du = du_ref[:, h * HDIM : (h + 1) * HDIM]
            dbl = contract(du, pv_ref[:, h * HDIM : (h + 1) * HDIM], ((1,), (1,)))
            halves.append(contract(blended, du, ((0,), (0,))))
            x = dbl * patches
            dw = x[:, :VPAD]
            for k in range(1, 5):
                dw = dw + x[:, k * VPAD : (k + 1) * VPAD]
            da = w * (dw - jnp.sum(w * dw, axis=-1, keepdims=True)) * FACTOR
            da_wide = jnp.concatenate([da] * 5, axis=1)
            dqz_ref[h : h + 1, :] = jnp.sum(da_wide * patches, axis=0, keepdims=True)
            total = total + (
                wide[:, : 4 * VPAD] * dbl[:, : 4 * VPAD]
                + da_wide[:, : 4 * VPAD] * qrow_ref[h : h + 1, : 4 * VPAD]
            )
        dpv_ref[:, pair * 128 : pair * 128 + 128] = jnp.concatenate(halves, axis=1)
    dpatch_ref[...] = total


def pool_backward(patches, weights, qrow, pv, du):
    rows = patches.shape[0]
    return pl.pallas_call(
        pool_bwd_kernel,
        out_shape=(
            jax.ShapeDtypeStruct((rows, 4 * VPAD), F32),
            jax.ShapeDtypeStruct((JPAD, D), F32),
            jax.ShapeDtypeStruct((HEADS, JPAD), F32),
        ),
        compiler_params=pltpu.CompilerParams(vmem_limit_bytes=48 * MIB),
        name="pool_bwd",
    )(patches, weights, qrow, pv, du)


def attn_fwd_kernel(heads, q_ref, k_ref, v_ref, out_ref, lse_ref):
    outs = []
    for h in range(heads):
        cols = slice(h * HDIM, (h + 1) * HDIM)
        scores = contract(k_ref[0, :, cols], q_ref[0, :, cols], ((1,), (1,))) * FACTOR
        top = jnp.max(scores, axis=0, keepdims=True)
        grown = jnp.exp(scores - top)
        total = jnp.sum(grown, axis=0, keepdims=True)
        probs = (grown * (1.0 / total)).astype(BF16)
        outs.append(contract(probs, v_ref[0, :, cols], ((0,), (0,))))
        lse_ref[0, h : h + 1, :] = top + jnp.log(total)
    out_ref[0] = jnp.concatenate(outs, axis=1).astype(BF16) if heads > 1 else outs[0].astype(BF16)


def attn_forward(q, k, v, heads, tile):
    items, seq, width = q.shape
    return pl.pallas_call(
        functools.partial(attn_fwd_kernel, heads),
        grid=(items, seq // tile),
        in_specs=[
            pl.BlockSpec((1, tile, width), lambda i, t: (i, t, 0)),
            pl.BlockSpec((1, seq, width), lambda i, t: (i, 0, 0)),
            pl.BlockSpec((1, seq, width), lambda i, t: (i, 0, 0)),
        ],
        out_specs=(
            pl.BlockSpec((1, tile, width), lambda i, t: (i, t, 0)),
            pl.BlockSpec((1, heads, tile), lambda i, t: (i, 0, t)),
        ),
        out_shape=(
            jax.ShapeDtypeStruct((items, seq, width), BF16),
            jax.ShapeDtypeStruct((items, heads, seq), F32),
        ),
        compiler_params=pltpu.CompilerParams(vmem_limit_bytes=56 * MIB),
        name="attn_fwd",
    )(q, k, v)


def attn_bwd_kernel(heads, q_ref, k_ref, v_ref, do_ref, lse_ref, dq_ref, dk_ref, dv_ref, dk_acc, dv_acc):
    tile = pl.program_id(1)

    @pl.when(tile == 0)
    def _():
        dk_acc[...] = jnp.zeros_like(dk_acc)
        dv_acc[...] = jnp.zeros_like(dv_acc)

    for h in range(heads):
        cols = slice(h * HDIM, (h + 1) * HDIM)
        q, k, v, do = q_ref[0, :, cols], k_ref[0, :, cols], v_ref[0, :, cols], do_ref[0, :, cols]
        scores = contract(k, q, ((1,), (1,))) * FACTOR
        probs = jnp.exp(scores - lse_ref[0, h : h + 1, :])
        dprobs = contract(v, do, ((1,), (1,)))
        delta = jnp.sum(probs * dprobs, axis=0, keepdims=True)
        dscores = (probs * (dprobs - delta)).astype(BF16)
        dv_acc[h] += product(probs.astype(BF16), do)
        dk_acc[h] += product(dscores, q)
        dq_ref[0, :, cols] = (contract(dscores, k, ((0,), (0,))) * FACTOR).astype(BF16)

    @pl.when(tile == pl.num_programs(1) - 1)
    def _():
        for h in range(heads):
            cols = slice(h * HDIM, (h + 1) * HDIM)
            dk_ref[0, :, cols] = (dk_acc[h] * FACTOR).astype(BF16)
            dv_ref[0, :, cols] = dv_acc[h].astype(BF16)


def attn_backward(q, k, v, do, lse, heads, tile):
    items, seq, width = q.shape
    tiled = pl.BlockSpec((1, tile, width), lambda i, t: (i, t, 0))
    full = pl.BlockSpec((1, seq, width), lambda i, t: (i, 0, 0))
    shape = jax.ShapeDtypeStruct((items, seq, width), BF16)
    return pl.pallas_call(
        functools.partial(attn_bwd_kernel, heads),
        grid=(items, seq // tile),
        in_specs=[tiled, full, full, tiled, pl.BlockSpec((1, heads, tile), lambda i, t: (i, 0, t))],
        out_specs=(tiled, full, full),
        out_shape=(shape, shape, shape),
        scratch_shapes=[pltpu.VMEM((heads, seq, HDIM), F32), pltpu.VMEM((heads, seq, HDIM), F32)],
        compiler_params=pltpu.CompilerParams(vmem_limit_bytes=56 * MIB),
        name="attn_bwd",
    )(q, k, v, do, lse)


def per_device(
    fields, variable_ids, variable_mask, position, patching, tagging, beacon, keying, valuing, lifting,
    merging, offset, scaling, centre, projecting, biasing, mixing, nudging, rescaling, recentre,
    widening, uplift, narrowing, settle, reading, baseline, cotangent,
):
    count, lon = lax.axis_size("batch"), lax.axis_size("lon")
    zi, li = lax.axis_index("batch"), lax.axis_index("lon")
    block = zi * lon + li
    items, cols_dev, lat = fields.shape[0], fields.shape[2], fields.shape[3]
    upatch = cols_dev // 2
    here = upatch * LATP
    rows = items * here
    own_heads = HEADS // lon
    width = own_heads * HDIM
    rows_dev = D // (count * lon)
    f = lambda a: a.astype(F32)

    canvas = jnp.stack([fields, cotangent])
    edge = lax.ppermute(canvas[:, :, :, -1:, :], "lon", [(i, (i + 1) % lon) for i in range(lon)])
    canvas = jnp.concatenate([edge, canvas[:, :, :, :-1, :]], axis=3)

    q_at = jnp.arange(lat)
    spread = ((q_at[:, None] % 2) * LATP + q_at[:, None] // 2 == q_at[None, :]).astype(BF16)
    choose = (variable_ids[:, :, None] == jnp.arange(VPAD, dtype=jnp.int32)[None, None, :]).astype(BF16)
    ordered = jnp.einsum("bsv,bswq->bwvq", choose, canvas[0], preferred_element_type=F32).astype(BF16)
    ptok = jnp.einsum("bwvq,qc->bwcv", ordered, spread, preferred_element_type=F32).astype(BF16)
    ptok = ptok.reshape(items, upatch, 2, 2, LATP, VPAD).transpose(0, 1, 4, 2, 3, 5).reshape(rows, 4 * VPAD)
    patches = jnp.concatenate([ptok, jnp.ones((rows, VPAD), BF16)], axis=1)
    ytok = jnp.einsum("bowq,qc->bwco", canvas[1], spread, preferred_element_type=F32).astype(BF16)
    dpred = ytok.reshape(items, upatch, 2, 2, LATP, NOUT).transpose(0, 1, 4, 2, 3, 5).reshape(rows, 4 * NOUT)
    live = jnp.einsum("bs,bsv->bv", variable_mask.astype(BF16), choose, preferred_element_type=F32) > 0.5
    lane = jnp.arange(VPAD)[None, :]
    mask = jnp.where(lane < NVAR, jnp.where(live, 0.0, -1e30), -2e30)
    mask = jnp.broadcast_to(mask[:, None, :], (items, here, VPAD)).reshape(rows, VPAD)

    source = jnp.concatenate([jnp.arange(NVAR * 4) % 4 * VPAD + jnp.arange(NVAR * 4) // 4, 4 * VPAD + jnp.arange(NVAR)])
    place = (source[:, None] == jnp.arange(JPAD)[None, :]).astype(BF16)
    embed = product(jnp.concatenate([patching, tagging], axis=1), place).astype(BF16)
    pv = contract(embed, valuing, ((0,), (0,))).astype(BF16)
    head_of = (jnp.arange(D)[:, None] // HDIM == jnp.arange(HEADS)[None, :])
    keymap = product(keying, jnp.where(head_of, beacon[:, None], jnp.zeros((), BF16)))
    qmap = jnp.dot(f(embed).T, keymap, precision=HIGH)
    same = (jnp.arange(4 * VPAD)[:, None] % VPAD == jnp.arange(VPAD)[None, :])
    logit_map = jnp.where(same[:, None, :], qmap[: 4 * VPAD, :, None], 0.0).reshape(4 * VPAD, HEADS * VPAD) * FACTOR
    tag_row = (qmap[4 * VPAD :, :].T * FACTOR).reshape(1, HEADS * VPAD)

    pooled, pool_w = pool_forward(patches, logit_map, tag_row, mask, pv, f(lifting)[None, :])
    placed = jnp.broadcast_to(f(position).reshape(1, here, D), (items, here, D)).reshape(rows, D)
    embedded = product(pooled, merging) + f(offset) + placed
    normal_one, inverse_one = normalize(embedded)
    normed = (normal_one * f(scaling) + f(centre)).astype(BF16)

    normed_all = lax.all_gather(normed.reshape(items, here, D), "lon", axis=1, tiled=True)
    seq = normed_all.shape[1]
    own = lax.dynamic_slice(projecting.reshape(D, 3, lon, width), (0, 0, li, 0), (D, 3, 1, width)).reshape(D, 3 * width)
    joint_bias = jnp.concatenate([biasing[:D], jnp.zeros((D,), BF16), biasing[D:]]).reshape(3, lon, width)
    own_bias = lax.dynamic_slice(joint_bias, (0, li, 0), (3, 1, width)).reshape(3 * width)
    joint = (product(normed_all.reshape(items * seq, D), own) + f(own_bias)).astype(BF16).reshape(items, seq, 3 * width)
    q, k, v = joint[:, :, :width], joint[:, :, width : 2 * width], joint[:, :, 2 * width :]
    attended, lse = attn_forward(q, k, v, own_heads, 512)

    def heads_to_tokens(a):
        w = a.shape[-1]
        a = lax.all_to_all(a.reshape(items, lon, here, w), "lon", 1, 1, tiled=True)
        return a.transpose(0, 2, 1, 3).reshape(rows, lon * w)

    def tokens_to_heads(a):
        w = a.shape[-1] // lon
        a = lax.all_to_all(a.reshape(items, here, lon, w).transpose(0, 2, 1, 3), "lon", 1, 1, tiled=True)
        return a.reshape(items, seq, w)

    attended_low = heads_to_tokens(attended)
    middle = embedded + (product(attended_low, mixing) + f(nudging))
    normal_two, inverse_two = normalize(middle)
    second = (normal_two * f(rescaling) + f(recentre)).astype(BF16)
    second_all = lax.all_gather(second, "lon", axis=0, tiled=True)
    activated, slope = gelu_parts(product(second, widening) + f(uplift))
    activated = activated.astype(BF16)
    final = (middle + (product(activated, narrowing) + f(settle))).astype(BF16)

    corner = jnp.arange(NOUT * 4)
    shuffle = ((corner % 4) * NOUT + corner // 4)[:, None] == corner[None, :]
    shuffle = shuffle.astype(BF16)
    reading_p = product(reading, shuffle).astype(BF16)
    baseline_p = product(baseline[None, :], shuffle)
    outputs = product(final, reading_p) + baseline_p
    canvas_out = outputs.astype(BF16).reshape(items, upatch, LATP, 2, 2, NOUT).transpose(0, 1, 3, 5, 4, 2)
    canvas_out = canvas_out.reshape(items, cols_dev, NOUT, lat)
    predicted = jnp.einsum("bwoc,qc->bowq", canvas_out, spread, preferred_element_type=F32).astype(BF16)
    folded = lax.ppermute(predicted[:, :, :1, :], "lon", [(i, (i - 1) % lon) for i in range(lon)])
    prediction = jnp.concatenate([predicted[:, :, 1:, :], folded], axis=2)

    baseline_local = jnp.sum(f(dpred), axis=0)
    reading_grad = contract(final, dpred, ((0,), (0,)))
    dfinal = contract(dpred, reading_p, ((1,), (1,)))
    dfinal_low = dfinal.astype(BF16)
    upstream_all = lax.all_gather(dfinal_low, "lon", axis=0, tiled=True)
    settle_local = jnp.sum(f(dfinal_low), axis=0)
    dhidden = (contract(dfinal_low, narrowing, ((1,), (1,))) * slope).astype(BF16)
    uplift_local = jnp.sum(f(dhidden), axis=0)
    dsecond = contract(dhidden, widening, ((1,), (1,)))
    rescaling_local = jnp.sum(dsecond * normal_two, axis=0)
    recentre_local = jnp.sum(dsecond, axis=0)
    dmiddle = dfinal + norm_back(dsecond, normal_two, inverse_two, f(rescaling))
    dmiddle_low = dmiddle.astype(BF16)
    nudging_local = jnp.sum(f(dmiddle_low), axis=0)
    mixing_grad = contract(attended_low, dmiddle_low, ((0,), (0,)))
    dattended = contract(dmiddle_low, mixing, ((1,), (1,))).astype(BF16)

    hid = FF // (count * lon)
    wide_own = lax.dynamic_slice(widening.reshape(D, count, lon, hid), (0, 0, li, 0), (D, count, 1, hid)).reshape(D, count * hid)
    narrow_own = lax.dynamic_slice(narrowing.reshape(count, lon, hid, D), (0, li, 0, 0), (count, 1, hid, D)).reshape(count * hid, D)
    uplift_own = lax.dynamic_slice(uplift.reshape(count, lon, hid), (0, li, 0), (count, 1, hid)).reshape(count * hid)
    value_own, slope_own = gelu_parts(product(second_all, wide_own) + f(uplift_own))
    dhidden_own = (contract(upstream_all, narrow_own, ((1,), (1,))) * slope_own).astype(BF16)
    narrowing_own = contract(value_own.astype(BF16), upstream_all, ((0,), (0,)))
    widening_own = contract(second_all, dhidden_own, ((0,), (0,)))
    narrowing_gradient = f(lax.psum_scatter(narrowing_own.astype(BF16), "batch", scatter_dimension=0, tiled=True))

    do = tokens_to_heads(dattended)
    dq, dk, dv = attn_backward(q, k, v, do, lse, own_heads, 512)
    djoint_own = jnp.concatenate([dq, dk, dv], axis=2)
    projecting_own = contract(normed_all.reshape(items * seq, D), djoint_own.reshape(items * seq, 3 * width), ((0,), (0,)))
    columns_own = jnp.concatenate([widening_own, projecting_own], axis=1).astype(BF16)
    columns_own = lax.psum_scatter(columns_own, "batch", scatter_dimension=0, tiled=True)
    columns_own = lax.all_to_all(columns_own.reshape(lon, rows_dev, -1), "lon", 0, 0, tiled=True)
    widening_gradient = f(columns_own[:, :, : count * hid].reshape(lon, rows_dev, count, hid).transpose(1, 2, 0, 3).reshape(rows_dev, FF))
    projecting_gradient = f(columns_own[:, :, count * hid :].reshape(lon, rows_dev, 3, width).transpose(1, 2, 0, 3).reshape(rows_dev, 3 * D))

    djoint = heads_to_tokens(djoint_own).reshape(rows, lon, 3, width).transpose(0, 2, 1, 3).reshape(rows, 3 * D)
    djoint_sum = jnp.sum(f(djoint), axis=0)
    dnormed = contract(djoint, projecting, ((1,), (1,)))
    scaling_local = jnp.sum(dnormed * normal_one, axis=0)
    centre_local = jnp.sum(dnormed, axis=0)
    dembedded = dmiddle + norm_back(dnormed, normal_one, inverse_one, f(scaling))
    position_local = jnp.sum(dembedded.reshape(items, here, D), axis=0)
    position_gradient = f(lax.psum(position_local.astype(BF16), "batch")).reshape(upatch, LATP, D)
    dembedded_low = dembedded.astype(BF16)
    offset_local = jnp.sum(f(dembedded_low), axis=0)
    merging_grad = contract(pooled, dembedded_low, ((0,), (0,)))
    dpooled = contract(dembedded_low, merging, ((1,), (1,))).astype(BF16)
    lifting_local = jnp.sum(f(dpooled), axis=0)
    dpatch, dpv, dqz = pool_backward(patches, pool_w, qmap.T, pv, dpooled)

    squares = jnp.concatenate([merging_grad, mixing_grad, reading_grad], axis=1).astype(BF16)
    squares = squares.reshape(count, lon, rows_dev, -1)
    squares = lax.psum_scatter(squares, "lon", scatter_dimension=1, tiled=True)
    squares = f(lax.psum_scatter(squares, "batch", scatter_dimension=0, tiled=True)).reshape(rows_dev, -1)
    merging_gradient, mixing_gradient = squares[:, :D], squares[:, D : 2 * D]
    reading_gradient = jnp.dot(squares[:, 2 * D :], f(shuffle).T, precision=HIGH)

    vectors = jnp.concatenate([
        lifting_local, offset_local, scaling_local, centre_local, djoint_sum[:D], djoint_sum[2 * D :],
        nudging_local, rescaling_local, recentre_local, settle_local, uplift_local, baseline_local, dqz.reshape(-1),
    ])
    vectors = lax.psum(lax.psum(vectors, "lon"), "batch")
    dpv = lax.psum(lax.psum(dpv.astype(BF16), "lon"), "batch")
    dqz = vectors[14 * D + 4 * NOUT :].reshape(HEADS, JPAD)

    def mine(a, size):
        return lax.dynamic_slice_in_dim(a, block * size, size, 0)

    vec = lambda i: mine(vectors[i * D : (i + 1) * D], rows_dev)
    biasing_gradient = mine(vectors[4 * D : 6 * D], 2 * rows_dev)
    uplift_gradient = mine(vectors[10 * D : 14 * D], 4 * rows_dev)
    baseline_gradient = jnp.dot(vectors[None, 14 * D : 14 * D + 4 * NOUT], f(shuffle).T, precision=HIGH)[0]

    embed_mine = mine(embed, rows_dev)
    valuing_gradient = product(embed_mine, dpv)
    dembed = contract(mine(valuing, rows_dev), dpv, ((1,), (1,))) + jnp.dot(mine(keymap, rows_dev), dqz, precision=HIGH)
    dembed = jnp.dot(dembed, f(place).T, precision=HIGH)
    patching_gradient, tagging_gradient = dembed[:, : 4 * NVAR], dembed[:, 4 * NVAR :]
    dkeymap = jnp.dot(f(embed), dqz.T, precision=HIGH)
    keying_gradient = jnp.repeat(mine(dkeymap, rows_dev), HDIM, axis=1) * f(beacon)
    beacon_all = jnp.sum(jnp.repeat(dkeymap, HDIM, axis=1) * f(keying), axis=0)
    beacon_gradient = mine(beacon_all, rows_dev)

    dcan = dpatch.reshape(items, upatch, LATP, 2, 2, VPAD).transpose(0, 1, 3, 5, 4, 2).reshape(items, cols_dev, VPAD, lat)
    dslots = jnp.einsum("bwvc,qc->bwvq", dcan, f(spread), precision=HIGH)
    dslots = jnp.einsum("bsv,bwvq->bswq", f(choose), dslots, precision=HIGH)
    returned = lax.ppermute(dslots[:, :, :1, :], "lon", [(i, (i - 1) % lon) for i in range(lon)])
    fields_gradient = jnp.concatenate([dslots[:, :, 1:, :], returned], axis=2)

    return (
        prediction, fields_gradient, position_gradient, patching_gradient, tagging_gradient, beacon_gradient,
        keying_gradient, valuing_gradient, vec(0), merging_gradient, vec(1), vec(2), vec(3), projecting_gradient,
        biasing_gradient, mixing_gradient, vec(6), vec(7), vec(8), widening_gradient, uplift_gradient,
        narrowing_gradient, vec(9), reading_gradient, baseline_gradient,
    )


def solution(mesh):
    both = ("batch", "lon")
    image, matrix, vector = P("batch", None, "lon", None), P(both, None), P(both)
    return jax.shard_map(
        per_device,
        mesh=mesh,
        in_specs=(image, P("batch", None), P("batch", None), P("lon", None, None)) + (P(),) * 22 + (image,),
        out_specs=(
            image, image, P("lon", None, None), matrix, matrix, vector, matrix, matrix, vector, matrix, vector,
            vector, vector, matrix, vector, matrix, vector, vector, vector, matrix, vector, matrix, vector, matrix, P(),
        ),
        check_vma=False,
    )
```

```python
import functools

import jax
import jax.numpy as jnp
from jax import lax
from jax.experimental import pallas as pl
from jax.experimental.pallas import tpu as pltpu
from jax.sharding import PartitionSpec as P

D = 1024
HEADS = 16
HDIM = 64
FF = 4096
NVAR = 48
NOUT = 48
LATP = 32
VPAD = 64
JPAD = 5 * VPAD

HIGH = lax.Precision.HIGHEST
EPSILON = 1e-06
F32 = jnp.float32
BF16 = jnp.bfloat16
FACTOR = HDIM ** (-0.5)
MIB = 2**20
MESH = pl.DeviceIdType.MESH


def product(left, right):
    return jnp.dot(left, right, preferred_element_type=F32)


def contract(left, right, dims):
    return lax.dot_general(left, right, (dims, ((), ())), preferred_element_type=F32)


def normalize(values):
    centred = values - jnp.mean(values, axis=-1, keepdims=True)
    inverse = lax.rsqrt(jnp.mean(centred * centred, axis=-1, keepdims=True) + EPSILON)
    return centred * inverse, inverse


def norm_back(upstream, normal, inverse, scaler):
    weighted = upstream * scaler
    return inverse * (
        weighted
        - jnp.mean(weighted, axis=-1, keepdims=True)
        - normal * jnp.mean(weighted * normal, axis=-1, keepdims=True)
    )


def gelu_parts(x):
    c = 0.7978845608028654
    t = jnp.tanh(c * (x + 0.044715 * (x * x * x)))
    value = 0.5 * x * (1.0 + t)
    slope = 0.5 * (1.0 + t) + 0.5 * x * (1.0 - t * t) * (c * (1.0 + 3 * 0.044715 * x * x))
    return value, slope


def pool_weights(patches_ref, logit_map_ref, tag_row_ref, mask_ref, weights):
    logits = jnp.dot(
        patches_ref[...].astype(F32)[:, : 4 * VPAD],
        logit_map_ref[...],
        precision=HIGH,
        preferred_element_type=F32,
    ) + tag_row_ref[...]
    mask = mask_ref[...]
    for h in range(HEADS):
        part = jnp.where(mask == 0.0, logits[:, h * VPAD : (h + 1) * VPAD], mask)
        top = jnp.max(part, axis=-1, keepdims=True)
        grown = jnp.exp(part - top)
        weights[h] = grown / jnp.sum(grown, axis=-1, keepdims=True)


def pool_fwd_kernel(patches_ref, logit_map_ref, tag_row_ref, mask_ref, pv_ref, lift_ref, out_ref, w_ref):
    pool_weights(patches_ref, logit_map_ref, tag_row_ref, mask_ref, w_ref)
    patches = patches_ref[...].astype(F32)
    for pair in range(HEADS // 2):
        halves = []
        for h in (2 * pair, 2 * pair + 1):
            w = w_ref[h]
            blended = (jnp.concatenate([w] * 5, axis=1) * patches).astype(BF16)
            halves.append(product(blended, pv_ref[:, h * HDIM : (h + 1) * HDIM]))
        cols = slice(pair * 128, pair * 128 + 128)
        out_ref[:, cols] = (jnp.concatenate(halves, axis=1) + lift_ref[:, cols]).astype(BF16)


def pool_forward(patches, logit_map, tag_row, mask, pv, lifting):
    rows = patches.shape[0]
    return pl.pallas_call(
        pool_fwd_kernel,
        out_shape=(
            jax.ShapeDtypeStruct((rows, D), BF16),
            jax.ShapeDtypeStruct((HEADS, rows, VPAD), F32),
        ),
        compiler_params=pltpu.CompilerParams(vmem_limit_bytes=48 * MIB),
        name="pool_fwd",
    )(patches, logit_map, tag_row, mask, pv, lifting)


def barrier_all(n, li):
    sem = pltpu.get_barrier_semaphore()
    for mask in range(1, n):
        pl.semaphore_signal(sem, inc=1, device_id={"lon": li ^ mask}, device_id_type=MESH)
    pl.semaphore_wait(sem, n - 1)


class Gather:
    def __init__(self, n, li, at, send, recv):
        self.n, self.li, self.at, self.send, self.recv = n, li, at, send, recv
        self.bits = [1 << i for i in range(1, n.bit_length() - 1)]

    def order(self, piece):
        return self.bits if piece % 2 == 0 else self.bits[::-1]

    def copy(self, mask, piece):
        bit = 1 if mask & 1 else [b for b in self.order(piece) if b & mask][-1]
        return pltpu.make_async_remote_copy(
            src_ref=self.at(mask ^ bit, piece),
            dst_ref=self.at(mask, piece),
            send_sem=self.send.at[mask, piece],
            recv_sem=self.recv.at[mask, piece],
            device_id={"lon": self.li ^ bit},
            device_id_type=MESH,
        )

    def forward(self, mask, piece):
        order = self.order(piece)
        used = [i for i, b in enumerate(order) if b & mask]
        for b in order[(used[-1] + 1 if used else 0):]:
            self.copy(mask | b, piece).start()
        self.copy(mask | 1, piece).start()

    def start(self, pieces):
        for piece in pieces:
            self.forward(0, piece)

    def evens(self):
        return sorted(range(2, self.n, 2), key=lambda m: bin(m).count("1"))

    def relay(self, pieces):
        for mask in self.evens():
            for piece in pieces:
                self.copy(mask, piece).wait_recv()
                self.forward(mask, piece)

    def finish(self, pieces):
        for mask in range(1, self.n, 2):
            for piece in pieces:
                self.copy(mask, piece).wait_recv()

    def drain(self, pieces):
        for mask in range(1, self.n):
            for piece in pieces:
                self.copy(mask, piece).wait_send()


def front_kernel(
    n, items, here, heads, normed_ref, w_ref, b_ref, att_ref, all_out, qkv_ref, lse_ref,
    rows_ref, obuf, land, gsend, grecv, osend, orecv, keep,
):
    li = lax.axis_index("lon")
    width = heads * HDIM
    seq = n * here
    tile = min(seq, 512)
    barrier_all(n, li)
    half = here // 2

    def at(slot, piece):
        return rows_ref.at[piece // 2, slot, pl.ds((piece % 2) * half, half)]

    gather = Gather(n, li, at, gsend, grecv)
    rows_ref[:, 0] = normed_ref[...]
    gather.start([0, 1])

    def give(i, mask):
        return pltpu.make_async_remote_copy(
            src_ref=obuf.at[i, mask],
            dst_ref=land.at[li, i],
            send_sem=osend.at[i, mask],
            recv_sem=orecv.at[i, mask],
            device_id={"lon": li ^ mask},
            device_id_type=MESH,
        )

    for i in range(items):
        pieces = [2 * i, 2 * i + 1]
        later = [2 * i + 2, 2 * i + 3] if i + 1 < items else []
        if i == 0:
            gather.relay(pieces)
        gather.start(later)
        gather.finish(pieces)
        pltpu.make_async_copy(rows_ref.at[i], all_out.at[i], keep.at[i]).start()
        joint = product(rows_ref[i].reshape(seq, D), w_ref[...]) + b_ref[...]
        qkv_ref[i] = joint.astype(BF16)
        for t in range(seq // tile):
            outs = []
            for h in range(heads):
                q = qkv_ref[i, t * tile : (t + 1) * tile, h * HDIM : (h + 1) * HDIM] * FACTOR
                k = qkv_ref[i, :, width + h * HDIM : width + (h + 1) * HDIM]
                v = qkv_ref[i, :, 2 * width + h * HDIM : 2 * width + (h + 1) * HDIM]
                scores = contract(q, k, ((1,), (1,)))
                top = jnp.max(scores, axis=1, keepdims=True)
                grown = jnp.exp(scores - top)
                total = jnp.sum(grown, axis=1, keepdims=True)
                outs.append(product(grown.astype(BF16), v) / total)
                lse = top + jnp.log(total)
                lse_ref[i, h : h + 1, t * tile : (t + 1) * tile] = jnp.transpose(lse)
                if t == 0 and h == 0:
                    gather.relay(later)
            out = jnp.concatenate(outs, axis=1) if heads > 1 else outs[0]
            obuf[i, t * (tile // here) : (t + 1) * (tile // here)] = out.astype(BF16).reshape(tile // here, here, width)
        for mask in range(1, n):
            give(i, mask).start()
        land[li, i] = obuf[i, 0]
    for i in range(items):
        for mask in range(1, n):
            give(i, mask).wait_recv()
        att_ref[i * here : (i + 1) * here, :] = jnp.concatenate([land[g, i] for g in range(n)], axis=1)
    for i in range(items):
        gather.drain([2 * i, 2 * i + 1])
        for mask in range(1, n):
            give(i, mask).wait_send()
        pltpu.make_async_copy(rows_ref.at[i], all_out.at[i], keep.at[i]).wait()


def front(normed, w, b, n, items, here, heads):
    width = heads * HDIM
    seq = n * here
    vm = pl.BlockSpec(memory_space=pltpu.VMEM)
    return pl.pallas_call(
        functools.partial(front_kernel, n, items, here, heads),
        in_specs=[vm, vm, vm],
        out_specs=(vm, pl.BlockSpec(memory_space=pl.ANY), vm, vm),
        out_shape=(
            jax.ShapeDtypeStruct((items * here, D), BF16),
            jax.ShapeDtypeStruct((items, n, here, D), BF16),
            jax.ShapeDtypeStruct((items, seq, 3 * width), BF16),
            jax.ShapeDtypeStruct((items, heads, seq), F32),
        ),
        scratch_shapes=[
            pltpu.VMEM((items, n, here, D), BF16),
            pltpu.VMEM((items, n, here, width), BF16),
            pltpu.VMEM((n, items, here, width), BF16),
            pltpu.SemaphoreType.DMA((n, 2 * items)),
            pltpu.SemaphoreType.DMA((n, 2 * items)),
            pltpu.SemaphoreType.DMA((items, n)),
            pltpu.SemaphoreType.DMA((items, n)),
            pltpu.SemaphoreType.DMA((items,)),
        ],
        compiler_params=pltpu.CompilerParams(collective_id=1, has_side_effects=True, vmem_limit_bytes=56 * MIB),
        name="front",
    )(normed, w, b)


def middle_kernel(
    n, items, here, heads, hidden_own, block,
    att_ref, emb_ref, mix_hbm, vec_ref, upl_ref, uplown_ref, w1_hbm, w2_hbm, read_ref, base_ref, dpred_ref,
    up_hbm, wown_hbm, nown_hbm,
    z_ref, sq_ref, narg_ref, widg_ref, dmid_ref, do_ref, vecg_ref, uplg_ref,
    w1, w2, mix, wown, nown, up, rows_ref, normal_ref, acc, slope_ref, dobuf, accn, accw,
    gsend, grecv, osend, orecv, load,
):
    li = lax.axis_index("lon")
    rows = items * here
    width = heads * HDIM
    blocks = FF // block

    def fetch1(b):
        return pltpu.make_async_copy(w1_hbm.at[:, pl.ds(pl.multiple_of(b * block, block), block)], w1.at[b], load.at[b])

    def fetch2(b):
        return pltpu.make_async_copy(w2_hbm.at[pl.ds(pl.multiple_of(b * block, block), block)], w2.at[b], load.at[blocks + b])

    fetch_mix = pltpu.make_async_copy(mix_hbm, mix, load.at[2 * blocks])
    fetch_mix.start()
    for b in range(blocks):
        fetch1(b).start()
        fetch2(b).start()
    extra = [pltpu.make_async_copy(wown_hbm, wown, load.at[2 * blocks + 1]), pltpu.make_async_copy(nown_hbm, nown, load.at[2 * blocks + 2])]
    extra += [pltpu.make_async_copy(up_hbm.at[li ^ m], up.at[m], load.at[2 * blocks + 3 + m]) for m in range(n)]
    for c in extra:
        c.start()
    barrier_all(n, li)

    nudging, rescaling, recentre, settle = (vec_ref[i : i + 1, :] for i in range(4))
    half = rows // 2
    gather = Gather(n, li, lambda slot, piece: rows_ref.at[slot, pl.ds(piece * half, half)], gsend, grecv)
    fetch_mix.wait()
    mid = emb_ref[...] + (product(att_ref[...], mix[...]) + nudging)
    dmid_ref[...] = mid
    normal, inverse = normalize(mid)
    normal_ref[...] = normal
    rows_ref[0] = (normal * rescaling + recentre).astype(BF16)
    gather.start([0, 1])
    acc[...] = jnp.zeros_like(acc)

    def ahead(b, _):
        fetch1(b).wait()
        hidden = product(rows_ref[0], w1[b]) + upl_ref[b]
        value, slope = gelu_parts(hidden)
        slope_ref[b] = slope
        fetch2(b).wait()
        acc[...] += product(value.astype(BF16), w2[b])
        return 0

    lax.fori_loop(0, blocks // 2, ahead, 0)
    gather.relay([0, 1])
    lax.fori_loop(blocks // 2, blocks, ahead, 0)
    final = (dmid_ref[...] + (acc[...] + settle)).astype(BF16)
    z_ref[...] = (product(final, read_ref[...]) + base_ref[...]).astype(BF16)
    dpred = dpred_ref[...]
    sq_ref[:, D:] = jnp.zeros((D, sq_ref.shape[1] - D), BF16)
    sq_ref[:, D : D + 4 * NOUT] = contract(final, dpred, ((0,), (0,))).astype(BF16)
    dfinal = contract(dpred, read_ref[...], ((1,), (1,)))
    dfinal_low = dfinal.astype(BF16)
    acc[...] = jnp.zeros_like(acc)

    def back(b, _):
        dhidden = (contract(dfinal_low, w2[b], ((1,), (1,))) * slope_ref[b]).astype(BF16)
        uplg_ref[b] = jnp.sum(dhidden.astype(F32), axis=0, keepdims=True)
        acc[...] += contract(dhidden, w1[b], ((1,), (1,)))
        return 0

    lax.fori_loop(0, blocks, back, 0)
    dsecond = acc[...]
    normal = normal_ref[...]
    dmid = dfinal + norm_back(dsecond, normal, inverse, rescaling)
    dmid_ref[...] = dmid
    dmid_low = dmid.astype(BF16)
    vecg_ref[...] = jnp.concatenate([
        jnp.sum(dmid_low.astype(F32), axis=0, keepdims=True),
        jnp.sum(dsecond * normal, axis=0, keepdims=True),
        jnp.sum(dsecond, axis=0, keepdims=True),
        jnp.sum(dfinal_low.astype(F32), axis=0, keepdims=True),
    ], axis=0)
    dout = contract(dmid_low, mix[...], ((1,), (1,))).astype(BF16)
    for g in range(n):
        dobuf[g] = dout[:, g * width : (g + 1) * width].reshape(items, here, width)

    def give(mask):
        return pltpu.make_async_remote_copy(
            src_ref=dobuf.at[li ^ mask],
            dst_ref=do_ref.at[mask],
            send_sem=osend.at[mask],
            recv_sem=orecv.at[mask],
            device_id={"lon": li ^ mask},
            device_id_type=MESH,
        )

    for mask in range(1, n):
        give(mask).start()
    do_ref[0] = dobuf[li]
    sq_ref[:, :D] = contract(att_ref[...], dmid_low, ((0,), (0,))).astype(BF16)
    gather.finish([0, 1])
    for c in extra:
        c.wait()
    accn[...] = jnp.zeros_like(accn)
    accw[...] = jnp.zeros_like(accw)

    def own(m, _):
        second, upstream = rows_ref[m], up[m]
        value, slope = gelu_parts(product(second, wown[...]) + uplown_ref[...])
        dhidden = (contract(upstream, nown[...], ((1,), (1,))) * slope).astype(BF16)
        accn[...] += contract(value.astype(BF16), upstream, ((0,), (0,)))
        accw[...] += contract(second, dhidden, ((0,), (0,)))
        return 0

    lax.fori_loop(0, n, own, 0)
    narg_ref[...] = accn[...].astype(BF16)
    widg_ref[...] = accw[...].astype(BF16)
    gather.drain([0, 1])
    for mask in range(1, n):
        give(mask).wait()


def middle_part(att, emb, mixing, vecs, uplift, uplift_own, widening, narrowing, read, base, dpred, up_all, wide_own, narrow_own, n, items, here, heads):
    rows = items * here
    width = heads * HDIM
    block = 512
    blocks = FF // block
    own = narrow_own.shape[0]
    vm = pl.BlockSpec(memory_space=pltpu.VMEM)
    hbm = pl.BlockSpec(memory_space=pl.ANY)
    shape = jax.ShapeDtypeStruct
    return pl.pallas_call(
        functools.partial(middle_kernel, n, items, here, heads, own, block),
        in_specs=[vm, vm, hbm, vm, vm, vm, hbm, hbm, vm, vm, vm, hbm, hbm, hbm],
        out_specs=(vm,) * 8,
        out_shape=(
            shape((rows, 4 * NOUT), BF16), shape((D, D + 256), BF16), shape((own, D), BF16),
            shape((D, own), BF16), shape((rows, D), F32), shape((n, items, here, width), BF16), shape((4, D), F32),
            shape((blocks, 1, block), F32),
        ),
        scratch_shapes=[
            pltpu.VMEM((blocks, D, block), BF16), pltpu.VMEM((blocks, block, D), BF16), pltpu.VMEM((D, D), BF16),
            pltpu.VMEM((D, own), BF16), pltpu.VMEM((own, D), BF16), pltpu.VMEM((n, rows, D), BF16),
            pltpu.VMEM((n, rows, D), BF16), pltpu.VMEM((rows, D), F32), pltpu.VMEM((rows, D), F32),
            pltpu.VMEM((blocks, rows, block), F32), pltpu.VMEM((n, items, here, width), BF16),
            pltpu.VMEM((own, D), F32), pltpu.VMEM((D, own), F32),
            pltpu.SemaphoreType.DMA((n, 2)), pltpu.SemaphoreType.DMA((n, 2)),
            pltpu.SemaphoreType.DMA((n,)), pltpu.SemaphoreType.DMA((n,)),
            pltpu.SemaphoreType.DMA((2 * blocks + 3 + n,)),
        ],
        compiler_params=pltpu.CompilerParams(collective_id=2, has_side_effects=True, vmem_limit_bytes=60 * MIB),
        name="middle",
    )(att, emb, mixing, vecs, uplift.reshape(blocks, 1, block), uplift_own, widening, narrowing, read, base, dpred, up_all, wide_own, narrow_own)


def greet(n, li, count, zi):
    sem = pltpu.get_barrier_semaphore()
    for mask in range(1, n):
        pl.semaphore_signal(sem, inc=1, device_id={"lon": li ^ mask}, device_id_type=MESH)
    for mask in range(1, count):
        pl.semaphore_signal(sem, inc=1, device_id={"batch": zi ^ mask}, device_id_type=MESH)
    pl.semaphore_wait(sem, n + count - 2)


class Halving:
    def __init__(self, count, zi, flip, own, stage, land, send, recv):
        self.count, self.zi, self.own, self.stage, self.land = count, zi, own, stage, land
        self.send_sem, self.recv_sem = send, recv
        self.bits = [1 << i for i in range(count.bit_length() - 1)]
        if flip:
            self.bits = self.bits[::-1]

    def at_step(self, step):
        return [r for r in range(1, self.count) if min(i for i, b in enumerate(self.bits) if b & r) == step]

    def copy(self, r, step):
        return pltpu.make_async_remote_copy(
            src_ref=self.own(self.zi ^ r) if step == 0 else self.stage.at[r],
            dst_ref=self.land.at[r],
            send_sem=self.send_sem.at[r],
            recv_sem=self.recv_sem.at[r],
            device_id={"batch": self.zi ^ self.bits[step]},
            device_id_type=MESH,
        )

    def send(self, step):
        for r in self.at_step(step):
            self.copy(r, step).start()

    def absorb(self, step):
        for r in self.at_step(step):
            self.copy(r, step).wait_recv()
            to = r ^ self.bits[step]
            base = self.own(self.zi ^ to)[...] if step == 0 else self.stage[to]
            total = base.astype(F32) + self.land[r].astype(F32)
            if step == len(self.bits) - 1:
                return total
            self.stage[to] = total.astype(BF16)

    def drain(self):
        for step in range(len(self.bits)):
            for r in self.at_step(step):
                self.copy(r, step).wait_send()


class RowSum:
    def __init__(self, n, li, count, zi, own, land1, stage1, land2, stage2, land3, sems):
        self.n, self.li, self.count, self.zi, self.own = n, li, count, zi, own
        self.land1, self.stage1, self.land2, self.stage2, self.land3 = land1, stage1, land2, stage2, land3
        self.s1, self.r1, self.s2, self.r2, self.s3, self.r3 = sems
        self.half = n // 2

    @staticmethod
    def scratch(n, count, rows, cols):
        half = pltpu.VMEM((n // 2, count, rows, cols), BF16)
        one = pltpu.VMEM((count, rows, cols), BF16)
        lon_sem, z_sem = pltpu.SemaphoreType.DMA((n // 2,)), pltpu.SemaphoreType.DMA((count,))
        return [half, half, half, one, one, lon_sem, lon_sem, lon_sem, lon_sem, z_sem, z_sem]

    def copy1(self, j):
        return pltpu.make_async_remote_copy(
            src_ref=self.own(self.li ^ (2 * j + 1)), dst_ref=self.land1.at[j], send_sem=self.s1.at[j],
            recv_sem=self.r1.at[j], device_id={"lon": self.li ^ 1}, device_id_type=MESH,
        )

    def copy2(self, j):
        return pltpu.make_async_remote_copy(
            src_ref=self.stage1.at[j], dst_ref=self.land2.at[j], send_sem=self.s2.at[j],
            recv_sem=self.r2.at[j], device_id={"lon": self.li ^ (2 * j)}, device_id_type=MESH,
        )

    def copy3(self, r):
        return pltpu.make_async_remote_copy(
            src_ref=self.stage2.at[self.zi ^ r], dst_ref=self.land3.at[r], send_sem=self.s3.at[r],
            recv_sem=self.r3.at[r], device_id={"batch": self.zi ^ r}, device_id_type=MESH,
        )

    def core(self):
        for j in range(self.half):
            self.copy1(j).start()

    def plane(self):
        for j in list(range(1, self.half)) + [0]:
            self.copy1(j).wait_recv()
            self.stage1[j] = (self.own(self.li ^ (2 * j))[...].astype(F32) + self.land1[j].astype(F32)).astype(BF16)
            if j:
                self.copy2(j).start()

    def depth(self):
        total = self.stage1[0].astype(F32)
        for j in range(1, self.half):
            self.copy2(j).wait_recv()
            total = total + self.land2[j].astype(F32)
        self.stage2[...] = total.astype(BF16)
        for r in range(1, self.count):
            self.copy3(r).start()

    def total(self):
        total = self.stage2[self.zi].astype(F32)
        for r in range(1, self.count):
            self.copy3(r).wait_recv()
            total = total + self.land3[r].astype(F32)
        return total

    def drain(self):
        for j in range(self.half):
            self.copy1(j).wait_send()
            if j:
                self.copy2(j).wait_send()
        for r in range(1, self.count):
            self.copy3(r).wait_send()


def back_kernel(
    n, count, items, here, heads, qkv_ref, lse_ref, do_ref, rows_hbm, narg_ref, widg_ref, sq_ref,
    e3_ref, projg_ref, nar_ref, wid_ref, sqo_ref,
    rows_ref, ebuf, eland, dk_acc, dv_acc, esend, erecv, load,
    nstage, nland, nsend, nrecv, wstage, wland, wsend, wrecv, *sums,
):
    li, zi = lax.axis_index("lon"), lax.axis_index("batch")
    width = heads * HDIM
    seq = n * here
    tile = min(seq, 512)
    fetch = pltpu.make_async_copy(rows_hbm, rows_ref, load)
    fetch.start()
    greet(n, li, count, zi)
    nar = Halving(count, zi, False, lambda b: narg_ref.at[b], nstage, nland, nsend, nrecv)
    wid = Halving(count, zi, True, lambda b: widg_ref.at[b], wstage, wland, wsend, wrecv)
    squares = RowSum(n, li, count, zi, lambda l: sq_ref.at[:, l], *sums[:5], sums[5:])
    nar.send(0)
    wid.send(0)
    squares.core()

    def give(i, mask):
        return pltpu.make_async_remote_copy(
            src_ref=ebuf.at[i, mask],
            dst_ref=eland.at[li, i],
            send_sem=esend.at[i, mask],
            recv_sem=erecv.at[i, mask],
            device_id={"lon": li ^ mask},
            device_id_type=MESH,
        )

    steps = len(nar.bits)
    for i in range(items):
        dk_acc[...] = jnp.zeros_like(dk_acc)
        dv_acc[...] = jnp.zeros_like(dv_acc)
        for t in range(seq // tile):
            part = slice(t * tile, (t + 1) * tile)
            outs = []
            do_rows = do_ref[t * (tile // here) : (t + 1) * (tile // here), i].reshape(tile, width)
            for h in range(heads):
                cols = slice(h * HDIM, (h + 1) * HDIM)
                q = qkv_ref[i, part, h * HDIM : (h + 1) * HDIM] * FACTOR
                k = qkv_ref[i, :, width + h * HDIM : width + (h + 1) * HDIM]
                v = qkv_ref[i, :, 2 * width + h * HDIM : 2 * width + (h + 1) * HDIM]
                do = do_rows[:, cols]
                scores = contract(k, q, ((1,), (1,)))
                probs = jnp.exp(scores - lse_ref[i, h : h + 1, part])
                dprobs = contract(v, do, ((1,), (1,)))
                delta = jnp.sum(probs * dprobs, axis=0, keepdims=True)
                dscores = (probs * (dprobs - delta)).astype(BF16)
                dv_acc[h] += product(probs.astype(BF16), do)
                dk_acc[h] += product(dscores, q)
                outs.append(contract(dscores, k, ((0,), (0,))) * FACTOR)
            out = jnp.concatenate(outs, axis=1) if heads > 1 else outs[0]
            ebuf[i, t * (tile // here) : (t + 1) * (tile // here), :, :width] = out.astype(BF16).reshape(tile // here, here, width)
            if i == 0 and t == 0:
                squares.plane()
        for h in range(heads):
            ebuf[i, :, :, width + h * HDIM : width + (h + 1) * HDIM] = dk_acc[h].astype(BF16).reshape(n, here, HDIM)
            ebuf[i, :, :, 2 * width + h * HDIM : 2 * width + (h + 1) * HDIM] = dv_acc[h].astype(BF16).reshape(n, here, HDIM)
        for mask in range(1, n):
            give(i, mask).start()
        eland[li, i] = ebuf[i, 0]
        if i == 0:
            squares.depth()
    fetch.wait()
    total = contract(rows_ref[0].reshape(seq, D), ebuf[0].reshape(seq, 3 * width), ((0,), (0,)))
    for i in range(1, items):
        total = total + contract(rows_ref[i].reshape(seq, D), ebuf[i].reshape(seq, 3 * width), ((0,), (0,)))
    projg_ref[...] = total.astype(BF16)
    for step in range(steps):
        n_total, w_total = nar.absorb(step), wid.absorb(step)
        if step + 1 < steps:
            nar.send(step + 1)
            wid.send(step + 1)
        if step == 0:
            for i in range(items):
                for mask in range(1, n):
                    give(i, mask).wait_recv()
                here_rows = slice(i * here, (i + 1) * here)
                for p in range(3):
                    e3_ref[here_rows, p * D : (p + 1) * D] = jnp.concatenate(
                        [eland[g, i, :, p * width : (p + 1) * width] for g in range(n)], axis=1
                    )
            sqo_ref[...] = squares.total()
    nar_ref[...] = n_total
    wid_ref[...] = w_total.astype(BF16)
    nar.drain()
    wid.drain()
    squares.drain()
    for i in range(items):
        for mask in range(1, n):
            give(i, mask).wait_send()


def back_part(qkv, lse, do, rows_all, narg, widg, squares, n, count, items, here, heads):
    width = heads * HDIM
    seq = n * here
    shape = jax.ShapeDtypeStruct
    vm = pl.BlockSpec(memory_space=pltpu.VMEM)
    hid, own = narg.shape[1], widg.shape[2]
    rd, cols = squares.shape[2], squares.shape[3]
    zsem = pltpu.SemaphoreType.DMA((count,))
    nbuf, wbuf = pltpu.VMEM(narg.shape, BF16), pltpu.VMEM(widg.shape, BF16)
    return pl.pallas_call(
        functools.partial(back_kernel, n, count, items, here, heads),
        in_specs=[vm, vm, vm, pl.BlockSpec(memory_space=pl.ANY), vm, vm, vm],
        out_specs=(vm,) * 5,
        out_shape=(
            shape((items * here, 3 * D), BF16), shape((D, 3 * width), BF16), shape((hid, D), F32),
            shape((D // count, own), BF16), shape((rd, cols), F32),
        ),
        scratch_shapes=[
            pltpu.VMEM((items, n, here, D), BF16), pltpu.VMEM((items, n, here, 3 * width), BF16),
            pltpu.VMEM((n, items, here, 3 * width), BF16), pltpu.VMEM((heads, seq, HDIM), F32), pltpu.VMEM((heads, seq, HDIM), F32),
            pltpu.SemaphoreType.DMA((items, n)), pltpu.SemaphoreType.DMA((items, n)), pltpu.SemaphoreType.DMA,
            nbuf, nbuf, zsem, zsem, wbuf, wbuf, zsem, zsem,
        ] + RowSum.scratch(n, count, rd, cols),
        compiler_params=pltpu.CompilerParams(collective_id=3, has_side_effects=True, vmem_limit_bytes=60 * MIB),
        name="back",
    )(qkv, lse, do, rows_all, narg, widg, squares)


ARROWS = 384


def last_kernel(
    n, count, items, here, heads, e3_ref, proj_hbm, merge_hbm, emb_ref, dmid_ref, pooled_ref, vec_ref, patches_ref,
    w_ref, qrow_ref, pv_ref, early_ref, projg_ref, wid_ref,
    pos_ref, mer_ref, dpatch_ref, ar_ref, col_ref,
    proj, merge, load, mbuf, du3, wide_w, arbuf, arland, arz, archunk, posbuf, posland, posall, colbuf,
    asend, arecv, azs, azr, ags, agr, bgs, bgr, pss, psr, pgs, pgr, cs, cr,
    pstage, pland, psend, precv, qstage, qland, qsend, qrecv, *sums,
):
    li, zi = lax.axis_index("lon"), lax.axis_index("batch")
    rows = items * here
    width = heads * HDIM
    rd = D // (n * count)
    fetch_p = [pltpu.make_async_copy(proj_hbm.at[:, p * D : (p + 1) * D], proj.at[p], load.at[p]) for p in range(3)]
    fetch_m = pltpu.make_async_copy(merge_hbm, merge, load.at[3])
    for c in fetch_p + [fetch_m]:
        c.start()
    greet(n, li, count, zi)
    hz = D // count // 2
    first = Halving(count, zi, False, lambda b: projg_ref.at[b, pl.ds(0, hz)], pstage, pland, psend, precv)
    second = Halving(count, zi, True, lambda b: projg_ref.at[b, pl.ds(hz, hz)], qstage, qland, qsend, qrecv)
    squares = RowSum(n, li, count, zi, lambda l: mbuf.at[:, l], *sums[:5], sums[5:])
    first.send(0)
    second.send(0)

    normal, inverse = normalize(emb_ref[...])
    scaling = vec_ref[0:1, :]
    dnormed = jnp.zeros((rows, D), F32)
    for p in range(3):
        fetch_p[p].wait()
        dnormed = dnormed + contract(e3_ref[:, p * D : (p + 1) * D], proj[p], ((1,), (1,)))
    demb = dmid_ref[...] + norm_back(dnormed, normal, inverse, scaling)
    demb_low = demb.astype(BF16)
    summed = demb[:here]
    for i in range(1, items):
        summed = summed + demb[i * here : (i + 1) * here]
    posbuf[...] = summed.astype(BF16).reshape(count, here // count, D)

    def pos_give(r):
        return pltpu.make_async_remote_copy(
            src_ref=posbuf.at[zi ^ r], dst_ref=posland.at[r], send_sem=pss.at[r], recv_sem=psr.at[r],
            device_id={"batch": zi ^ r}, device_id_type=MESH,
        )

    def pos_share(r):
        return pltpu.make_async_remote_copy(
            src_ref=posall.at[zi], dst_ref=posall.at[zi], send_sem=pgs.at[r], recv_sem=pgr.at[r],
            device_id={"batch": zi ^ r}, device_id_type=MESH,
        )

    for r in range(1, count):
        pos_give(r).start()
    fetch_m.wait()
    mbuf[...] = contract(pooled_ref[...], demb_low, ((0,), (0,))).astype(BF16).reshape(mbuf.shape)
    squares.core()
    dpooled = contract(demb_low, merge[...], ((1,), (1,))).astype(BF16)
    total = lambda a: jnp.sum(a, axis=0, keepdims=True)
    e3 = lambda p: total(e3_ref[:, p * D : (p + 1) * D].astype(F32))
    vectors = jnp.concatenate([
        total(dpooled.astype(F32)), total(demb_low.astype(F32)), total(dnormed * normal), total(dnormed), e3(0), e3(2), early_ref[...],
    ], axis=0).astype(BF16)
    for g in range(n):
        du3[g] = dpooled[:, g * width : (g + 1) * width]
        arbuf[g, JPAD : JPAD + 16] = vectors[:, g * width : (g + 1) * width]
    squares.plane()
    patches = patches_ref[...].astype(F32)
    dpatch_ref[...] = jnp.zeros_like(dpatch_ref)
    lines = -(-JPAD // width)

    def give(mask):
        return pltpu.make_async_remote_copy(
            src_ref=arbuf.at[li ^ mask], dst_ref=arland.at[mask], send_sem=asend.at[mask], recv_sem=arecv.at[mask],
            device_id={"lon": li ^ mask}, device_id_type=MESH,
        )

    def group(mask):
        g = li ^ mask
        halves, extra = [], []
        patch_total = jnp.zeros((rows, 4 * VPAD), F32)
        du_all, pv_all = du3[g], pv_ref[g]
        for s in range(heads):
            h = g * heads + s
            w = w_ref[h]
            wide = jnp.concatenate([w] * 5, axis=1)
            blended = (wide * patches).astype(BF16)
            du = du_all[:, s * HDIM : (s + 1) * HDIM]
            dbl = contract(du, pv_all[:, s * HDIM : (s + 1) * HDIM], ((1,), (1,)))
            halves.append(contract(blended, du, ((0,), (0,))))
            x = dbl * patches
            dw = x[:, :VPAD]
            for c in range(1, 5):
                dw = dw + x[:, c * VPAD : (c + 1) * VPAD]
            da = w * (dw - jnp.sum(w * dw, axis=-1, keepdims=True)) * FACTOR
            da_wide = jnp.concatenate([da] * 5, axis=1)
            line = total(da_wide * patches)
            line = jnp.concatenate([line, jnp.zeros((1, lines * width - JPAD), F32)], axis=1) if lines * width > JPAD else line
            extra += [line[:, c * width : (c + 1) * width] for c in range(lines)]
            patch_total = patch_total + (wide[:, : 4 * VPAD] * dbl[:, : 4 * VPAD] + da_wide[:, : 4 * VPAD] * qrow_ref[h][:, : 4 * VPAD])
        dpatch_ref[...] += patch_total
        arbuf[g, :JPAD] = (jnp.concatenate(halves, axis=1) if heads > 1 else halves[0]).astype(BF16)
        tail = jnp.concatenate(extra + [jnp.zeros((ARROWS - JPAD - 16 - heads * lines, width), F32)], axis=0)
        arbuf[g, JPAD + 16 :] = tail.astype(BF16)

    for mask in range(1, n):
        group(mask)
        give(mask).start()
        if mask == 2:
            posall[zi] = posbuf[zi]
            pos_sum = posbuf[zi].astype(F32)
            for r in range(1, count):
                pos_give(r).wait_recv()
                pos_sum = pos_sum + posland[r].astype(F32)
            posall[zi] = pos_sum.astype(BF16)
            for r in range(1, count):
                pos_share(r).start()
        if mask == 4:
            first.absorb(0)
            second.absorb(0)
            for step in range(1, len(first.bits)):
                first.send(step)
                second.send(step)
                if step + 1 < len(first.bits):
                    first.absorb(step)
                    second.absorb(step)
        if mask == 5:
            squares.depth()
    group(0)

    last = len(first.bits) - 1
    own = wid_ref.shape[-1]
    top, low = first.absorb(last).astype(BF16), second.absorb(last).astype(BF16)
    cols = jnp.concatenate([wid_ref[...], jnp.concatenate([top, low], axis=0)], axis=1)
    colbuf[...] = cols.reshape(colbuf.shape)

    def col_give(mask):
        return pltpu.make_async_remote_copy(
            src_ref=colbuf.at[li ^ mask], dst_ref=col_ref.at[li], send_sem=cs.at[mask], recv_sem=cr.at[mask],
            device_id={"lon": li ^ mask}, device_id_type=MESH,
        )

    chunk = arbuf[li].astype(F32)
    for mask in range(1, n):
        give(mask).wait_recv()
        chunk = chunk + arland[mask].astype(F32)
    piece = ARROWS // count
    archunk[...] = chunk.astype(BF16).reshape(archunk.shape)

    def z_give(r):
        return pltpu.make_async_remote_copy(
            src_ref=archunk.at[zi ^ r], dst_ref=arz.at[r], send_sem=azs.at[r], recv_sem=azr.at[r],
            device_id={"batch": zi ^ r}, device_id_type=MESH,
        )

    def z_share(r):
        return pltpu.make_async_remote_copy(
            src_ref=ar_ref.at[li, zi], dst_ref=ar_ref.at[li, zi], send_sem=ags.at[r], recv_sem=agr.at[r],
            device_id={"batch": zi ^ r}, device_id_type=MESH,
        )

    for r in range(1, count):
        z_give(r).start()
    for mask in range(1, n):
        col_give(mask).start()
    col_ref[li] = colbuf[li]
    piece_sum = archunk[zi].astype(F32)
    for r in range(1, count):
        z_give(r).wait_recv()
        piece_sum = piece_sum + arz[r].astype(F32)
    ar_ref[li, zi] = piece_sum.astype(BF16)
    for r in range(1, count):
        z_share(r).start()
    mer_ref[...] = squares.total()
    for r in range(1, count):
        z_share(r).wait_recv()

    def l_share(mask):
        return pltpu.make_async_remote_copy(
            src_ref=ar_ref.at[li], dst_ref=ar_ref.at[li], send_sem=bgs.at[mask], recv_sem=bgr.at[mask],
            device_id={"lon": li ^ mask}, device_id_type=MESH,
        )

    def l_relay(mask):
        return pltpu.make_async_remote_copy(
            src_ref=ar_ref.at[li ^ mask], dst_ref=ar_ref.at[li ^ mask], send_sem=bgs.at[mask | 1], recv_sem=bgr.at[mask | 1],
            device_id={"lon": li ^ 1}, device_id_type=MESH,
        )

    for mask in range(2, n, 2):
        l_share(mask).start()
    l_relay(0).start()
    for r in range(1, count):
        pos_share(r).wait_recv()
    pos_ref[...] = posall[...].reshape(here, D).astype(F32)
    for mask in range(2, n, 2):
        l_share(mask).wait_recv()
        l_relay(mask).start()
    for mask in range(0, n, 2):
        l_relay(mask).wait_recv()
    for mask in range(1, n):
        col_give(mask).wait()
        give(mask).wait_send()
    for mask in range(0, n, 2):
        l_relay(mask).wait_send()
        if mask:
            l_share(mask).wait_send()
    for r in range(1, count):
        z_give(r).wait_send()
        z_share(r).wait_send()
        pos_give(r).wait_send()
        pos_share(r).wait_send()
    first.drain()
    second.drain()
    squares.drain()


def last_part(e3, projecting, merging, emb, dmid, pooled, vecs, patches, pool_w, qrow, pv, early, projg, wid, n, count, items, here, heads):
    rows, width = items * here, heads * HDIM
    rd = D // (n * count)
    shape = jax.ShapeDtypeStruct
    vm, hbm = pl.BlockSpec(memory_space=pltpu.VMEM), pl.BlockSpec(memory_space=pl.ANY)
    own = wid.shape[1]
    piece = ARROWS // count
    hz = D // count // 2
    lsem, zsem = pltpu.SemaphoreType.DMA((n,)), pltpu.SemaphoreType.DMA((count,))
    zbuf = pltpu.VMEM((count, hz, 3 * width), BF16)
    pos = pltpu.VMEM((count, here // count, D), BF16)
    return pl.pallas_call(
        functools.partial(last_kernel, n, count, items, here, heads),
        in_specs=[vm, hbm, hbm] + [vm] * 11,
        out_specs=(vm,) * 5,
        out_shape=(
            shape((here, D), F32), shape((rd, D), F32), shape((rows, 4 * VPAD), F32),
            shape((n, count, piece, width), BF16), shape((n, rd, own + 3 * width), BF16),
        ),
        scratch_shapes=[
            pltpu.VMEM((3, D, D), BF16), pltpu.VMEM((D, D), BF16), pltpu.SemaphoreType.DMA((4,)),
            pltpu.VMEM((count, n, rd, D), BF16), pltpu.VMEM((n, rows, width), BF16), pltpu.VMEM((8, 128), F32),
            pltpu.VMEM((n, ARROWS, width), BF16), pltpu.VMEM((n, ARROWS, width), BF16), pltpu.VMEM((count, piece, width), BF16),
            pltpu.VMEM((count, piece, width), BF16), pos, pos, pos, pltpu.VMEM((n, rd, own + 3 * width), BF16),
            lsem, lsem, zsem, zsem, zsem, zsem, lsem, lsem, zsem, zsem, zsem, zsem, lsem, lsem,
            zbuf, zbuf, zsem, zsem, zbuf, zbuf, zsem, zsem,
        ] + RowSum.scratch(n, count, rd, D),
        compiler_params=pltpu.CompilerParams(collective_id=4, has_side_effects=True, vmem_limit_bytes=60 * MIB),
        name="last",
    )(e3, projecting, merging, emb, dmid, pooled, vecs, patches, pool_w, qrow, pv, early, projg, wid)


def per_device(
    fields, variable_ids, variable_mask, position, patching, tagging, beacon, keying, valuing, lifting,
    merging, offset, scaling, centre, projecting, biasing, mixing, nudging, rescaling, recentre,
    widening, uplift, narrowing, settle, reading, baseline, cotangent,
):
    count, lon = lax.axis_size("batch"), lax.axis_size("lon")
    zi, li = lax.axis_index("batch"), lax.axis_index("lon")
    block = zi * lon + li
    items, cols_dev, lat = fields.shape[0], fields.shape[2], fields.shape[3]
    upatch = cols_dev // 2
    here = upatch * LATP
    rows = items * here
    own_heads = HEADS // lon
    width = own_heads * HDIM
    rows_dev = D // (count * lon)
    f = lambda a: a.astype(F32)

    canvas = jnp.stack([fields, cotangent])
    edge = lax.ppermute(canvas[:, :, :, -1:, :], "lon", [(i, (i + 1) % lon) for i in range(lon)])
    canvas = jnp.concatenate([edge, canvas[:, :, :, :-1, :]], axis=3)

    q_at = jnp.arange(lat)
    spread = ((q_at[:, None] % 2) * LATP + q_at[:, None] // 2 == q_at[None, :]).astype(BF16)
    choose = (variable_ids[:, :, None] == jnp.arange(VPAD, dtype=jnp.int32)[None, None, :]).astype(BF16)
    ordered = jnp.einsum("bsv,bswq->bwvq", choose, canvas[0], preferred_element_type=F32).astype(BF16)
    ptok = jnp.einsum("bwvq,qc->bwcv", ordered, spread, preferred_element_type=F32).astype(BF16)
    ptok = ptok.reshape(items, upatch, 2, 2, LATP, VPAD).transpose(0, 1, 4, 2, 3, 5).reshape(rows, 4 * VPAD)
    patches = jnp.concatenate([ptok, jnp.ones((rows, VPAD), BF16)], axis=1)
    ytok = jnp.einsum("bowq,qc->bwco", canvas[1], spread, preferred_element_type=F32).astype(BF16)
    dpred = ytok.reshape(items, upatch, 2, 2, LATP, NOUT).transpose(0, 1, 4, 2, 3, 5).reshape(rows, 4 * NOUT)
    live = jnp.einsum("bs,bsv->bv", variable_mask.astype(BF16), choose, preferred_element_type=F32) > 0.5
    lane = jnp.arange(VPAD)[None, :]
    mask = jnp.where(lane < NVAR, jnp.where(live, 0.0, -1e30), -2e30)
    mask = jnp.broadcast_to(mask[:, None, :], (items, here, VPAD)).reshape(rows, VPAD)

    source = jnp.concatenate([jnp.arange(NVAR * 4) % 4 * VPAD + jnp.arange(NVAR * 4) // 4, 4 * VPAD + jnp.arange(NVAR)])
    place = (source[:, None] == jnp.arange(JPAD)[None, :]).astype(BF16)
    embed = product(jnp.concatenate([patching, tagging], axis=1), place).astype(BF16)
    pv = contract(embed, valuing, ((0,), (0,))).astype(BF16)
    head_of = (jnp.arange(D)[:, None] // HDIM == jnp.arange(HEADS)[None, :])
    keymap = product(keying, jnp.where(head_of, beacon[:, None], jnp.zeros((), BF16)))
    qmap = jnp.dot(f(embed).T, keymap, precision=HIGH)
    same = (jnp.arange(4 * VPAD)[:, None] % VPAD == jnp.arange(VPAD)[None, :])
    logit_map = jnp.where(same[:, None, :], qmap[: 4 * VPAD, :, None], 0.0).reshape(4 * VPAD, HEADS * VPAD) * FACTOR
    tag_row = (qmap[4 * VPAD :, :].T * FACTOR).reshape(1, HEADS * VPAD)

    pooled, pool_w = pool_forward(patches, logit_map, tag_row, mask, pv, f(lifting)[None, :])
    placed = jnp.broadcast_to(f(position).reshape(1, here, D), (items, here, D)).reshape(rows, D)
    embedded = product(pooled, merging) + f(offset) + placed
    normal_one, inverse_one = normalize(embedded)
    normed = (normal_one * f(scaling) + f(centre)).astype(BF16)

    seq = lon * here
    columns = lambda a, start, size: lax.dynamic_slice_in_dim(a, start, size, 1)
    own = jnp.concatenate([columns(projecting, p * D + li * width, width) for p in range(3)], axis=1)
    joint_bias = jnp.concatenate([biasing[:D], jnp.zeros((D,), BF16), biasing[D:]]).reshape(3, lon, width)
    own_bias = lax.dynamic_slice(joint_bias, (0, li, 0), (3, 1, width)).reshape(1, 3 * width)
    attended_low, normed_all, joint, lse = front(normed.reshape(items, here, D), own, f(own_bias), lon, items, here, own_heads)
    q, k, v = joint[:, :, :width], joint[:, :, width : 2 * width], joint[:, :, 2 * width :]

    def heads_to_tokens(a):
        w = a.shape[-1]
        slots = jnp.arange(lon) ^ li
        a = jnp.take(a.reshape(items, lon, here, w), slots, axis=1)
        a = lax.all_to_all(a, "lon", 1, 1, tiled=True)
        return a.transpose(0, 2, 1, 3).reshape(rows, lon * w)

    corner = jnp.arange(NOUT * 4)
    shuffle = ((corner % 4) * NOUT + corner // 4)[:, None] == corner[None, :]
    shuffle = shuffle.astype(BF16)
    reading_p = product(reading, shuffle).astype(BF16)
    baseline_p = product(baseline[None, :], shuffle)
    dfinal_low = contract(dpred, reading_p, ((1,), (1,))).astype(BF16)
    upstream_all = lax.all_gather(dfinal_low, "lon", axis=0)
    hid = FF // (count * lon)
    starts = [(c * lon + li) * hid for c in range(count)]
    wide_own = jnp.concatenate([columns(widening, s, hid) for s in starts], axis=1)
    narrow_own = jnp.concatenate([lax.dynamic_slice_in_dim(narrowing, s, hid, 0) for s in starts], axis=0)
    uplift_own = jnp.concatenate([lax.dynamic_slice_in_dim(uplift, s, hid, 0) for s in starts])[None, :]
    vecs = f(jnp.stack([nudging, rescaling, recentre, settle]))
    outputs, squares, narrowing_own, widening_own, dmiddle, do, vec_grads, uplift_local = middle_part(
        attended_low, embedded, mixing, vecs, f(uplift), f(uplift_own), widening, narrowing, reading_p, baseline_p, dpred,
        upstream_all, wide_own, narrow_own, lon, items, here, own_heads,
    )
    canvas_out = outputs.reshape(items, upatch, LATP, 2, 2, NOUT).transpose(0, 1, 3, 5, 4, 2)
    canvas_out = canvas_out.reshape(items, cols_dev, NOUT, lat)
    predicted = jnp.einsum("bwoc,qc->bowq", canvas_out, spread, preferred_element_type=F32).astype(BF16)
    folded = lax.ppermute(predicted[:, :, :1, :], "lon", [(i, (i - 1) % lon) for i in range(lon)])
    prediction = jnp.concatenate([predicted[:, :, 1:, :], folded], axis=2)

    baseline_local = jnp.pad(jnp.sum(f(dpred), axis=0), (0, D - 4 * NOUT))
    djoint, projecting_own, narrowing_gradient, widening_rows, squares = back_part(
        joint, lse, do, normed_all, narrowing_own.reshape(count, hid, D), widening_own.reshape(count, D // count, count * hid),
        squares.reshape(count, lon, rows_dev, -1), lon, count, items, here, own_heads,
    )
    early = jnp.concatenate([vec_grads, uplift_local.reshape(FF // D, D), baseline_local[None, :], jnp.zeros((1, D), F32)], axis=0)
    position_gradient, merging_gradient, dpatch, summed, columns_own = last_part(
        djoint, projecting, merging, embedded, dmiddle, pooled, f(scaling)[None, :], patches, pool_w, qmap.T.reshape(HEADS, 1, JPAD),
        pv.reshape(JPAD, lon, width).transpose(1, 0, 2), early, projecting_own.reshape(count, D // count, 3 * width), widening_rows,
        lon, count, items, here, own_heads,
    )
    position_gradient = position_gradient.reshape(upatch, LATP, D)
    widening_gradient = f(columns_own[:, :, : count * hid].reshape(lon, rows_dev, count, hid).transpose(1, 2, 0, 3).reshape(rows_dev, FF))
    projecting_gradient = f(columns_own[:, :, count * hid :].reshape(lon, rows_dev, 3, width).transpose(1, 2, 0, 3).reshape(rows_dev, 3 * D))
    mixing_gradient = squares[:, :D]
    reading_gradient = jnp.dot(squares[:, D : D + 4 * NOUT], f(shuffle).T, precision=HIGH)
    summed = summed.reshape(lon, ARROWS, width)
    dpv = summed[:, :JPAD].transpose(1, 0, 2).reshape(JPAD, D)
    vectors = f(summed[:, JPAD : JPAD + 16]).transpose(1, 0, 2).reshape(16 * D)
    lines = -(-JPAD // width)
    dqz = f(summed[:, JPAD + 16 : JPAD + 16 + own_heads * lines]).reshape(HEADS, lines * width)[:, :JPAD]

    def mine(a, size):
        return lax.dynamic_slice_in_dim(a, block * size, size, 0)

    vec = lambda i: mine(vectors[i * D : (i + 1) * D], rows_dev)
    biasing_gradient = mine(vectors[4 * D : 6 * D], 2 * rows_dev)
    uplift_gradient = mine(vectors[10 * D : 14 * D], 4 * rows_dev)
    baseline_gradient = jnp.dot(vectors[None, 14 * D : 14 * D + 4 * NOUT], f(shuffle).T, precision=HIGH)[0]

    embed_mine = mine(embed, rows_dev)
    valuing_gradient = product(embed_mine, dpv)
    dembed = contract(mine(valuing, rows_dev), dpv, ((1,), (1,))) + jnp.dot(mine(keymap, rows_dev), dqz, precision=HIGH)
    dembed = jnp.dot(dembed, f(place).T, precision=HIGH)
    patching_gradient, tagging_gradient = dembed[:, : 4 * NVAR], dembed[:, 4 * NVAR :]
    dkeymap = jnp.dot(f(embed), dqz.T, precision=HIGH)
    keying_gradient = jnp.repeat(mine(dkeymap, rows_dev), HDIM, axis=1) * f(beacon)
    beacon_all = jnp.sum(jnp.repeat(dkeymap, HDIM, axis=1) * f(keying), axis=0)
    beacon_gradient = mine(beacon_all, rows_dev)

    dcan = dpatch.reshape(items, upatch, LATP, 2, 2, VPAD).transpose(0, 1, 3, 5, 4, 2).reshape(items, cols_dev, VPAD, lat)
    dslots = jnp.einsum("bwvc,qc->bwvq", dcan, f(spread), precision=HIGH)
    dslots = jnp.einsum("bsv,bwvq->bswq", f(choose), dslots, precision=HIGH)
    returned = lax.ppermute(dslots[:, :, :1, :], "lon", [(i, (i - 1) % lon) for i in range(lon)])
    fields_gradient = jnp.concatenate([dslots[:, :, 1:, :], returned], axis=2)

    return (
        prediction, fields_gradient, position_gradient, patching_gradient, tagging_gradient, beacon_gradient,
        keying_gradient, valuing_gradient, vec(0), merging_gradient, vec(1), vec(2), vec(3), projecting_gradient,
        biasing_gradient, mixing_gradient, vec(6), vec(7), vec(8), widening_gradient, uplift_gradient,
        narrowing_gradient, vec(9), reading_gradient, baseline_gradient,
    )


def solution(mesh):
    both = ("batch", "lon")
    image, matrix, vector = P("batch", None, "lon", None), P(both, None), P(both)
    return jax.shard_map(
        per_device,
        mesh=mesh,
        in_specs=(image, P("batch", None), P("batch", None), P("lon", None, None)) + (P(),) * 22 + (image,),
        out_specs=(
            image, image, P("lon", None, None), matrix, matrix, vector, matrix, matrix, vector, matrix, vector,
            vector, vector, matrix, vector, matrix, vector, vector, vector, matrix, vector, matrix, vector, matrix, P(),
        ),
        check_vma=False,
    )
```

```python
import functools

import jax
import jax.numpy as jnp
from jax import lax
from jax.experimental import pallas as pl
from jax.experimental.pallas import tpu as pltpu
from jax.sharding import PartitionSpec as P

D = 1024
HEADS = 16
HDIM = 64
FF = 4096
NVAR = 48
NOUT = 48
LATP = 32
VPAD = 64
JPAD = 5 * VPAD

HIGH = lax.Precision.HIGHEST
EPSILON = 1e-06
F32 = jnp.float32
BF16 = jnp.bfloat16
FACTOR = HDIM ** (-0.5)
MIB = 2**20
MESH = pl.DeviceIdType.MESH


def product(left, right):
    return jnp.dot(left, right, preferred_element_type=F32)


def contract(left, right, dims):
    return lax.dot_general(left, right, (dims, ((), ())), preferred_element_type=F32)


def normalize(values):
    centred = values - jnp.mean(values, axis=-1, keepdims=True)
    inverse = lax.rsqrt(jnp.mean(centred * centred, axis=-1, keepdims=True) + EPSILON)
    return centred * inverse, inverse


def norm_back(upstream, normal, inverse, scaler):
    weighted = upstream * scaler
    return inverse * (
        weighted
        - jnp.mean(weighted, axis=-1, keepdims=True)
        - normal * jnp.mean(weighted * normal, axis=-1, keepdims=True)
    )


def gelu_parts(x):
    c = 0.7978845608028654
    t = jnp.tanh(c * (x + 0.044715 * (x * x * x)))
    value = 0.5 * x * (1.0 + t)
    slope = 0.5 * (1.0 + t) + 0.5 * x * (1.0 - t * t) * (c * (1.0 + 3 * 0.044715 * x * x))
    return value, slope


def places(rows, cols, start, step, shift):
    row = lax.broadcasted_iota(jnp.int32, (rows, cols), 0)
    col = lax.broadcasted_iota(jnp.int32, (rows, cols), 1)
    return (start + (row & (step - 1)) * VPAD + (row >> shift) == col).astype(BF16)


def latitudes(lat):
    row = lax.broadcasted_iota(jnp.int32, (lat, lat), 0)
    col = lax.broadcasted_iota(jnp.int32, (lat, lat), 1)
    half = lat // 2
    return (2 * (row & (half - 1)) + (row >> (half.bit_length() - 1)) == col).astype(BF16)


def by_head(row):
    head = lax.broadcasted_iota(jnp.int32, (HEADS, D), 0)
    col = lax.broadcasted_iota(jnp.int32, (HEADS, D), 1)
    return jnp.where(col >> 6 == head, jnp.broadcast_to(row, (HEADS, D)), jnp.zeros((), row.dtype))


def pieces(a, count):
    parts = []
    for _ in range(count):
        parts.append(a.astype(BF16))
        a = a - parts[-1].astype(F32)
    return jnp.concatenate(parts, axis=0)


class Moves:
    def __init__(self, sem):
        self.sem, self.started = sem, []

    def go(self, src, dst):
        copy = pltpu.make_async_copy(src, dst, self.sem.at[len(self.started)])
        self.started.append(copy)
        copy.start()
        return copy


def folded(a, count):
    rows = a.shape[0] // count
    total = a[:rows]
    for i in range(1, count):
        total = total + a[i * rows : (i + 1) * rows]
    return total


def barrier_all(n, li):
    sem = pltpu.get_barrier_semaphore()
    for mask in range(1, n):
        pl.semaphore_signal(sem, inc=1, device_id={"lon": li ^ mask}, device_id_type=MESH)
    pl.semaphore_wait(sem, n - 1)


class Gather:
    def __init__(self, n, li, at, send, recv):
        self.n, self.li, self.at, self.send, self.recv = n, li, at, send, recv
        self.bits = [1 << i for i in range(1, n.bit_length() - 1)]

    def order(self, piece):
        return self.bits if piece % 2 == 0 else self.bits[::-1]

    def copy(self, mask, piece):
        bit = 1 if mask & 1 else [b for b in self.order(piece) if b & mask][-1]
        return pltpu.make_async_remote_copy(
            src_ref=self.at(mask ^ bit, piece),
            dst_ref=self.at(mask, piece),
            send_sem=self.send.at[mask, piece],
            recv_sem=self.recv.at[mask, piece],
            device_id={"lon": self.li ^ bit},
            device_id_type=MESH,
        )

    def forward(self, mask, piece):
        order = self.order(piece)
        used = [i for i, b in enumerate(order) if b & mask]
        for b in order[(used[-1] + 1 if used else 0):]:
            self.copy(mask | b, piece).start()
        self.copy(mask | 1, piece).start()

    def start(self, pieces):
        for piece in pieces:
            self.forward(0, piece)

    def evens(self):
        return sorted(range(2, self.n, 2), key=lambda m: bin(m).count("1"))

    def relay(self, pieces, first=True, rest=True):
        for depth in range(1, len(self.bits) + 1):
            if (first if depth == 1 else rest):
                for piece in pieces:
                    for mask in self.evens():
                        if bin(mask).count("1") == depth:
                            self.copy(mask, piece).wait_recv()
                            self.forward(mask, piece)

    def finish(self, pieces):
        for mask in range(1, self.n, 2):
            for piece in pieces:
                self.copy(mask, piece).wait_recv()

    def drain(self, pieces):
        for mask in range(1, self.n):
            for piece in pieces:
                self.copy(mask, piece).wait_send()


def front_kernel(
    n, items, here, heads, direct, fields_ref, cot_ref, ids_ref, mask_ref, patching_ref, tagging_ref, read_ref, beacon_ref, lifting_ref,
    offset_ref, scaling_ref, centre_ref, biasing_ref, place_ref, key_hbm, val_hbm, mer_hbm, proj_hbm,
    att_ref, all_out, qkv_out, lse_ref, up_out, emb_out, pooled_out, patches_out, pw_out, qrow_ref, pv_out, dpred_ref, base_ref, readp_out,
    keymap_ref, embed_out,
    keying, valuing, merging, own_w, load, seam, seam_land, seam_send, seam_recv, up_ref, usend, urecv,
    rows_ref, obuf, land, gsend, grecv, osend, orecv, keep, qkv_ref, emb_ref, pooled_ref, patches_ref, pw_ref, pv_ref, readp_ref, embed_ref,
):
    li = lax.axis_index("lon")
    width = heads * HDIM
    seq = n * here
    tile = min(seq, 512)
    rows = items * here
    lat = 2 * LATP
    wide = fields_ref.shape[2]
    loads, keeps = Moves(load), Moves(keep)
    fetch_key, fetch_val, fetch_mer = (loads.go(h, v) for h, v in ((key_hbm, keying), (val_hbm, valuing), (mer_hbm, merging)))
    if direct:
        fetch_own = [loads.go(proj_hbm.at[:, pl.ds(pl.multiple_of(p * D + li * width, width), width)], own_w.at[:, p * width : (p + 1) * width]) for p in range(3)]
    else:
        fetch_own = [loads.go(proj_hbm, own_w)]
    for i in range(items):
        seam[0, i] = fields_ref[i, :, wide - 1, :]
        seam[1, i] = cot_ref[i, :, wide - 1, :]
    barrier_all(n, li)
    east = pltpu.make_async_remote_copy(
        src_ref=seam, dst_ref=seam_land, send_sem=seam_send, recv_sem=seam_recv,
        device_id={"lon": lax.rem(li + 1, n)}, device_id_type=MESH,
    )
    east.start()

    row = lambda ref: ref[...].reshape(1, -1)
    embed = contract(places(4 * NVAR, JPAD, 0, 4, 2), patching_ref[...], ((0,), (0,)))
    embed = (embed + contract(places(NVAR, JPAD, 4 * VPAD, 1, 0), tagging_ref[...], ((0,), (0,)))).astype(BF16)
    embed_ref[...] = embed
    keeps.go(embed_ref, embed_out)
    readp_ref[...] = contract(places(4 * NOUT, 4 * VPAD, 0, 4, 2), read_ref[...], ((0,), (0,))).astype(BF16)
    keeps.go(readp_ref, readp_out)

    spread = latitudes(lat)
    var = lax.broadcasted_iota(jnp.int32, (VPAD, NVAR), 0)
    same = (var == lax.broadcasted_iota(jnp.int32, (VPAD, NVAR), 1)).astype(BF16)
    lane = lax.broadcasted_iota(jnp.int32, (8, VPAD), 1)
    patches_ref[:, 4 * VPAD :] = jnp.ones((rows, VPAD), BF16)
    east.wait()

    def tokens(ref, which, i, choose, out):
        canvas = jnp.concatenate([seam_land[which, i]] + [ref[i, :, w, :] for w in range(wide - 1)], axis=1)
        canvas = product(choose, canvas).astype(BF16)
        for w in range(wide):
            token = contract(spread, canvas[:, w * lat : (w + 1) * lat], ((1,), (1,))).astype(BF16)
            for e in range(2):
                corner = (w % 2) * 2 + e
                at = i * here + (w // 2) * LATP
                out[at : at + LATP, corner * VPAD : (corner + 1) * VPAD] = token[e * LATP : (e + 1) * LATP]

    for i in range(items):
        tokens(cot_ref, 1, i, same, dpred_ref)
    half_rows = rows // 2
    ups = Gather(n, li, lambda slot, piece: up_ref.at[slot, pl.ds(piece * half_rows, half_rows)], usend, urecv)
    up_ref[0] = dpred_ref[...]
    ups.start([0, 1])
    base_ref[...] = jnp.sum(dpred_ref[...].astype(F32), axis=0, keepdims=True)
    fetch_key.wait()
    keymap = contract(by_head(row(beacon_ref)), keying[...], ((1,), (1,)))
    keymap_ref[...] = keymap
    qrow = folded(contract(pieces(keymap, 3), embed, ((1,), (1,))), 3)
    for h in range(HEADS):
        qrow_ref[h] = qrow[h : h + 1, :]
    fetch_val.wait()
    pv = product(embed, valuing[...]).astype(BF16)
    for g in range(n):
        pv_ref[g] = pv[:, g * width : (g + 1) * width]
    keeps.go(pv_ref, pv_out)
    masks = []
    for i in range(items):
        choose = (var == ids_ref[i : i + 1, :]).astype(BF16)
        tokens(fields_ref, 0, i, choose, patches_ref)
        kept = jnp.broadcast_to(mask_ref[i : i + 1, :], (8, NVAR)).astype(F32).astype(BF16)
        live = contract(kept, choose, ((1,), (1,)))
        off = jnp.where(lane < NVAR, jnp.where(live > 0.5, 0.0, -1e30), -2e30)
        masks.append(jnp.broadcast_to(off[:1], (here, VPAD)))
    mask = jnp.concatenate(masks, axis=0)
    patches = patches_ref[...].astype(F32)
    keeps.go(patches_ref, patches_out)
    lifting = row(lifting_ref).astype(F32)

    for pair in range(HEADS // 2):
        halves = []
        for h in (2 * pair, 2 * pair + 1):
            x = patches[:, : 4 * VPAD] * qrow[h : h + 1, : 4 * VPAD]
            x = x[:, : 2 * VPAD] + x[:, 2 * VPAD :]
            logits = (x[:, :VPAD] + x[:, VPAD:] + qrow[h : h + 1, 4 * VPAD :]) * FACTOR
            logits = jnp.where(mask == 0.0, logits, mask)
            grown = jnp.exp(logits - jnp.max(logits, axis=-1, keepdims=True))
            w = grown / jnp.sum(grown, axis=-1, keepdims=True)
            pw_ref[h] = w.astype(BF16)
            blended = (jnp.concatenate([w] * 5, axis=1) * patches).astype(BF16)
            halves.append(product(blended, pv[:, h * HDIM : (h + 1) * HDIM]))
        cols = slice(pair * 128, pair * 128 + 128)
        pooled_ref[:, cols] = (jnp.concatenate(halves, axis=1) + lifting[:, cols]).astype(BF16)
    keeps.go(pw_ref, pw_out)
    keeps.go(pooled_ref, pooled_out)
    ups.relay([0, 1])
    fetch_mer.wait()
    placed = jnp.concatenate([place_ref[...].astype(F32)] * items, axis=0)
    emb = product(pooled_ref[...], merging[...]) + row(offset_ref).astype(F32) + placed
    emb_ref[...] = emb
    keeps.go(emb_ref, emb_out)
    normal, _ = normalize(emb)
    normed = (normal * row(scaling_ref).astype(F32) + row(centre_ref).astype(F32)).astype(BF16)
    for i in range(items):
        rows_ref[i, 0] = normed[i * here : (i + 1) * here]
    half = here // 2

    def at(slot, piece):
        return rows_ref.at[piece // 2, slot, pl.ds((piece % 2) * half, half)]

    gather = Gather(n, li, at, gsend, grecv)
    gather.start([0, 1])

    def give(i, mask):
        return pltpu.make_async_remote_copy(
            src_ref=obuf.at[i, mask],
            dst_ref=land.at[li, i],
            send_sem=osend.at[i, mask],
            recv_sem=orecv.at[i, mask],
            device_id={"lon": li ^ mask},
            device_id_type=MESH,
        )

    column = lax.broadcasted_iota(jnp.int32, (D, width), 1)
    mine = (lax.broadcasted_iota(jnp.int32, (D, width), 0) == li * width + column).astype(BF16)
    biases = jnp.broadcast_to(row(biasing_ref), (8, 2 * D))
    own_bias = jnp.concatenate(
        [product(biases[:, :D], mine)[:1], jnp.zeros((1, width), F32), product(biases[:, D:], mine)[:1]], axis=1
    )
    for c in fetch_own:
        c.wait()
    for i in range(items):
        parts = [2 * i, 2 * i + 1]
        later = [2 * i + 2, 2 * i + 3] if i + 1 < items else []
        if i == 0:
            gather.relay(parts)
        gather.start(later)
        gather.finish(parts)
        keeps.go(rows_ref.at[i], all_out.at[i])
        joint = product(rows_ref[i].reshape(seq, D), own_w[...]) + own_bias
        qkv_ref[i] = joint.astype(BF16)
        keeps.go(qkv_ref.at[i], qkv_out.at[i])
        for t in range(seq // tile):
            outs = []
            for h in range(heads):
                q = qkv_ref[i, t * tile : (t + 1) * tile, h * HDIM : (h + 1) * HDIM] * FACTOR
                k = qkv_ref[i, :, width + h * HDIM : width + (h + 1) * HDIM]
                v = qkv_ref[i, :, 2 * width + h * HDIM : 2 * width + (h + 1) * HDIM]
                scores = contract(q, k, ((1,), (1,)))
                top = jnp.max(scores, axis=1, keepdims=True)
                grown = jnp.exp(scores - top)
                total = jnp.sum(grown, axis=1, keepdims=True)
                outs.append(product(grown.astype(BF16), v) / total)
                lse = top + jnp.log(total)
                lse_ref[i, h : h + 1, t * tile : (t + 1) * tile] = jnp.transpose(lse)
                if t == 0 and h == 0 and i == 0:
                    gather.relay(later)
                    ups.finish([0, 1])
                    keeps.go(up_ref, up_out)
            out = jnp.concatenate(outs, axis=1) if heads > 1 else outs[0]
            obuf[i, t * (tile // here) : (t + 1) * (tile // here)] = out.astype(BF16).reshape(tile // here, here, width)
        for mask in range(1, n):
            give(i, mask).start()
        land[li, i] = obuf[i, 0]
    for i in range(items):
        for mask in range(1, n):
            give(i, mask).wait_recv()
        att_ref[i * here : (i + 1) * here, :] = jnp.concatenate([land[g, i] for g in range(n)], axis=1)
    ups.drain([0, 1])
    for i in range(items):
        gather.drain([2 * i, 2 * i + 1])
        for mask in range(1, n):
            give(i, mask).wait_send()
    for c in keeps.started:
        c.wait()


def front(fields, cot, ids, mask, patching, tagging, reading, beacon, lifting, offset, scaling, centre, biasing, place, keying, valuing, merging, proj, direct, n, items, here, heads):
    width = heads * HDIM
    seq = n * here
    rows = items * here
    vm, hbm = pl.BlockSpec(memory_space=pltpu.VMEM), pl.BlockSpec(memory_space=pl.ANY)
    shape = jax.ShapeDtypeStruct
    dma = pltpu.SemaphoreType.DMA
    low = lambda *a: pltpu.VMEM(a, BF16)
    edge = low(2, items, NVAR, 2 * LATP)
    return pl.pallas_call(
        functools.partial(front_kernel, n, items, here, heads, direct),
        in_specs=[vm] * 14 + [hbm] * 4,
        out_specs=(vm, hbm, hbm, vm, hbm, hbm, hbm, hbm, hbm, vm, hbm, vm, vm, hbm, vm, hbm),
        out_shape=(
            shape((rows, D), BF16), shape((items, n, here, D), BF16), shape((items, seq, 3 * width), BF16), shape((items, heads, seq), F32),
            shape((n, rows, 4 * VPAD), BF16), shape((rows, D), F32), shape((rows, D), BF16), shape((rows, JPAD), BF16),
            shape((HEADS, rows, VPAD), BF16), shape((HEADS, 1, JPAD), F32), shape((n, JPAD, width), BF16), shape((rows, 4 * VPAD), BF16),
            shape((1, 4 * VPAD), F32), shape((4 * VPAD, D), BF16), shape((HEADS, D), F32), shape((JPAD, D), BF16),
        ),
        scratch_shapes=[
            low(D, D), low(D, D), low(D, D), low(D, 3 * width), dma((8,)), edge, edge, dma, dma,
            low(n, rows, 4 * VPAD), dma((n, 2)), dma((n, 2)),
            low(items, n, here, D), low(items, n, here, width), low(n, items, here, width),
            dma((n, 2 * items)), dma((n, 2 * items)), dma((items, n)), dma((items, n)), dma((2 * items + 9,)),
            low(items, seq, 3 * width), pltpu.VMEM((rows, D), F32), low(rows, D), low(rows, JPAD), low(HEADS, rows, VPAD),
            low(n, JPAD, width), low(4 * VPAD, D), low(JPAD, D),
        ],
        compiler_params=pltpu.CompilerParams(collective_id=1, has_side_effects=True, vmem_limit_bytes=60 * MIB),
        name="front",
    )(fields, cot, ids, mask, patching, tagging, reading, beacon, lifting, offset, scaling, centre, biasing, place, keying, valuing, merging, proj)


def middle_kernel(
    n, items, here, heads, block,
    att_ref, emb_ref, mix_hbm, nudging_ref, rescaling_ref, recentre_ref, settle_ref, uplift_ref, baseline_ref, w1_hbm, w2_hbm, read_ref, dpred_ref,
    z_ref, sq_ref, dmid_ref, do_ref, vecg_ref, uplg_ref, rows_out,
    w1, w2, mix, rows_ref, normal_ref, acc, slope_ref, upl_ref, gsend, grecv, load, keep,
):
    li = lax.axis_index("lon")
    rows = items * here
    width = heads * HDIM
    blocks = FF // block

    def fetch1(b):
        return pltpu.make_async_copy(w1_hbm.at[:, pl.ds(pl.multiple_of(b * block, block), block)], w1.at[b], load.at[b])

    def fetch2(b):
        return pltpu.make_async_copy(w2_hbm.at[pl.ds(pl.multiple_of(b * block, block), block)], w2.at[b], load.at[blocks + b])

    fetch_mix = pltpu.make_async_copy(mix_hbm, mix, load.at[2 * blocks])
    fetch_mix.start()
    for b in range(blocks):
        fetch1(b).start()
        fetch2(b).start()
    barrier_all(n, li)

    row = lambda ref: ref[...].reshape(1, -1).astype(F32)
    nudging, rescaling, recentre, settle = (row(a) for a in (nudging_ref, rescaling_ref, recentre_ref, settle_ref))
    uplift = row(uplift_ref)
    for b in range(blocks):
        upl_ref[b] = uplift[:, b * block : (b + 1) * block]
    quarter = rows // 4
    every = list(range(4))
    gather = Gather(n, li, lambda slot, piece: rows_ref.at[slot, pl.ds(piece * quarter, quarter)], gsend, grecv)
    fetch_mix.wait()
    mid = emb_ref[...] + (product(att_ref[...], mix[...]) + nudging)
    dmid_ref[...] = mid
    normal, inverse = normalize(mid)
    normal_ref[...] = normal
    rows_ref[0] = (normal * rescaling + recentre).astype(BF16)
    gather.start(every)
    acc[...] = jnp.zeros_like(acc)

    def ahead(b, _):
        fetch1(b).wait()
        hidden = product(rows_ref[0], w1[b]) + upl_ref[b]
        value, slope = gelu_parts(hidden)
        slope_ref[b] = slope
        fetch2(b).wait()
        acc[...] += product(value.astype(BF16), w2[b])
        return 0

    lax.fori_loop(0, blocks, ahead, 0)
    final = (dmid_ref[...] + (acc[...] + settle)).astype(BF16)
    baseline = jnp.broadcast_to(baseline_ref[...].reshape(1, -1), (8, 4 * NOUT))
    baseline = product(baseline, places(4 * NOUT, 4 * VPAD, 0, 4, 2))[:1]
    z_ref[...] = (contract(final, read_ref[...], ((1,), (1,))) + baseline).astype(BF16)
    dpred = dpred_ref[...]
    sq_ref[:, D:] = contract(final, dpred, ((0,), (0,))).astype(BF16)
    dfinal = product(dpred, read_ref[...])
    dfinal_low = dfinal.astype(BF16)
    acc[...] = jnp.zeros_like(acc)

    def back(b, _):
        dhidden = (contract(dfinal_low, w2[b], ((1,), (1,))) * slope_ref[b]).astype(BF16)
        uplg_ref[b] = jnp.sum(dhidden.astype(F32), axis=0, keepdims=True)
        acc[...] += contract(dhidden, w1[b], ((1,), (1,)))
        return 0

    gather.relay(every[:2], rest=False)
    lax.fori_loop(0, blocks // 2, back, 0)
    gather.relay(every[2:], rest=False)
    lax.fori_loop(blocks // 2, blocks, back, 0)
    gather.relay(every, first=False)
    dsecond = acc[...]
    normal = normal_ref[...]
    dmid = dfinal + norm_back(dsecond, normal, inverse, rescaling)
    dmid_ref[...] = dmid
    dmid_low = dmid.astype(BF16)
    vecg_ref[...] = jnp.concatenate([
        jnp.sum(dmid_low.astype(F32), axis=0, keepdims=True),
        jnp.sum(dsecond * normal, axis=0, keepdims=True),
        jnp.sum(dsecond, axis=0, keepdims=True),
        jnp.sum(dfinal_low.astype(F32), axis=0, keepdims=True),
    ], axis=0)
    dout = contract(dmid_low, mix[...], ((1,), (1,))).astype(BF16)
    for g in range(n):
        do_ref[g] = dout[:, g * width : (g + 1) * width].reshape(items, here, width)
    sq_ref[:, :D] = contract(att_ref[...], dmid_low, ((0,), (0,))).astype(BF16)
    gather.finish(every)
    out = pltpu.make_async_copy(rows_ref, rows_out, keep)
    out.start()
    gather.drain(every)
    out.wait()


def middle_part(att, emb, mixing, nudging, rescaling, recentre, settle, uplift, baseline, widening, narrowing, read, dpred, n, items, here, heads):
    rows = items * here
    width = heads * HDIM
    block = 512
    blocks = FF // block
    vm = pl.BlockSpec(memory_space=pltpu.VMEM)
    hbm = pl.BlockSpec(memory_space=pl.ANY)
    shape = jax.ShapeDtypeStruct
    return pl.pallas_call(
        functools.partial(middle_kernel, n, items, here, heads, block),
        in_specs=[vm, vm, hbm, vm, vm, vm, vm, vm, vm, hbm, hbm, vm, vm],
        out_specs=(vm,) * 6 + (hbm,),
        out_shape=(
            shape((rows, 4 * VPAD), BF16), shape((D, D + 4 * VPAD), BF16), shape((rows, D), F32),
            shape((n, items, here, width), BF16), shape((4, D), F32), shape((blocks, 1, block), F32), shape((n, rows, D), BF16),
        ),
        scratch_shapes=[
            pltpu.VMEM((blocks, D, block), BF16), pltpu.VMEM((blocks, block, D), BF16), pltpu.VMEM((D, D), BF16),
            pltpu.VMEM((n, rows, D), BF16), pltpu.VMEM((rows, D), F32), pltpu.VMEM((rows, D), F32),
            pltpu.VMEM((blocks, rows, block), F32), pltpu.VMEM((blocks, 1, block), F32),
            pltpu.SemaphoreType.DMA((n, 4)), pltpu.SemaphoreType.DMA((n, 4)),
            pltpu.SemaphoreType.DMA((2 * blocks + 1,)), pltpu.SemaphoreType.DMA,
        ],
        compiler_params=pltpu.CompilerParams(collective_id=2, has_side_effects=True, vmem_limit_bytes=60 * MIB),
        name="middle",
    )(att, emb, mixing, nudging, rescaling, recentre, settle, uplift, baseline, widening, narrowing, read, dpred)


def greet(n, li, count, zi):
    sem = pltpu.get_barrier_semaphore()
    for mask in range(1, n):
        pl.semaphore_signal(sem, inc=1, device_id={"lon": li ^ mask}, device_id_type=MESH)
    for mask in range(1, count):
        pl.semaphore_signal(sem, inc=1, device_id={"batch": zi ^ mask}, device_id_type=MESH)
    pl.semaphore_wait(sem, n + count - 2)


class Halving:
    def __init__(self, count, zi, flip, own, stage, land, send, recv):
        self.count, self.zi, self.own, self.stage, self.land = count, zi, own, stage, land
        self.send_sem, self.recv_sem = send, recv
        self.bits = [1 << i for i in range(count.bit_length() - 1)]
        if flip:
            self.bits = self.bits[::-1]

    def at_step(self, step):
        return [r for r in range(1, self.count) if min(i for i, b in enumerate(self.bits) if b & r) == step]

    def copy(self, r, step):
        return pltpu.make_async_remote_copy(
            src_ref=self.own(self.zi ^ r) if step == 0 else self.stage.at[r],
            dst_ref=self.land.at[r],
            send_sem=self.send_sem.at[r],
            recv_sem=self.recv_sem.at[r],
            device_id={"batch": self.zi ^ self.bits[step]},
            device_id_type=MESH,
        )

    def send(self, step):
        for r in self.at_step(step):
            self.copy(r, step).start()

    def absorb(self, step):
        for r in self.at_step(step):
            self.copy(r, step).wait_recv()
            to = r ^ self.bits[step]
            base = self.own(self.zi ^ to)[...] if step == 0 else self.stage[to]
            total = base.astype(F32) + self.land[r].astype(F32)
            if step == len(self.bits) - 1:
                return total
            self.stage[to] = total.astype(BF16)

    def drain(self):
        for step in range(len(self.bits)):
            for r in self.at_step(step):
                self.copy(r, step).wait_send()


class RowSum:
    def __init__(self, n, li, count, zi, own, land1, stage1, land2, stage2, land3, sems):
        self.n, self.li, self.count, self.zi, self.own = n, li, count, zi, own
        self.land1, self.stage1, self.land2, self.stage2, self.land3 = land1, stage1, land2, stage2, land3
        self.s1, self.r1, self.s2, self.r2, self.s3, self.r3 = sems
        self.half = n // 2

    @staticmethod
    def scratch(n, count, rows, cols):
        half = pltpu.VMEM((n // 2, count, rows, cols), BF16)
        one = pltpu.VMEM((count, rows, cols), BF16)
        lon_sem, z_sem = pltpu.SemaphoreType.DMA((n // 2,)), pltpu.SemaphoreType.DMA((count,))
        return [half, half, half, one, one, lon_sem, lon_sem, lon_sem, lon_sem, z_sem, z_sem]

    def copy1(self, j):
        return pltpu.make_async_remote_copy(
            src_ref=self.own(self.li ^ (2 * j + 1)), dst_ref=self.land1.at[j], send_sem=self.s1.at[j],
            recv_sem=self.r1.at[j], device_id={"lon": self.li ^ 1}, device_id_type=MESH,
        )

    def copy2(self, j):
        return pltpu.make_async_remote_copy(
            src_ref=self.stage1.at[j], dst_ref=self.land2.at[j], send_sem=self.s2.at[j],
            recv_sem=self.r2.at[j], device_id={"lon": self.li ^ (2 * j)}, device_id_type=MESH,
        )

    def copy3(self, r):
        return pltpu.make_async_remote_copy(
            src_ref=self.stage2.at[self.zi ^ r], dst_ref=self.land3.at[r], send_sem=self.s3.at[r],
            recv_sem=self.r3.at[r], device_id={"batch": self.zi ^ r}, device_id_type=MESH,
        )

    def core(self):
        for j in range(self.half):
            self.copy1(j).start()

    def plane(self):
        for j in list(range(1, self.half)) + [0]:
            self.copy1(j).wait_recv()
            self.stage1[j] = (self.own(self.li ^ (2 * j))[...].astype(F32) + self.land1[j].astype(F32)).astype(BF16)
            if j:
                self.copy2(j).start()

    def depth(self):
        total = self.stage1[0].astype(F32)
        for j in range(1, self.half):
            self.copy2(j).wait_recv()
            total = total + self.land2[j].astype(F32)
        self.stage2[...] = total.astype(BF16)
        for r in range(1, self.count):
            self.copy3(r).start()

    def total(self):
        total = self.stage2[self.zi].astype(F32)
        for r in range(1, self.count):
            self.copy3(r).wait_recv()
            total = total + self.land3[r].astype(F32)
        return total

    def drain(self):
        for j in range(self.half):
            self.copy1(j).wait_send()
            if j:
                self.copy2(j).wait_send()
        for r in range(1, self.count):
            self.copy3(r).wait_send()


ARROWS = 384


def rear_kernel(
    n, count, items, here, heads, direct,
    do_ref, sq_ref, second_hbm, up_hbm, wown_hbm, nown_hbm, uplown_ref, read_ref, qkv_hbm, lse_ref, rows_hbm,
    proj_hbm, merge_hbm, emb_hbm, dmid_hbm, pooled_hbm, scaling_ref, patches_hbm, w_hbm, qrow_ref, pv_hbm, vecg_ref, uplg_ref, base_ref,
    ids_ref, z_hbm,
    nar_ref, sqo_ref, pos_ref, mer_ref, pred_ref, grad_ref, ar_ref, wcol_ref, pcol_ref,
    dpatch_ref, zsend, gsend, zland, gland, seams, wown, nown, bufa, bufb, dz, accn, accw, narg, widg, do_land, ebuf, eland, dk_acc, dv_acc, projg,
    mbuf, du3, arbuf, arland, arz, archunk, posbuf, posland, posall, wcolbuf, pcolbuf, upl,
    qkv_ref, emb_ref, dmid_ref, pooled_ref, patches_ref, w_ref, pv_ref, z_ref,
    load, osend, orecv, esend, erecv, nstage, nland, nsend, nrecv, wstage, wland, wsend, wrecv, xstage, xland, xsend, xrecv,
    pstage, pland, psend, precv, qstage, qland, qsend, qrecv,
    asend, arecv, azs, azr, ags, agr, bgs, bgr, pss, psr, pgs, pgr, ws, wr, cs, cr, *sums,
):
    li, zi = lax.axis_index("lon"), lax.axis_index("batch")
    rows = items * here
    width = heads * HDIM
    seq = n * here
    rd = D // (n * count)
    hid = FF // (n * count)
    tile = 512 if seq <= 1024 else 256
    total = lambda a: jnp.sum(a, axis=0, keepdims=True)

    loads = Moves(load)
    starts = [pl.multiple_of((c * n + li) * hid, hid) for c in range(count)]
    fetch_own = [loads.go(nown_hbm.at[pl.ds(at, hid)], nown.at[pl.ds(c * hid, hid)]) for c, at in enumerate(starts)]
    if direct:
        fetch_own += [loads.go(wown_hbm.at[:, pl.ds(at, hid)], wown.at[:, c * hid : (c + 1) * hid]) for c, at in enumerate(starts)]
    else:
        fetch_own.append(loads.go(wown_hbm, wown))
    fetch_own.append(loads.go(up_hbm, dz))
    fetch_rows = [loads.go(second_hbm.at[m], bufa.at[m]) for m in range(n)]
    fetch_z = loads.go(z_hbm, z_ref)
    fetch_qkv = loads.go(qkv_hbm, qkv_ref)
    per = D // rows
    fetch_p = [
        [loads.go(proj_hbm.at[pl.ds(j * rows, rows), p * D : (p + 1) * D], bufb.at[p * per + j]) for j in range(per)]
        for p in range(2)
    ]
    fetch_late = [
        loads.go(h, v)
        for h, v in ((emb_hbm, emb_ref), (dmid_hbm, dmid_ref), (pooled_hbm, pooled_ref), (patches_hbm, patches_ref), (w_hbm, w_ref), (pv_hbm, pv_ref))
    ]
    for c in range(count):
        upl[:, c * hid : (c + 1) * hid] = uplown_ref[c * n + li]
    greet(n, li, count, zi)
    nar = Halving(count, zi, False, lambda b: narg.at[b], nstage, nland, nsend, nrecv)
    cut = count // 2
    wide_a = Halving(count, zi, False, lambda b: widg.at[pl.ds(0, cut), pl.ds(b * (D // count), D // count)], wstage, wland, wsend, wrecv)
    wide_b = Halving(count, zi, True, lambda b: widg.at[pl.ds(cut, cut), pl.ds(b * (D // count), D // count)], xstage, xland, xsend, xrecv)
    squares = RowSum(n, li, count, zi, lambda l: sq_ref.at[:, l], *sums[:5], sums[10:16])
    merging = RowSum(n, li, count, zi, lambda l: mbuf.at[:, l], *sums[5:10], sums[16:22])
    hz = D // count // 2
    first = Halving(count, zi, False, lambda b: projg.at[pl.ds(b * 2 * hz, hz)], pstage, pland, psend, precv)
    second = Halving(count, zi, True, lambda b: projg.at[pl.ds(b * 2 * hz + hz, hz)], qstage, qland, qsend, qrecv)
    steps = len(nar.bits)

    def onward(*sums):
        for step in range(steps - 1):
            for one in sums:
                one.absorb(step)
                one.send(step + 1)

    def give_do(mask):
        return pltpu.make_async_remote_copy(
            src_ref=do_ref.at[li ^ mask], dst_ref=do_land.at[mask], send_sem=osend.at[mask], recv_sem=orecv.at[mask],
            device_id={"lon": li ^ mask}, device_id_type=MESH,
        )

    for mask in range(1, n):
        give_do(mask).start()
    do_land[0] = do_ref[li]
    squares.core()

    for c in fetch_own:
        c.wait()
    slopes = contract(nown[...], read_ref[...], ((1,), (1,))).astype(BF16)
    for c in fetch_rows:
        c.wait()
    half = count * hid // 2
    for part in range(2):
        cols = slice(part * half, (part + 1) * half)
        accn[...] = jnp.zeros_like(accn)
        accw[...] = jnp.zeros_like(accw)

        def own(m, _):
            normed, upstream = bufa[m], dz[m]
            value, slope = gelu_parts(product(normed, wown[:, cols]) + upl[:, cols])
            dhidden = (contract(upstream, slopes[cols], ((1,), (1,))) * slope).astype(BF16)
            accn[...] += contract(value.astype(BF16), upstream, ((0,), (0,)))
            accw[...] += contract(normed, dhidden, ((0,), (0,)))
            return 0

        lax.fori_loop(0, n, own, 0)
        for j in range(cut):
            narg[part * cut + j] = accn[j * hid : (j + 1) * hid, :].astype(BF16)
            widg[part * cut + j] = accw[:, j * hid : (j + 1) * hid].astype(BF16)
        if part == 0:
            wide_a.send(0)
            squares.plane()
    wide_b.send(0)
    nar.send(0)
    fetch_n1 = [loads.go(rows_hbm.at[i], bufa.at[:, pl.ds(i * here, here)]) for i in range(items)]

    lat = 2 * LATP
    wide = pred_ref.shape[2]
    spread = latitudes(lat)

    def seam(j, src, dst):
        return pltpu.make_async_remote_copy(
            src_ref=src, dst_ref=dst, send_sem=seams.at[2 * j], recv_sem=seams.at[2 * j + 1],
            device_id={"lon": lax.rem(li + n - 1, n)}, device_id_type=MESH,
        )

    def stacked(ref, i, w):
        at = i * here + (w // 2) * LATP
        corner = (w % 2) * 2
        return jnp.concatenate([ref[at : at + LATP, (corner + e) * VPAD : (corner + e + 1) * VPAD] for e in range(2)], axis=0)

    fetch_z.wait()
    for i in range(items):
        for w in range(wide // lat):
            pixels = contract(stacked(z_ref, i, w), spread, ((0,), (0,)))[:NOUT].astype(BF16)
            if w == 0:
                zsend[i] = pixels
            else:
                pred_ref[i, :, (w - 1) * lat : w * lat] = pixels
    west_z = seam(0, zsend, zland)
    west_z.start()

    def give(i, mask):
        return pltpu.make_async_remote_copy(
            src_ref=ebuf.at[i, mask], dst_ref=eland.at[li, i], send_sem=esend.at[i, mask], recv_sem=erecv.at[i, mask],
            device_id={"lon": li ^ mask}, device_id_type=MESH,
        )

    fetch_qkv.wait()
    for mask in range(1, n):
        give_do(mask).wait_recv()
    for i in range(items):
        dk_acc[...] = jnp.zeros_like(dk_acc)
        dv_acc[...] = jnp.zeros_like(dv_acc)
        for t in range(seq // tile):
            part = slice(t * tile, (t + 1) * tile)
            outs = []
            do_rows = do_land[t * (tile // here) : (t + 1) * (tile // here), i].reshape(tile, width)
            for h in range(heads):
                cols = slice(h * HDIM, (h + 1) * HDIM)
                q = qkv_ref[i, part, h * HDIM : (h + 1) * HDIM] * FACTOR
                k = qkv_ref[i, :, width + h * HDIM : width + (h + 1) * HDIM]
                v = qkv_ref[i, :, 2 * width + h * HDIM : 2 * width + (h + 1) * HDIM]
                do = do_rows[:, cols]
                scores = contract(k, q, ((1,), (1,)))
                probs = jnp.exp(scores - lse_ref[i, h : h + 1, part])
                dprobs = contract(v, do, ((1,), (1,)))
                delta = jnp.sum(probs * dprobs, axis=0, keepdims=True)
                dscores = (probs * (dprobs - delta)).astype(BF16)
                dv_acc[h] += product(probs.astype(BF16), do)
                dk_acc[h] += product(dscores, q)
                outs.append(contract(dscores, k, ((0,), (0,))) * FACTOR)
            out = jnp.concatenate(outs, axis=1) if heads > 1 else outs[0]
            ebuf[i, t * (tile // here) : (t + 1) * (tile // here), :, :width] = out.astype(BF16).reshape(tile // here, here, width)
        for h in range(heads):
            ebuf[i, :, :, width + h * HDIM : width + (h + 1) * HDIM] = dk_acc[h].astype(BF16).reshape(n, here, HDIM)
            ebuf[i, :, :, 2 * width + h * HDIM : 2 * width + (h + 1) * HDIM] = dv_acc[h].astype(BF16).reshape(n, here, HDIM)
        for mask in range(1, n):
            give(i, mask).start()
        eland[li, i] = ebuf[i, 0]
        if i == 0:
            squares.depth()
            onward(wide_a)
    onward(wide_b, nar)
    for c in fetch_n1:
        c.wait()
    joint = jnp.zeros((D, 3 * width), F32)
    for i in range(items):
        joint = joint + contract(bufa[:, i * here : (i + 1) * here].reshape(seq, D), ebuf[i].reshape(seq, 3 * width), ((0,), (0,)))
    projg[...] = joint.astype(BF16)
    fetch_p.append([loads.go(proj_hbm.at[pl.ds(j * rows, rows), 2 * D : 3 * D], bufa.at[j]) for j in range(per)])
    fetch_m = [loads.go(merge_hbm.at[pl.ds(j * rows, rows)], bufa.at[per + j]) for j in range(per)]
    first.send(0)
    second.send(0)
    for c in fetch_p[0] + fetch_p[1] + fetch_late:
        c.wait()

    for i in range(items):
        for mask in range(1, n):
            give(i, mask).wait_recv()
    normal, inverse = normalize(emb_ref[...])
    scaling = scaling_ref[...].reshape(1, -1).astype(F32)
    dnormed = jnp.zeros((rows, D), F32)
    e3_sums = []
    for p, buf, at in ((0, bufb, 0), (1, bufb, per), (2, bufa, 0)):
        if p == 2:
            for c in fetch_p[2]:
                c.wait()
        e3 = jnp.concatenate(
            [eland[g, :, :, p * width : (p + 1) * width].reshape(rows, width) for g in range(n)], axis=1
        )
        e3_sums.append(total(e3.astype(F32)))
        dnormed = dnormed + contract(e3, buf[at : at + per].reshape(D, D), ((1,), (1,)))
    demb = dmid_ref[...] + norm_back(dnormed, normal, inverse, scaling)
    demb_low = demb.astype(BF16)
    summed = demb[:here]
    for i in range(1, items):
        summed = summed + demb[i * here : (i + 1) * here]
    posbuf[...] = summed.astype(BF16).reshape(count, here // count, D)

    def pos_give(r):
        return pltpu.make_async_remote_copy(
            src_ref=posbuf.at[zi ^ r], dst_ref=posland.at[r], send_sem=pss.at[r], recv_sem=psr.at[r],
            device_id={"batch": zi ^ r}, device_id_type=MESH,
        )

    def pos_share(r):
        return pltpu.make_async_remote_copy(
            src_ref=posall.at[zi], dst_ref=posall.at[zi], send_sem=pgs.at[r], recv_sem=pgr.at[r],
            device_id={"batch": zi ^ r}, device_id_type=MESH,
        )

    for r in range(1, count):
        pos_give(r).start()
    mbuf[...] = contract(pooled_ref[...], demb_low, ((0,), (0,))).astype(BF16).reshape(mbuf.shape)
    merging.core()
    for c in fetch_m:
        c.wait()
    dpooled = contract(demb_low, bufa[per : 2 * per].reshape(D, D), ((1,), (1,))).astype(BF16)
    vectors = jnp.concatenate([
        total(dpooled.astype(F32)), total(demb_low.astype(F32)), total(dnormed * normal), total(dnormed), e3_sums[0], e3_sums[2], vecg_ref[...],
    ] + [jnp.concatenate([uplg_ref[2 * j], uplg_ref[2 * j + 1]], axis=1) for j in range(FF // D)] + [
        jnp.concatenate([base_ref[...], jnp.zeros((1, D - 4 * VPAD), F32)], axis=1), jnp.zeros((1, D), F32),
    ], axis=0).astype(BF16)
    for g in range(n):
        du3[g] = dpooled[:, g * width : (g + 1) * width]
        arbuf[g, JPAD : JPAD + 16] = vectors[:, g * width : (g + 1) * width]
    merging.plane()
    patches = patches_ref[...].astype(F32)
    dpatch_ref[...] = jnp.zeros_like(dpatch_ref)
    lines = -(-JPAD // width)

    def pool_give(mask):
        return pltpu.make_async_remote_copy(
            src_ref=arbuf.at[li ^ mask], dst_ref=arland.at[mask], send_sem=asend.at[mask], recv_sem=arecv.at[mask],
            device_id={"lon": li ^ mask}, device_id_type=MESH,
        )

    def group(mask):
        g = li ^ mask
        halves, extra = [], []
        patch_total = jnp.zeros((rows, 4 * VPAD), F32)
        du_all, pv_all = du3[g], pv_ref[g]
        for s in range(heads):
            h = g * heads + s
            w = w_ref[h].astype(F32)
            wide = jnp.concatenate([w] * 5, axis=1)
            blended = (wide * patches).astype(BF16)
            du = du_all[:, s * HDIM : (s + 1) * HDIM]
            dbl = contract(du, pv_all[:, s * HDIM : (s + 1) * HDIM], ((1,), (1,)))
            halves.append(contract(blended, du, ((0,), (0,))))
            x = dbl * patches
            dw = x[:, :VPAD]
            for c in range(1, 5):
                dw = dw + x[:, c * VPAD : (c + 1) * VPAD]
            da = w * (dw - jnp.sum(w * dw, axis=-1, keepdims=True)) * FACTOR
            da_wide = jnp.concatenate([da] * 5, axis=1)
            line = total(da_wide * patches)
            line = jnp.concatenate([line, jnp.zeros((1, lines * width - JPAD), F32)], axis=1) if lines * width > JPAD else line
            extra += [line[:, c * width : (c + 1) * width] for c in range(lines)]
            patch_total = patch_total + (wide[:, : 4 * VPAD] * dbl[:, : 4 * VPAD] + da_wide[:, : 4 * VPAD] * qrow_ref[h][:, : 4 * VPAD])
        dpatch_ref[...] += patch_total
        arbuf[g, :JPAD] = (jnp.concatenate(halves, axis=1) if heads > 1 else halves[0]).astype(BF16)
        tail = jnp.concatenate(extra + [jnp.zeros((ARROWS - JPAD - 16 - heads * lines, width), F32)], axis=0)
        arbuf[g, JPAD + 16 :] = tail.astype(BF16)

    for mask in range(1, n):
        group(mask)
        pool_give(mask).start()
        if mask == 2:
            pos_sum = posbuf[zi].astype(F32)
            for r in range(1, count):
                pos_give(r).wait_recv()
                pos_sum = pos_sum + posland[r].astype(F32)
            posall[zi] = pos_sum.astype(BF16)
            for r in range(1, count):
                pos_share(r).start()
            sqo_ref[...] = squares.total()
        if mask == 4:
            merging.depth()
        if mask == 5:
            onward(first, second)
    group(0)
    for i in range(items):
        var = lax.broadcasted_iota(jnp.int32, (VPAD, NVAR), 0)
        choose = (var == ids_ref[i : i + 1, :]).astype(BF16)
        for w in range(wide // lat):
            parts = pieces(stacked(dpatch_ref, i, w), 2)
            pixels = contract(parts[:lat], spread, ((0,), (0,))) + contract(parts[lat:], spread, ((0,), (0,)))
            parts = pieces(pixels, 2)
            slots = contract(choose, parts[:VPAD], ((0,), (0,))) + contract(choose, parts[VPAD:], ((0,), (0,)))
            if w == 0:
                gsend[i] = slots
            else:
                grad_ref[i, :, (w - 1) * lat : w * lat] = slots
    west_g = seam(1, gsend, gland)
    west_g.start()
    west_z.wait()
    pred_ref[:, :, wide - lat :] = zland[...]

    def wide_give(mask):
        return pltpu.make_async_remote_copy(
            src_ref=wcolbuf.at[li ^ mask], dst_ref=wcol_ref.at[li], send_sem=ws.at[mask], recv_sem=wr.at[mask],
            device_id={"lon": li ^ mask}, device_id_type=MESH,
        )

    def col_give(mask):
        return pltpu.make_async_remote_copy(
            src_ref=pcolbuf.at[li ^ mask], dst_ref=pcol_ref.at[li], send_sem=cs.at[mask], recv_sem=cr.at[mask],
            device_id={"lon": li ^ mask}, device_id_type=MESH,
        )

    chunk = arbuf[li].astype(F32)
    for mask in range(1, n):
        pool_give(mask).wait_recv()
        chunk = chunk + arland[mask].astype(F32)
    piece = ARROWS // count
    archunk[...] = chunk.astype(BF16).reshape(archunk.shape)

    def z_give(r):
        return pltpu.make_async_remote_copy(
            src_ref=archunk.at[zi ^ r], dst_ref=arz.at[r], send_sem=azs.at[r], recv_sem=azr.at[r],
            device_id={"batch": zi ^ r}, device_id_type=MESH,
        )

    def z_share(r):
        return pltpu.make_async_remote_copy(
            src_ref=ar_ref.at[li, zi], dst_ref=ar_ref.at[li, zi], send_sem=ags.at[r], recv_sem=agr.at[r],
            device_id={"batch": zi ^ r}, device_id_type=MESH,
        )

    for r in range(1, count):
        z_give(r).start()
    nar_ref[...] = nar.absorb(steps - 1)
    for k, one in enumerate((wide_a, wide_b)):
        w_total = one.absorb(steps - 1).astype(BF16)
        for l in range(n):
            wcolbuf[l, k * cut : (k + 1) * cut] = w_total[:, l * rd : (l + 1) * rd]
    for mask in range(1, n):
        wide_give(mask).start()
    wcol_ref[li] = wcolbuf[li]
    piece_sum = archunk[zi].astype(F32)
    for r in range(1, count):
        z_give(r).wait_recv()
        piece_sum = piece_sum + arz[r].astype(F32)
    ar_ref[li, zi] = piece_sum.astype(BF16)
    for r in range(1, count):
        z_share(r).start()
    mer_ref[...] = merging.total()
    top, low = first.absorb(steps - 1).astype(BF16), second.absorb(steps - 1).astype(BF16)
    pcolbuf[...] = jnp.concatenate([top, low], axis=0).reshape(pcolbuf.shape)
    for mask in range(1, n):
        col_give(mask).start()
    pcol_ref[li] = pcolbuf[li]
    for r in range(1, count):
        z_share(r).wait_recv()

    def l_share(mask):
        return pltpu.make_async_remote_copy(
            src_ref=ar_ref.at[li], dst_ref=ar_ref.at[li], send_sem=bgs.at[mask], recv_sem=bgr.at[mask],
            device_id={"lon": li ^ mask}, device_id_type=MESH,
        )

    def l_relay(mask):
        return pltpu.make_async_remote_copy(
            src_ref=ar_ref.at[li ^ mask], dst_ref=ar_ref.at[li ^ mask], send_sem=bgs.at[mask | 1], recv_sem=bgr.at[mask | 1],
            device_id={"lon": li ^ 1}, device_id_type=MESH,
        )

    for mask in range(2, n, 2):
        l_share(mask).start()
    l_relay(0).start()
    for r in range(1, count):
        pos_share(r).wait_recv()
    pos_ref[...] = posall[...].reshape(here, D).astype(F32)
    for mask in range(2, n, 2):
        l_share(mask).wait_recv()
        l_relay(mask).start()
    for mask in range(0, n, 2):
        l_relay(mask).wait_recv()
    for mask in range(1, n):
        col_give(mask).wait()
        wide_give(mask).wait()
        pool_give(mask).wait_send()
        give_do(mask).wait_send()
        for i in range(items):
            give(i, mask).wait_send()
    for mask in range(0, n, 2):
        l_relay(mask).wait_send()
        if mask:
            l_share(mask).wait_send()
    for r in range(1, count):
        z_give(r).wait_send()
        z_share(r).wait_send()
        pos_give(r).wait_send()
        pos_share(r).wait_send()
    for part in (first, second, nar, wide_a, wide_b, squares, merging):
        part.drain()
    west_g.wait()
    grad_ref[:, :, wide - lat :] = gland[...]


def rear_part(
    do, squares, second, up, wown, nown, uplown, read, qkv, lse, rows_all, projecting, merging, emb, dmid, pooled, scaling, patches, pool_w, qrow, pv,
    vec_grads, uplift_grads, base, ids, z, direct, n, count, items, here, heads,
):
    rows, width, seq = items * here, heads * HDIM, n * here
    rd, hid = D // (n * count), FF // (n * count)
    own = count * hid
    wide = here // LATP * 2 * 2 * LATP
    shape = jax.ShapeDtypeStruct
    vm, hbm = pl.BlockSpec(memory_space=pltpu.VMEM), pl.BlockSpec(memory_space=pl.ANY)
    cols = squares.shape[3]
    piece = ARROWS // count
    hz = D // count // 2
    dma = pltpu.SemaphoreType.DMA
    lsem, zsem, isem = dma((n,)), dma((count,)), dma((items, n))
    low = lambda *s: pltpu.VMEM(s, BF16)
    full = lambda *s: pltpu.VMEM(s, F32)
    pos = low(count, here // count, D)
    nbuf, wbuf, pbuf = low(count, hid, 4 * VPAD), low(count, count // 2, D // count, hid), low(count, hz, 3 * width)
    one, two = RowSum.scratch(n, count, rd, cols), RowSum.scratch(n, count, rd, D)
    return pl.pallas_call(
        functools.partial(rear_kernel, n, count, items, here, heads, direct),
        in_specs=[vm, vm, hbm, hbm, hbm, hbm, vm, vm, hbm, vm, hbm, hbm, hbm, hbm, hbm, hbm, vm, hbm, hbm, vm, hbm, vm, vm, vm, vm, hbm],
        out_specs=(vm,) * 9,
        out_shape=(
            shape((hid, 4 * VPAD), F32), shape((rd, cols), F32), shape((here, D), F32), shape((rd, D), F32),
            shape((items, NOUT, wide), BF16), shape((items, NVAR, wide), F32), shape((n, count, piece, width), BF16), shape((n, count, rd, hid), BF16), shape((n, rd, 3 * width), BF16),
        ),
        scratch_shapes=[
            full(rows, 4 * VPAD), low(items, NOUT, 2 * LATP), full(items, NVAR, 2 * LATP), low(items, NOUT, 2 * LATP), full(items, NVAR, 2 * LATP), dma((4,)),
            low(D, own), low(own, D), low(n, rows, D), low(2 * D // rows, rows, D), low(n, rows, 4 * VPAD), full(own // 2, 4 * VPAD), full(D, own // 2),
            low(count, hid, 4 * VPAD), low(count, D, hid), low(n, items, here, width),
            low(items, n, here, 3 * width), low(n, items, here, 3 * width), full(heads, seq, HDIM), full(heads, seq, HDIM),
            low(D, 3 * width), low(count, n, rd, D), low(n, rows, width),
            low(n, ARROWS, width), low(n, ARROWS, width), low(count, piece, width), low(count, piece, width), pos, pos, pos,
            low(n, count, rd, hid), low(n, rd, 3 * width), full(1, own),
            low(items, seq, 3 * width), full(rows, D), full(rows, D), low(rows, D), low(rows, JPAD), low(HEADS, rows, VPAD), low(n, JPAD, width), low(rows, 4 * VPAD),
            dma((2 * count + n + items + 4 * (D // rows) + 9,)), lsem, lsem, isem, isem, nbuf, nbuf, zsem, zsem, wbuf, wbuf, zsem, zsem, wbuf, wbuf, zsem, zsem,
            pbuf, pbuf, zsem, zsem, pbuf, pbuf, zsem, zsem,
            lsem, lsem, zsem, zsem, zsem, zsem, lsem, lsem, zsem, zsem, zsem, zsem, lsem, lsem, lsem, lsem,
        ] + one[:5] + two[:5] + one[5:] + two[5:],
        compiler_params=pltpu.CompilerParams(collective_id=3, has_side_effects=True, vmem_limit_bytes=63 * MIB + 3 * MIB // 4),
        name="rear",
    )(do, squares, second, up, wown, nown, uplown, read, qkv, lse, rows_all, projecting, merging, emb, dmid, pooled, scaling, patches, pool_w, qrow, pv, vec_grads, uplift_grads, base, ids, z)


def finish_kernel(
    n, count, heads, sum_ref, wcol_ref, pcol_ref, nar_ref, sq_ref, mer_ref, pos_ref, pred_ref, grad_ref, embed_ref, read_ref, val_ref, key_ref, keymap_ref, beacon_ref,
    prediction_ref, fields_ref, position_ref, patching_ref, tagging_ref, beacon_out, keying_ref, valuing_ref, lifting_ref, merging_ref, offset_ref, scaling_ref,
    centre_ref, projecting_ref, biasing_ref, mixing_ref, nudging_ref, rescaling_ref, recentre_ref, widening_ref, uplift_ref,
    narrowing_ref, settle_ref, reading_ref, baseline_ref,
):
    li, zi = lax.axis_index("lon"), lax.axis_index("batch")
    block = zi * n + li
    rd = D // (n * count)
    hid = FF // (n * count)
    width = heads * HDIM
    lines = -(-JPAD // width)
    exact = lambda a, b, dims: lax.dot_general(a, b, (dims, ((), ())), precision=HIGH, preferred_element_type=F32)

    def mine(size):
        row = lax.broadcasted_iota(jnp.int32, (D, size), 0)
        col = lax.broadcasted_iota(jnp.int32, (D, size), 1)
        return (row == ((block * size + col) & (D - 1))).astype(BF16)

    lat = 2 * LATP
    for i in range(pred_ref.shape[0]):
        for w in range(pred_ref.shape[2] // lat):
            prediction_ref[i, :, w, :] = pred_ref[i, :, w * lat : (w + 1) * lat]
            fields_ref[i, :, w, :] = grad_ref[i, :, w * lat : (w + 1) * lat]
    position_ref[...] = pos_ref[...]
    merging_ref[...] = mer_ref[...]
    mixing_ref[...] = sq_ref[:, :D]
    narrowing_ref[...] = folded(product(pieces(nar_ref[...], 2), read_ref[...]), 2)
    reading_ref[...] = exact(sq_ref[:, D:], places(4 * NOUT, 4 * VPAD, 0, 4, 2).astype(F32), ((1,), (1,)))
    for g in range(n):
        for p in range(3):
            projecting_ref[:, p * D + g * width : p * D + (g + 1) * width] = pcol_ref[g, :, p * width : (p + 1) * width].astype(F32)
        for c in range(count):
            at = (c * n + g) * hid
            widening_ref[:, at : at + hid] = wcol_ref[g, c].astype(F32)

    sums = [sum_ref[g].reshape(ARROWS, width) for g in range(n)]
    vectors = jnp.concatenate([a[JPAD : JPAD + 16] for a in sums], axis=1)
    one, two, four = mine(rd), mine(2 * rd), mine(4 * rd)
    short = product(vectors, one)
    for j, ref in ((0, lifting_ref), (1, offset_ref), (2, scaling_ref), (3, centre_ref), (6, nudging_ref), (7, rescaling_ref), (8, recentre_ref), (9, settle_ref)):
        ref[...] = short[j : j + 1].reshape(rd)

    def across(start, size, select, ref):
        found = product(vectors, select)
        row = (block * size) // D
        total = jnp.zeros((1, size), F32)
        for k in range(size // rd):
            total = total + jnp.where(row == k, found[start + k : start + k + 1], 0.0)
        ref[...] = total.reshape(size)

    across(4, 2 * rd, two, biasing_ref)
    across(10, 4 * rd, four, uplift_ref)
    baseline_ref[...] = contract(vectors[:, : 4 * VPAD], places(4 * NOUT, 4 * VPAD, 0, 4, 2), ((1,), (1,)))[14:15].reshape(4 * NOUT)

    dqz = []
    for h in range(HEADS):
        base = JPAD + 16 + (h % heads) * lines
        lined = sums[h // heads]
        dqz.append(jnp.concatenate([lined[base + c : base + c + 1].astype(F32) for c in range(lines)], axis=1)[:, :JPAD])
    dqz = jnp.concatenate(dqz, axis=0)
    embed = embed_ref[...]
    embed_mine = product(embed, one).astype(BF16)
    val_mine = contract(one, val_ref[...], ((0,), (0,))).astype(BF16)
    keymap_mine = exact(keymap_ref[...], one.astype(F32), ((1,), (0,)))
    dembed = exact(keymap_mine, dqz, ((0,), (0,)))
    for g in range(n):
        dpv = sums[g][:JPAD]
        valuing_ref[:, g * width : (g + 1) * width] = contract(embed_mine, dpv, ((0,), (0,)))
        dembed = dembed + contract(val_mine[:, g * width : (g + 1) * width], dpv, ((1,), (1,)))
    patching_ref[...] = exact(dembed, places(4 * NVAR, JPAD, 0, 4, 2).astype(F32), ((1,), (1,)))
    tagging_ref[...] = dembed[:, 4 * VPAD : 4 * VPAD + NVAR]
    dkeymap = product(dqz.astype(BF16), embed)
    keying_ref[...] = exact(exact(dkeymap, one.astype(F32), ((1,), (0,))), by_head(beacon_ref[...].reshape(1, -1).astype(F32)), ((0,), (0,)))
    down = folded(product(pieces(dkeymap, 2), key_ref[...]), 2)
    beacon = jnp.sum(jnp.where(by_head(jnp.ones((1, D), F32)) > 0.5, down, 0.0), axis=0, keepdims=True)
    beacon_out[...] = exact(jnp.broadcast_to(beacon, (8, D)), one.astype(F32), ((1,), (0,)))[:1].reshape(rd)


def finish(summed, wcol, pcol, nar, squares, mer, pos, pred, grad, embed, read, valuing, keying, keymap, beacon, n, count, heads):
    rd, hid = D // (n * count), FF // (n * count)
    shape = lambda *s: jax.ShapeDtypeStruct(s, F32)
    vec = shape(rd)
    lat = 2 * LATP
    items, wide = pred.shape[0], pred.shape[2] // lat
    return pl.pallas_call(
        functools.partial(finish_kernel, n, count, heads),
        out_shape=(
            jax.ShapeDtypeStruct((items, NOUT, wide, lat), BF16), shape(items, NVAR, wide, lat),
            shape(*pos.shape), shape(rd, 4 * NVAR), shape(rd, NVAR), vec, shape(rd, D), shape(rd, D), vec, shape(rd, D), vec, vec, vec,
            shape(rd, 3 * D), shape(2 * rd), shape(rd, D), vec, vec, vec, shape(rd, FF), shape(4 * rd), shape(hid, D), vec,
            shape(rd, 4 * NOUT), shape(4 * NOUT),
        ),
        compiler_params=pltpu.CompilerParams(vmem_limit_bytes=60 * MIB),
        name="finish",
    )(summed, wcol, pcol, nar, squares, mer, pos, pred, grad, embed, read, valuing, keying, keymap, beacon)


def per_device(
    fields, variable_ids, variable_mask, position, patching, tagging, beacon, keying, valuing, lifting,
    merging, offset, scaling, centre, projecting, biasing, mixing, nudging, rescaling, recentre,
    widening, uplift, narrowing, settle, reading, baseline, cotangent,
):
    count, lon = lax.axis_size("batch"), lax.axis_size("lon")
    zi, li = lax.axis_index("batch"), lax.axis_index("lon")
    items, cols_dev, lat = fields.shape[0], fields.shape[2], fields.shape[3]
    upatch = cols_dev // 2
    here = upatch * LATP
    heads = HEADS // lon
    width = heads * HDIM
    rows_dev = D // (count * lon)
    hid = FF // (count * lon)
    f = lambda a: a.astype(F32)

    columns = lambda a, start, size: lax.dynamic_slice_in_dim(a, start, size, 1)
    direct_heads, direct_hidden = width % 128 == 0, hid % 128 == 0
    proj_own = projecting if direct_heads else jnp.concatenate([columns(projecting, p * D + li * width, width) for p in range(3)], axis=1)
    wide_own = widening if direct_hidden else jnp.concatenate([columns(widening, (c * lon + li) * hid, hid) for c in range(count)], axis=1)
    (
        attended, normed_all, joint, lse, dpred_all, embedded, pooled, patches, pool_w, qrow, pv, dpred, base, reading_p, keymap, embed,
    ) = front(
        fields, cotangent, variable_ids, variable_mask, patching.T, tagging.T, reading.T, beacon, lifting, offset, scaling, centre, biasing,
        position.reshape(here, D), keying, valuing, merging, proj_own, direct_heads, lon, items, here, heads,
    )
    outputs, squares, dmiddle, do, vec_grads, uplift_grads, second_all = middle_part(
        attended, embedded, mixing, nudging, rescaling, recentre, settle, uplift, baseline, widening, narrowing, reading_p, dpred,
        lon, items, here, heads,
    )
    nar, squares, pos, mer, prediction, fields_gradient, summed, wide_cols, joint_cols = rear_part(
        do, squares.reshape(count, lon, rows_dev, -1), second_all, dpred_all, wide_own, narrowing, f(uplift).reshape(count * lon, 1, hid), reading_p,
        joint, lse, normed_all, projecting, merging, embedded, dmiddle, pooled, scaling, patches, pool_w, qrow, pv, vec_grads, uplift_grads, base,
        variable_ids, outputs, direct_hidden, lon, count, items, here, heads,
    )
    outs = list(finish(
        summed, wide_cols, joint_cols, nar, squares, mer, pos, prediction, fields_gradient, embed, reading_p, valuing, keying, keymap, beacon,
        lon, count, heads,
    ))
    outs[2] = outs[2].reshape(upatch, LATP, D)
    return tuple(outs)


def solution(mesh):
    both = ("batch", "lon")
    image, matrix, vector = P("batch", None, "lon", None), P(both, None), P(both)
    return jax.shard_map(
        per_device,
        mesh=mesh,
        in_specs=(image, P("batch", None), P("batch", None), P("lon", None, None)) + (P(),) * 22 + (image,),
        out_specs=(
            image, image, P("lon", None, None), matrix, matrix, vector, matrix, matrix, vector, matrix, vector,
            vector, vector, matrix, vector, matrix, vector, vector, vector, matrix, vector, matrix, vector, matrix, P(),
        ),
        check_vma=False,
    )
```

```python
import functools

import jax
import jax.numpy as jnp
from jax import lax
from jax.experimental import pallas as pl
from jax.experimental.pallas import tpu as pltpu
from jax.sharding import PartitionSpec as P

D = 1024
HEADS = 16
HDIM = 64
FF = 4096
NVAR = 48
NOUT = 48
LATP = 32
VPAD = 64
JPAD = 5 * VPAD

HIGH = lax.Precision.HIGHEST
EPSILON = 1e-06
F32 = jnp.float32
BF16 = jnp.bfloat16
FACTOR = HDIM ** (-0.5)
MIB = 2**20
MESH = pl.DeviceIdType.MESH


def product(left, right):
    return jnp.dot(left, right, preferred_element_type=F32)


def contract(left, right, dims):
    return lax.dot_general(left, right, (dims, ((), ())), preferred_element_type=F32)


def normalize(values):
    centred = values - jnp.mean(values, axis=-1, keepdims=True)
    inverse = lax.rsqrt(jnp.mean(centred * centred, axis=-1, keepdims=True) + EPSILON)
    return centred * inverse, inverse


def norm_back(upstream, normal, inverse, scaler):
    weighted = upstream * scaler
    return inverse * (
        weighted
        - jnp.mean(weighted, axis=-1, keepdims=True)
        - normal * jnp.mean(weighted * normal, axis=-1, keepdims=True)
    )


def gelu_parts(x):
    c = 0.7978845608028654
    t = jnp.tanh(c * (x + 0.044715 * (x * x * x)))
    value = 0.5 * x * (1.0 + t)
    slope = 0.5 * (1.0 + t) + 0.5 * x * (1.0 - t * t) * (c * (1.0 + 3 * 0.044715 * x * x))
    return value, slope


def places(rows, cols, start, step, shift):
    row = lax.broadcasted_iota(jnp.int32, (rows, cols), 0)
    col = lax.broadcasted_iota(jnp.int32, (rows, cols), 1)
    return (start + (row & (step - 1)) * VPAD + (row >> shift) == col).astype(BF16)


def latitudes(lat):
    row = lax.broadcasted_iota(jnp.int32, (lat, lat), 0)
    col = lax.broadcasted_iota(jnp.int32, (lat, lat), 1)
    half = lat // 2
    return (2 * (row & (half - 1)) + (row >> (half.bit_length() - 1)) == col).astype(BF16)


def by_head(row):
    head = lax.broadcasted_iota(jnp.int32, (HEADS, D), 0)
    col = lax.broadcasted_iota(jnp.int32, (HEADS, D), 1)
    return jnp.where(col >> 6 == head, jnp.broadcast_to(row, (HEADS, D)), jnp.zeros((), row.dtype))


def pieces(a, count):
    parts = []
    for _ in range(count):
        parts.append(a.astype(BF16))
        a = a - parts[-1].astype(F32)
    return jnp.concatenate(parts, axis=0)


class Moves:
    def __init__(self, sem):
        self.sem, self.started = sem, []

    def go(self, src, dst):
        copy = pltpu.make_async_copy(src, dst, self.sem.at[len(self.started)])
        self.started.append(copy)
        copy.start()
        return copy


def folded(a, count):
    rows = a.shape[0] // count
    total = a[:rows]
    for i in range(1, count):
        total = total + a[i * rows : (i + 1) * rows]
    return total


def barrier_all(n, li):
    sem = pltpu.get_barrier_semaphore()
    for mask in range(1, n):
        pl.semaphore_signal(sem, inc=1, device_id={"lon": li ^ mask}, device_id_type=MESH)
    pl.semaphore_wait(sem, n - 1)


class Gather:
    def __init__(self, n, li, at, send, recv):
        self.n, self.li, self.at, self.send, self.recv = n, li, at, send, recv
        self.bits = [1 << i for i in range(1, n.bit_length() - 1)]

    def order(self, piece):
        return self.bits if piece % 2 == 0 else self.bits[::-1]

    def copy(self, mask, piece):
        bit = 1 if mask & 1 else [b for b in self.order(piece) if b & mask][-1]
        return pltpu.make_async_remote_copy(
            src_ref=self.at(mask ^ bit, piece),
            dst_ref=self.at(mask, piece),
            send_sem=self.send.at[mask, piece],
            recv_sem=self.recv.at[mask, piece],
            device_id={"lon": self.li ^ bit},
            device_id_type=MESH,
        )

    def forward(self, mask, piece):
        order = self.order(piece)
        used = [i for i, b in enumerate(order) if b & mask]
        for b in order[(used[-1] + 1 if used else 0):]:
            self.copy(mask | b, piece).start()
        self.copy(mask | 1, piece).start()

    def start(self, pieces):
        for piece in pieces:
            self.forward(0, piece)

    def evens(self):
        return sorted(range(2, self.n, 2), key=lambda m: bin(m).count("1"))

    def relay(self, pieces, first=True, rest=True):
        for depth in range(1, len(self.bits) + 1):
            if (first if depth == 1 else rest):
                for piece in pieces:
                    for mask in self.evens():
                        if bin(mask).count("1") == depth:
                            self.copy(mask, piece).wait_recv()
                            self.forward(mask, piece)

    def finish(self, pieces):
        for mask in range(1, self.n, 2):
            for piece in pieces:
                self.copy(mask, piece).wait_recv()

    def drain(self, pieces):
        for mask in range(1, self.n):
            for piece in pieces:
                self.copy(mask, piece).wait_send()


def front_kernel(
    n, items, here, heads, direct, fields_ref, cot_ref, ids_ref, mask_ref, patching_ref, tagging_ref, read_ref, beacon_ref, lifting_ref,
    offset_ref, scaling_ref, centre_ref, biasing_ref, place_ref, key_hbm, val_hbm, mer_hbm, proj_hbm,
    att_ref, all_out, qkv_out, lse_ref, up_out, emb_out, pooled_out, patches_out, pw_out, qrow_ref, pv_out, dpred_ref, base_ref, readp_out,
    keymap_mine, embed_mine, val_mine, kk_mine,
    keying, valuing, merging, own_w, load, seam, seam_land, seam_send, seam_recv, up_ref, usend, urecv,
    rows_ref, obuf, land, gsend, grecv, osend, orecv, keep, qkv_ref, emb_ref, pooled_ref, patches_ref, pw_ref, pv_ref, readp_ref,
):
    li = lax.axis_index("lon")
    block = lax.axis_index("batch") * n + li
    rd = val_mine.shape[0]
    width = heads * HDIM
    seq = n * here
    tile = min(seq, 512)
    rows = items * here
    lat = 2 * LATP
    wide = fields_ref.shape[2]
    loads, keeps = Moves(load), Moves(keep)
    fetch_key, fetch_val, fetch_mer = (loads.go(h, v) for h, v in ((key_hbm, keying), (val_hbm, valuing), (mer_hbm, merging)))
    if direct:
        fetch_own = [loads.go(proj_hbm.at[:, pl.ds(pl.multiple_of(p * D + li * width, width), width)], own_w.at[:, p * width : (p + 1) * width]) for p in range(3)]
    else:
        fetch_own = [loads.go(proj_hbm, own_w)]
    for i in range(items):
        seam[0, i] = fields_ref[i, :, wide - 1, :]
        seam[1, i] = cot_ref[i, :, wide - 1, :]
    barrier_all(n, li)
    east = pltpu.make_async_remote_copy(
        src_ref=seam, dst_ref=seam_land, send_sem=seam_send, recv_sem=seam_recv,
        device_id={"lon": lax.rem(li + 1, n)}, device_id_type=MESH,
    )
    east.start()

    row = lambda ref: ref[...].reshape(1, -1)
    embed = contract(places(4 * NVAR, JPAD, 0, 4, 2), patching_ref[...], ((0,), (0,)))
    embed = (embed + contract(places(NVAR, JPAD, 4 * VPAD, 1, 0), tagging_ref[...], ((0,), (0,)))).astype(BF16)
    readp_ref[...] = contract(places(4 * NOUT, 4 * VPAD, 0, 4, 2), read_ref[...], ((0,), (0,))).astype(BF16)
    keeps.go(readp_ref, readp_out)

    fetch_key.wait()
    keymap = contract(by_head(row(beacon_ref)), keying[...], ((1,), (1,)))
    qrow = folded(contract(pieces(keymap, 3), embed, ((1,), (1,))), 3)
    for h in range(HEADS):
        qrow_ref[h] = qrow[h : h + 1, :]
    fetch_val.wait()
    pv = product(embed, valuing[...]).astype(BF16)
    for g in range(n):
        pv_ref[g] = pv[:, g * width : (g + 1) * width]
    keeps.go(pv_ref, pv_out)

    spread = latitudes(lat)
    var = lax.broadcasted_iota(jnp.int32, (VPAD, NVAR), 0)
    same = (var == lax.broadcasted_iota(jnp.int32, (VPAD, NVAR), 1)).astype(BF16)
    lane = lax.broadcasted_iota(jnp.int32, (8, VPAD), 1)
    patches_ref[:, 4 * VPAD :] = jnp.ones((rows, VPAD), BF16)
    east.wait()

    def tokens(ref, which, i, choose, out):
        pixels = [seam_land[which, i]] + [ref[i, :, w, :] for w in range(wide - 1)]
        stack = jnp.concatenate([product(choose, p).astype(BF16) for p in pixels], axis=0)
        turned = contract(spread, stack, ((1,), (1,))).astype(BF16)
        for w in range(wide):
            token = turned[:, w * VPAD : (w + 1) * VPAD]
            for e in range(2):
                corner = (w % 2) * 2 + e
                at = i * here + (w // 2) * LATP
                out[at : at + LATP, corner * VPAD : (corner + 1) * VPAD] = token[e * LATP : (e + 1) * LATP]

    for i in range(items):
        tokens(cot_ref, 1, i, same, dpred_ref)
    half_rows = rows // 2
    ups = Gather(n, li, lambda slot, piece: up_ref.at[slot, pl.ds(piece * half_rows, half_rows)], usend, urecv)
    up_ref[0] = dpred_ref[...]
    ups.start([0, 1])
    base_ref[...] = jnp.sum(dpred_ref[...].astype(F32), axis=0, keepdims=True)
    cuts = 4
    share = here // cuts
    pieces_of = lambda i: list(range(cuts * i, cuts * (i + 1)))

    def at(slot, piece):
        return rows_ref.at[piece // cuts, slot, pl.ds((piece % cuts) * share, share)]

    gather = Gather(n, li, at, gsend, grecv)
    lifting = row(lifting_ref).astype(F32)
    offset, scaling, centre = (row(a).astype(F32) for a in (offset_ref, scaling_ref, centre_ref))

    for i in range(items):
        part = slice(i * here, (i + 1) * here)
        choose = (var == ids_ref[i : i + 1, :]).astype(BF16)
        tokens(fields_ref, 0, i, choose, patches_ref)
        kept = jnp.broadcast_to(mask_ref[i : i + 1, :], (8, NVAR)).astype(F32).astype(BF16)
        live = contract(kept, choose, ((1,), (1,)))
        mask = jnp.broadcast_to(jnp.where(lane < NVAR, jnp.where(live > 0.5, 0.0, -1e30), -2e30)[:1], (here, VPAD))
        patches = patches_ref[part, :].astype(F32)
        for pair in range(HEADS // 2):
            halves = []
            for h in (2 * pair, 2 * pair + 1):
                x = patches[:, : 4 * VPAD] * qrow[h : h + 1, : 4 * VPAD]
                x = x[:, : 2 * VPAD] + x[:, 2 * VPAD :]
                logits = (x[:, :VPAD] + x[:, VPAD:] + qrow[h : h + 1, 4 * VPAD :]) * FACTOR
                logits = jnp.where(mask == 0.0, logits, mask)
                grown = jnp.exp(logits - jnp.max(logits, axis=-1, keepdims=True))
                w = grown / jnp.sum(grown, axis=-1, keepdims=True)
                pw_ref[h, part, :] = w.astype(BF16)
                blended = (jnp.concatenate([w] * 5, axis=1) * patches).astype(BF16)
                halves.append(product(blended, pv[:, h * HDIM : (h + 1) * HDIM]))
            cols = slice(pair * 128, pair * 128 + 128)
            pooled_ref[part, cols] = (jnp.concatenate(halves, axis=1) + lifting[:, cols]).astype(BF16)
        if i == 0:
            fetch_mer.wait()
        emb = product(pooled_ref[part, :], merging[...]) + offset + place_ref[...].astype(F32)
        emb_ref[part, :] = emb
        normal, _ = normalize(emb)
        rows_ref[i, 0] = (normal * scaling + centre).astype(BF16)
        gather.start(pieces_of(i))
    ups.relay([0, 1])
    gather.relay(pieces_of(0))
    for src, dst in ((patches_ref, patches_out), (pw_ref, pw_out), (pooled_ref, pooled_out), (emb_ref, emb_out)):
        keeps.go(src, dst)

    one = (lax.broadcasted_iota(jnp.int32, (D, rd), 0) == block * rd + lax.broadcasted_iota(jnp.int32, (D, rd), 1)).astype(BF16)
    embed_mine[...] = product(embed, one).astype(BF16)
    val_mine[...] = contract(one, valuing[...], ((0,), (0,))).astype(BF16)
    keymap_mine[...] = jnp.dot(keymap, one.astype(F32), precision=HIGH, preferred_element_type=F32)
    kk_mine[...] = product(embed, product(keying[...], one).astype(BF16))

    def give(i, mask):
        return pltpu.make_async_remote_copy(
            src_ref=obuf.at[i, mask],
            dst_ref=land.at[li, i],
            send_sem=osend.at[i, mask],
            recv_sem=orecv.at[i, mask],
            device_id={"lon": li ^ mask},
            device_id_type=MESH,
        )

    column = lax.broadcasted_iota(jnp.int32, (D, width), 1)
    mine = (lax.broadcasted_iota(jnp.int32, (D, width), 0) == li * width + column).astype(BF16)
    biases = jnp.broadcast_to(row(biasing_ref), (8, 2 * D))
    own_bias = jnp.concatenate(
        [product(biases[:, :D], mine)[:1], jnp.zeros((1, width), F32), product(biases[:, D:], mine)[:1]], axis=1
    )
    for c in fetch_own:
        c.wait()
    for i in range(items):
        later = pieces_of(i + 1) if i + 1 < items else []
        gather.finish(pieces_of(i))
        keeps.go(rows_ref.at[i], all_out.at[i])
        joint = product(rows_ref[i].reshape(seq, D), own_w[...]) + own_bias
        qkv_ref[i] = joint.astype(BF16)
        keeps.go(qkv_ref.at[i], qkv_out.at[i])
        for t in range(seq // tile):
            outs = []
            for h in range(heads):
                q = qkv_ref[i, t * tile : (t + 1) * tile, h * HDIM : (h + 1) * HDIM] * FACTOR
                k = qkv_ref[i, :, width + h * HDIM : width + (h + 1) * HDIM]
                v = qkv_ref[i, :, 2 * width + h * HDIM : 2 * width + (h + 1) * HDIM]
                scores = contract(q, k, ((1,), (1,)))
                top = jnp.max(scores, axis=1, keepdims=True)
                grown = jnp.exp(scores - top)
                total = jnp.sum(grown, axis=1, keepdims=True)
                outs.append(product(grown.astype(BF16), v) / total)
                lse = top + jnp.log(total)
                lse_ref[i, h : h + 1, t * tile : (t + 1) * tile] = jnp.transpose(lse)
                if t == 0 and h == 0:
                    gather.relay(later)
            out = jnp.concatenate(outs, axis=1) if heads > 1 else outs[0]
            slots = range(t * (tile // here), (t + 1) * (tile // here))
            obuf[i, t * (tile // here) : (t + 1) * (tile // here)] = out.astype(BF16).reshape(tile // here, here, width)
            for mask in slots:
                if mask:
                    give(i, mask).start()
        land[li, i] = obuf[i, 0]
    ups.finish([0, 1])
    keeps.go(up_ref, up_out)
    for i in range(items):
        for mask in range(1, n):
            give(i, mask).wait_recv()
        att_ref[i * here : (i + 1) * here, :] = jnp.concatenate([land[g, i] for g in range(n)], axis=1)
    ups.drain([0, 1])
    for i in range(items):
        gather.drain(pieces_of(i))
        for mask in range(1, n):
            give(i, mask).wait_send()
    for c in keeps.started:
        c.wait()


def front(fields, cot, ids, mask, patching, tagging, reading, beacon, lifting, offset, scaling, centre, biasing, place, keying, valuing, merging, proj, rd, direct, n, items, here, heads):
    width = heads * HDIM
    seq = n * here
    rows = items * here
    vm, hbm = pl.BlockSpec(memory_space=pltpu.VMEM), pl.BlockSpec(memory_space=pl.ANY)
    shape = jax.ShapeDtypeStruct
    dma = pltpu.SemaphoreType.DMA
    low = lambda *a: pltpu.VMEM(a, BF16)
    edge = low(2, items, NVAR, 2 * LATP)
    return pl.pallas_call(
        functools.partial(front_kernel, n, items, here, heads, direct),
        in_specs=[vm] * 14 + [hbm] * 4,
        out_specs=(vm, hbm, hbm, vm, hbm, hbm, hbm, hbm, hbm, vm, hbm, vm, vm, hbm, vm, vm, vm, vm),
        out_shape=(
            shape((rows, D), BF16), shape((items, n, here, D), BF16), shape((items, seq, 3 * width), BF16), shape((items, heads, seq), F32),
            shape((n, rows, 4 * VPAD), BF16), shape((rows, D), F32), shape((rows, D), BF16), shape((rows, JPAD), BF16),
            shape((HEADS, rows, VPAD), BF16), shape((HEADS, 1, JPAD), F32), shape((n, JPAD, width), BF16), shape((rows, 4 * VPAD), BF16),
            shape((1, 4 * VPAD), F32), shape((4 * VPAD, D), BF16), shape((HEADS, rd), F32), shape((JPAD, rd), BF16), shape((rd, D), BF16), shape((JPAD, rd), F32),
        ),
        scratch_shapes=[
            low(D, D), low(D, D), low(D, D), low(D, 3 * width), dma((8,)), edge, edge, dma, dma,
            low(n, rows, 4 * VPAD), dma((n, 2)), dma((n, 2)),
            low(items, n, here, D), low(items, n, here, width), low(n, items, here, width),
            dma((n, 4 * items)), dma((n, 4 * items)), dma((items, n)), dma((items, n)), dma((2 * items + 9,)),
            low(items, seq, 3 * width), pltpu.VMEM((rows, D), F32), low(rows, D), low(rows, JPAD), low(HEADS, rows, VPAD),
            low(n, JPAD, width), low(4 * VPAD, D),
        ],
        compiler_params=pltpu.CompilerParams(collective_id=1, has_side_effects=True, vmem_limit_bytes=60 * MIB),
        name="front",
    )(fields, cot, ids, mask, patching, tagging, reading, beacon, lifting, offset, scaling, centre, biasing, place, keying, valuing, merging, proj)


def middle_kernel(
    n, items, here, heads, block,
    att_ref, emb_ref, mix_hbm, nudging_ref, rescaling_ref, recentre_ref, settle_ref, uplift_ref, baseline_ref, w1_hbm, w2_hbm, read_ref, dpred_ref,
    z_ref, sq_out, dmid_ref, do_ref, vecg_ref, uplg_ref, rows_out,
    w1, w2, mix, rows_ref, normal_ref, acc, slope_ref, upl_ref, sq_ref, gsend, grecv, load, keep,
):
    li = lax.axis_index("lon")
    rows = items * here
    width = heads * HDIM
    blocks = FF // block

    def fetch1(b):
        return pltpu.make_async_copy(w1_hbm.at[:, pl.ds(pl.multiple_of(b * block, block), block)], w1.at[b], load.at[b])

    def fetch2(b):
        return pltpu.make_async_copy(w2_hbm.at[pl.ds(pl.multiple_of(b * block, block), block)], w2.at[b], load.at[blocks + b])

    fetch_mix = pltpu.make_async_copy(mix_hbm, mix, load.at[2 * blocks])
    fetch_mix.start()
    for b in range(blocks):
        fetch1(b).start()
        fetch2(b).start()
    barrier_all(n, li)

    row = lambda ref: ref[...].reshape(1, -1).astype(F32)
    nudging, rescaling, recentre, settle = (row(a) for a in (nudging_ref, rescaling_ref, recentre_ref, settle_ref))
    uplift = row(uplift_ref)
    for b in range(blocks):
        upl_ref[b] = uplift[:, b * block : (b + 1) * block]
    quarter = rows // 4
    keeps = Moves(keep)
    every = list(range(4))
    gather = Gather(n, li, lambda slot, piece: rows_ref.at[slot, pl.ds(piece * quarter, quarter)], gsend, grecv)
    fetch_mix.wait()
    mid = emb_ref[...] + (product(att_ref[...], mix[...]) + nudging)
    dmid_ref[...] = mid
    normal, inverse = normalize(mid)
    normal_ref[...] = normal
    rows_ref[0] = (normal * rescaling + recentre).astype(BF16)
    gather.start(every)
    acc[...] = jnp.zeros_like(acc)

    def ahead(b, _):
        fetch1(b).wait()
        hidden = product(rows_ref[0], w1[b]) + upl_ref[b]
        value, slope = gelu_parts(hidden)
        slope_ref[b] = slope
        fetch2(b).wait()
        acc[...] += product(value.astype(BF16), w2[b])
        return 0

    lax.fori_loop(0, blocks, ahead, 0)
    final = (dmid_ref[...] + (acc[...] + settle)).astype(BF16)
    baseline = jnp.broadcast_to(baseline_ref[...].reshape(1, -1), (8, 4 * NOUT))
    baseline = product(baseline, places(4 * NOUT, 4 * VPAD, 0, 4, 2))[:1]
    z_ref[...] = (contract(final, read_ref[...], ((1,), (1,))) + baseline).astype(BF16)
    dpred = dpred_ref[...]
    sq_ref[:, D:] = contract(final, dpred, ((0,), (0,))).astype(BF16)
    keeps.go(sq_ref.at[:, pl.ds(D, 4 * VPAD)], sq_out.at[:, pl.ds(D, 4 * VPAD)])
    dfinal = product(dpred, read_ref[...])
    dfinal_low = dfinal.astype(BF16)
    acc[...] = jnp.zeros_like(acc)

    def back(b, _):
        dhidden = (contract(dfinal_low, w2[b], ((1,), (1,))) * slope_ref[b]).astype(BF16)
        uplg_ref[b] = jnp.sum(dhidden.astype(F32), axis=0, keepdims=True)
        acc[...] += contract(dhidden, w1[b], ((1,), (1,)))
        return 0

    gather.relay(every[:2], rest=False)
    lax.fori_loop(0, blocks // 2, back, 0)
    gather.relay(every[2:], rest=False)
    lax.fori_loop(blocks // 2, blocks, back, 0)
    gather.relay(every, first=False)
    for mask in range(0, n, 2):
        keeps.go(rows_ref.at[mask], rows_out.at[mask])
    dsecond = acc[...]
    normal = normal_ref[...]
    dmid = dfinal + norm_back(dsecond, normal, inverse, rescaling)
    dmid_ref[...] = dmid
    dmid_low = dmid.astype(BF16)
    vecg_ref[...] = jnp.concatenate([
        jnp.sum(dmid_low.astype(F32), axis=0, keepdims=True),
        jnp.sum(dsecond * normal, axis=0, keepdims=True),
        jnp.sum(dsecond, axis=0, keepdims=True),
        jnp.sum(dfinal_low.astype(F32), axis=0, keepdims=True),
    ], axis=0)
    dout = contract(dmid_low, mix[...], ((1,), (1,))).astype(BF16)
    for g in range(n):
        do_ref[g] = dout[:, g * width : (g + 1) * width].reshape(items, here, width)
    sq_ref[:, :D] = contract(att_ref[...], dmid_low, ((0,), (0,))).astype(BF16)
    keeps.go(sq_ref.at[:, pl.ds(0, D)], sq_out.at[:, pl.ds(0, D)])
    for mask in range(1, n, 2):
        for piece in every:
            gather.copy(mask, piece).wait_recv()
        keeps.go(rows_ref.at[mask], rows_out.at[mask])
    gather.drain(every)
    for c in keeps.started:
        c.wait()


def middle_part(att, emb, mixing, nudging, rescaling, recentre, settle, uplift, baseline, widening, narrowing, read, dpred, n, items, here, heads):
    rows = items * here
    width = heads * HDIM
    block = 512
    blocks = FF // block
    vm = pl.BlockSpec(memory_space=pltpu.VMEM)
    hbm = pl.BlockSpec(memory_space=pl.ANY)
    shape = jax.ShapeDtypeStruct
    return pl.pallas_call(
        functools.partial(middle_kernel, n, items, here, heads, block),
        in_specs=[vm, vm, hbm, vm, vm, vm, vm, vm, vm, hbm, hbm, vm, vm],
        out_specs=(vm, hbm, vm, vm, vm, vm, hbm),
        out_shape=(
            shape((rows, 4 * VPAD), BF16), shape((D, D + 4 * VPAD), BF16), shape((rows, D), F32),
            shape((n, items, here, width), BF16), shape((4, D), F32), shape((blocks, 1, block), F32), shape((n, rows, D), BF16),
        ),
        scratch_shapes=[
            pltpu.VMEM((blocks, D, block), BF16), pltpu.VMEM((blocks, block, D), BF16), pltpu.VMEM((D, D), BF16),
            pltpu.VMEM((n, rows, D), BF16), pltpu.VMEM((rows, D), F32), pltpu.VMEM((rows, D), F32),
            pltpu.VMEM((blocks, rows, block), F32), pltpu.VMEM((blocks, 1, block), F32), pltpu.VMEM((D, D + 4 * VPAD), BF16),
            pltpu.SemaphoreType.DMA((n, 4)), pltpu.SemaphoreType.DMA((n, 4)),
            pltpu.SemaphoreType.DMA((2 * blocks + 1,)), pltpu.SemaphoreType.DMA((n + 2,)),
        ],
        compiler_params=pltpu.CompilerParams(collective_id=2, has_side_effects=True, vmem_limit_bytes=60 * MIB),
        name="middle",
    )(att, emb, mixing, nudging, rescaling, recentre, settle, uplift, baseline, widening, narrowing, read, dpred)


def greet(n, li, count, zi):
    sem = pltpu.get_barrier_semaphore()
    for mask in range(1, n):
        pl.semaphore_signal(sem, inc=1, device_id={"lon": li ^ mask}, device_id_type=MESH)
    for mask in range(1, count):
        pl.semaphore_signal(sem, inc=1, device_id={"batch": zi ^ mask}, device_id_type=MESH)
    pl.semaphore_wait(sem, n + count - 2)


class Halving:
    def __init__(self, count, zi, flip, own, stage, land, send, recv):
        self.count, self.zi, self.own, self.stage, self.land = count, zi, own, stage, land
        self.send_sem, self.recv_sem = send, recv
        self.bits = [1 << i for i in range(count.bit_length() - 1)]
        if flip:
            self.bits = self.bits[::-1]

    def at_step(self, step):
        return [r for r in range(1, self.count) if min(i for i, b in enumerate(self.bits) if b & r) == step]

    def copy(self, r, step):
        return pltpu.make_async_remote_copy(
            src_ref=self.own(self.zi ^ r) if step == 0 else self.stage.at[r],
            dst_ref=self.land.at[r],
            send_sem=self.send_sem.at[r],
            recv_sem=self.recv_sem.at[r],
            device_id={"batch": self.zi ^ self.bits[step]},
            device_id_type=MESH,
        )

    def send(self, step):
        for r in self.at_step(step):
            self.copy(r, step).start()

    def absorb(self, step):
        for r in self.at_step(step):
            self.copy(r, step).wait_recv()
            to = r ^ self.bits[step]
            base = self.own(self.zi ^ to)[...] if step == 0 else self.stage[to]
            total = base.astype(F32) + self.land[r].astype(F32)
            if step == len(self.bits) - 1:
                return total
            self.stage[to] = total.astype(BF16)

    def drain(self):
        for step in range(len(self.bits)):
            for r in self.at_step(step):
                self.copy(r, step).wait_send()


class RowSum:
    def __init__(self, n, li, count, zi, own, land1, stage1, land2, stage2, land3, sems):
        self.n, self.li, self.count, self.zi, self.own = n, li, count, zi, own
        self.land1, self.stage1, self.land2, self.stage2, self.land3 = land1, stage1, land2, stage2, land3
        self.s1, self.r1, self.s2, self.r2, self.s3, self.r3 = sems
        self.half = n // 2

    @staticmethod
    def scratch(n, count, rows, cols):
        half = pltpu.VMEM((n // 2, count, rows, cols), BF16)
        one = pltpu.VMEM((count, rows, cols), BF16)
        lon_sem, z_sem = pltpu.SemaphoreType.DMA((n // 2,)), pltpu.SemaphoreType.DMA((count,))
        return [half, half, half, one, one, lon_sem, lon_sem, lon_sem, lon_sem, z_sem, z_sem]

    def copy1(self, j):
        return pltpu.make_async_remote_copy(
            src_ref=self.own(self.li ^ (2 * j + 1)), dst_ref=self.land1.at[j], send_sem=self.s1.at[j],
            recv_sem=self.r1.at[j], device_id={"lon": self.li ^ 1}, device_id_type=MESH,
        )

    def copy2(self, j):
        return pltpu.make_async_remote_copy(
            src_ref=self.stage1.at[j], dst_ref=self.land2.at[j], send_sem=self.s2.at[j],
            recv_sem=self.r2.at[j], device_id={"lon": self.li ^ (2 * j)}, device_id_type=MESH,
        )

    def copy3(self, r):
        return pltpu.make_async_remote_copy(
            src_ref=self.stage2.at[self.zi ^ r], dst_ref=self.land3.at[r], send_sem=self.s3.at[r],
            recv_sem=self.r3.at[r], device_id={"batch": self.zi ^ r}, device_id_type=MESH,
        )

    def core(self):
        for j in range(self.half):
            self.copy1(j).start()

    def plane(self):
        for j in list(range(1, self.half)) + [0]:
            self.copy1(j).wait_recv()
            self.stage1[j] = (self.own(self.li ^ (2 * j))[...].astype(F32) + self.land1[j].astype(F32)).astype(BF16)
            if j:
                self.copy2(j).start()

    def depth(self):
        total = self.stage1[0].astype(F32)
        for j in range(1, self.half):
            self.copy2(j).wait_recv()
            total = total + self.land2[j].astype(F32)
        self.stage2[...] = total.astype(BF16)
        for r in range(1, self.count):
            self.copy3(r).start()

    def total(self):
        total = self.stage2[self.zi].astype(F32)
        for r in range(1, self.count):
            self.copy3(r).wait_recv()
            total = total + self.land3[r].astype(F32)
        return total

    def drain(self):
        for j in range(self.half):
            self.copy1(j).wait_send()
            if j:
                self.copy2(j).wait_send()
        for r in range(1, self.count):
            self.copy3(r).wait_send()


ARROWS = 384


def rear_kernel(
    n, count, items, here, heads, direct,
    do_ref, sq_ref, second_hbm, up_hbm, wown_hbm, nown_hbm, uplift_ref, read_ref, qkv_hbm, lse_ref, rows_hbm,
    proj_hbm, merge_hbm, emb_hbm, dmid_hbm, pooled_hbm, scaling_ref, patches_hbm, w_hbm, qrow_ref, pv_hbm, vecg_ref, uplg_ref, base_ref,
    ids_ref, z_hbm,
    nar_ref, sqo_ref, pos_ref, mer_ref, pred_ref, grad_ref, ar_ref, wcol_ref, pcol_ref,
    dpatch_ref, zsend, gsend, zland, gland, seams, wown, nown, bufa, bufb, dz, accn, accw, narg, widg, do_land, ebuf, eland, dk_acc, dv_acc, projg,
    mbuf, du3, arbuf, arland, arz, archunk, posbuf, posland, posall, wcolbuf, pcolbuf, upl, upall,
    qkv_ref, emb_ref, dmid_ref, pooled_ref, patches_ref, w_ref, pv_ref, z_ref,
    load, osend, orecv, esend, erecv, nstage, nland, nsend, nrecv, wstage, wland, wsend, wrecv, xstage, xland, xsend, xrecv,
    pstage, pland, psend, precv, qstage, qland, qsend, qrecv,
    asend, arecv, azs, azr, ags, agr, bgs, bgr, pss, psr, pgs, pgr, ws, wr, cs, cr, *sums,
):
    li, zi = lax.axis_index("lon"), lax.axis_index("batch")
    rows = items * here
    width = heads * HDIM
    seq = n * here
    rd = D // (n * count)
    hid = FF // (n * count)
    tile = 512 if seq <= 1024 else 256
    total = lambda a: jnp.sum(a, axis=0, keepdims=True)

    loads = Moves(load)
    starts = [pl.multiple_of((c * n + li) * hid, hid) for c in range(count)]
    fetch_own = [loads.go(nown_hbm.at[pl.ds(at, hid)], nown.at[pl.ds(c * hid, hid)]) for c, at in enumerate(starts)]
    if direct:
        fetch_own += [loads.go(wown_hbm.at[:, pl.ds(at, hid)], wown.at[:, c * hid : (c + 1) * hid]) for c, at in enumerate(starts)]
    else:
        fetch_own.append(loads.go(wown_hbm, wown))
    fetch_own.append(loads.go(up_hbm, dz))
    fetch_rows = [loads.go(second_hbm.at[m], bufa.at[m]) for m in range(n)]
    fetch_z = loads.go(z_hbm, z_ref)
    fetch_qkv = loads.go(qkv_hbm, qkv_ref)
    per = D // rows
    roomy = n <= 2 * per
    buf_rows, buf_proj = (bufb, bufa) if roomy else (bufa, bufb)

    def fetch_normed():
        return [loads.go(rows_hbm.at[i], buf_rows.at[pl.ds(0, n), pl.ds(i * here, here)]) for i in range(items)]

    def fetch_square(hbm, first, buf, at):
        return [loads.go(hbm.at[pl.ds(j * rows, rows), first : first + D], buf.at[at + j]) for j in range(per)]

    def fetch_joint():
        return fetch_square(proj_hbm, 0, buf_proj, 0) + fetch_square(proj_hbm, D, buf_proj, per)

    fetch_early = fetch_normed() if roomy else fetch_joint()
    fetch_late = [
        loads.go(h, v)
        for h, v in ((emb_hbm, emb_ref), (dmid_hbm, dmid_ref), (pooled_hbm, pooled_ref), (patches_hbm, patches_ref), (w_hbm, w_ref), (pv_hbm, pv_ref))
    ]
    greet(n, li, count, zi)
    nar = Halving(count, zi, False, lambda b: narg.at[b], nstage, nland, nsend, nrecv)
    cut = count // 2
    wide_a = Halving(count, zi, False, lambda b: widg.at[b, pl.ds(0, cut)], wstage, wland, wsend, wrecv)
    wide_b = Halving(count, zi, True, lambda b: widg.at[b, pl.ds(cut, cut)], xstage, xland, xsend, xrecv)
    squares = RowSum(n, li, count, zi, lambda l: sq_ref.at[:, l], *sums[:5], sums[10:16])
    merging = RowSum(n, li, count, zi, lambda l: mbuf.at[:, l], *sums[5:10], sums[16:22])
    hz = D // count // 2
    first = Halving(count, zi, False, lambda b: projg.at[pl.ds(b * 2 * hz, hz)], pstage, pland, psend, precv)
    second = Halving(count, zi, True, lambda b: projg.at[pl.ds(b * 2 * hz + hz, hz)], qstage, qland, qsend, qrecv)
    steps = len(nar.bits)

    def onward(*sums):
        for step in range(steps - 1):
            for one in sums:
                one.absorb(step)
                one.send(step + 1)

    def give_do(mask):
        return pltpu.make_async_remote_copy(
            src_ref=do_ref.at[li ^ mask], dst_ref=do_land.at[mask], send_sem=osend.at[mask], recv_sem=orecv.at[mask],
            device_id={"lon": li ^ mask}, device_id_type=MESH,
        )

    for mask in range(1, n):
        give_do(mask).start()
    do_land[0] = do_ref[li]
    squares.core()

    for c in fetch_own:
        c.wait()
    slopes = contract(nown[...], read_ref[...], ((1,), (1,))).astype(BF16)
    uplift = uplift_ref[...].reshape(1, FF).astype(F32)
    for j in range(n * count):
        upall[j] = uplift[:, j * hid : (j + 1) * hid]
    upl[...] = jnp.concatenate([upall[c * n + li] for c in range(count)], axis=1)
    for c in fetch_rows:
        c.wait()
    group_of = D // rows
    half = count * hid // 2

    def own_units(part):
        cols = slice(part * half, (part + 1) * half)
        accn[...] = jnp.zeros_like(accn)
        accw[...] = jnp.zeros_like(accw)

        def own(m, _):
            take = pl.ds(m * group_of, group_of)
            normed, upstream = bufa[take].reshape(D, D), dz[take].reshape(D, 4 * VPAD)
            value, slope = gelu_parts(product(normed, wown[:, cols]) + upl[:, cols])
            dhidden = (contract(upstream, slopes[cols], ((1,), (1,))) * slope).astype(BF16)
            accn[...] += contract(value.astype(BF16), upstream, ((0,), (0,)))
            accw[...] += contract(dhidden, normed, ((0,), (0,)))
            return 0

        lax.fori_loop(0, n // group_of, own, 0)
        for j in range(cut):
            narg[part * cut + j] = accn[j * hid : (j + 1) * hid, :].astype(BF16)
            for b in range(count):
                widg[b, part * cut + j] = accw[j * hid : (j + 1) * hid, b * (D // count) : (b + 1) * (D // count)].astype(BF16)

    squares.plane()
    own_units(0)
    wide_a.send(0)

    def give(i, mask):
        return pltpu.make_async_remote_copy(
            src_ref=ebuf.at[i, mask], dst_ref=eland.at[li, i], send_sem=esend.at[i, mask], recv_sem=erecv.at[i, mask],
            device_id={"lon": li ^ mask}, device_id_type=MESH,
        )

    fetch_qkv.wait()
    for mask in range(1, n):
        give_do(mask).wait_recv()
    for i in range(items):
        dk_acc[...] = jnp.zeros_like(dk_acc)
        dv_acc[...] = jnp.zeros_like(dv_acc)
        for t in range(seq // tile):
            part = slice(t * tile, (t + 1) * tile)
            outs = []
            do_rows = do_land[t * (tile // here) : (t + 1) * (tile // here), i].reshape(tile, width)
            for h in range(heads):
                cols = slice(h * HDIM, (h + 1) * HDIM)
                q = qkv_ref[i, part, h * HDIM : (h + 1) * HDIM] * FACTOR
                k = qkv_ref[i, :, width + h * HDIM : width + (h + 1) * HDIM]
                v = qkv_ref[i, :, 2 * width + h * HDIM : 2 * width + (h + 1) * HDIM]
                do = do_rows[:, cols]
                probs = jnp.exp(contract(q, k, ((1,), (1,))) - jnp.transpose(lse_ref[i, h : h + 1, part]))
                dprobs = contract(do, v, ((1,), (1,)))
                delta = jnp.sum(probs * dprobs, axis=1, keepdims=True)
                dscores = (probs * (dprobs - delta)).astype(BF16)
                dv_acc[h] += contract(do, probs.astype(BF16), ((0,), (0,)))
                dk_acc[h] += contract(q, dscores, ((0,), (0,)))
                outs.append(product(dscores, k) * FACTOR)
            out = jnp.concatenate(outs, axis=1) if heads > 1 else outs[0]
            ebuf[i, t * (tile // here) : (t + 1) * (tile // here), :, :width] = out.astype(BF16).reshape(tile // here, here, width)
        for h in range(heads):
            ebuf[i, :, :, width + h * HDIM : width + (h + 1) * HDIM] = jnp.transpose(dk_acc[h]).astype(BF16).reshape(n, here, HDIM)
            ebuf[i, :, :, 2 * width + h * HDIM : 2 * width + (h + 1) * HDIM] = jnp.transpose(dv_acc[h]).astype(BF16).reshape(n, here, HDIM)
        for mask in range(1, n):
            give(i, mask).start()
        eland[li, i] = ebuf[i, 0]
        if i == 0:
            onward(wide_a)
            squares.depth()
    own_units(1)
    wide_b.send(0)
    nar.send(0)
    fetch_next = fetch_joint() if roomy else fetch_normed()
    for c in fetch_early if roomy else fetch_next:
        c.wait()
    joint = jnp.zeros((D, 3 * width), F32)
    for i in range(items):
        joint = joint + contract(buf_rows[:n, i * here : (i + 1) * here].reshape(seq, D), ebuf[i].reshape(seq, 3 * width), ((0,), (0,)))
    projg[...] = joint.astype(BF16)
    fetch_third = fetch_square(proj_hbm, 2 * D, buf_rows, 0)
    fetch_m = fetch_square(merge_hbm, 0, buf_rows, per)
    first.send(0)
    second.send(0)
    for c in (fetch_next if roomy else fetch_early) + fetch_late:
        c.wait()

    normal, inverse = normalize(emb_ref[...])
    lat = 2 * LATP
    wide = pred_ref.shape[2]
    spread = latitudes(lat)

    def seam(j, src, dst):
        return pltpu.make_async_remote_copy(
            src_ref=src, dst_ref=dst, send_sem=seams.at[2 * j], recv_sem=seams.at[2 * j + 1],
            device_id={"lon": lax.rem(li + n - 1, n)}, device_id_type=MESH,
        )

    def stacked(ref, i, w):
        at = i * here + (w // 2) * LATP
        corner = (w % 2) * 2
        return jnp.concatenate([ref[at : at + LATP, (corner + e) * VPAD : (corner + e + 1) * VPAD] for e in range(2)], axis=0)

    fetch_z.wait()
    for i in range(items):
        for w in range(wide // lat):
            pixels = contract(stacked(z_ref, i, w), spread, ((0,), (0,)))[:NOUT].astype(BF16)
            if w == 0:
                zsend[i] = pixels
            else:
                pred_ref[i, :, (w - 1) * lat : w * lat] = pixels
    west_z = seam(0, zsend, zland)
    west_z.start()

    for i in range(items):
        for mask in range(1, n):
            give(i, mask).wait_recv()
    scaling = scaling_ref[...].reshape(1, -1).astype(F32)
    dnormed = jnp.zeros((rows, D), F32)
    e3_sums = []
    for p, buf, at in ((0, buf_proj, 0), (1, buf_proj, per), (2, buf_rows, 0)):
        if p == 2:
            for c in fetch_third:
                c.wait()
        e3 = jnp.concatenate(
            [eland[g, :, :, p * width : (p + 1) * width].reshape(rows, width) for g in range(n)], axis=1
        )
        e3_sums.append(total(e3.astype(F32)))
        dnormed = dnormed + contract(e3, buf[at : at + per].reshape(D, D), ((1,), (1,)))
    demb = dmid_ref[...] + norm_back(dnormed, normal, inverse, scaling)
    demb_low = demb.astype(BF16)
    summed = demb[:here]
    for i in range(1, items):
        summed = summed + demb[i * here : (i + 1) * here]
    posbuf[...] = summed.astype(BF16).reshape(count, here // count, D)

    def pos_give(r):
        return pltpu.make_async_remote_copy(
            src_ref=posbuf.at[zi ^ r], dst_ref=posland.at[r], send_sem=pss.at[r], recv_sem=psr.at[r],
            device_id={"batch": zi ^ r}, device_id_type=MESH,
        )

    def pos_share(r):
        return pltpu.make_async_remote_copy(
            src_ref=posall.at[zi], dst_ref=posall.at[zi], send_sem=pgs.at[r], recv_sem=pgr.at[r],
            device_id={"batch": zi ^ r}, device_id_type=MESH,
        )

    for r in range(1, count):
        pos_give(r).start()
    mbuf[...] = contract(pooled_ref[...], demb_low, ((0,), (0,))).astype(BF16).reshape(mbuf.shape)
    merging.core()
    for c in fetch_m:
        c.wait()
    dpooled = contract(demb_low, buf_rows[per : 2 * per].reshape(D, D), ((1,), (1,))).astype(BF16)
    vectors = jnp.concatenate([
        total(dpooled.astype(F32)), total(demb_low.astype(F32)), total(dnormed * normal), total(dnormed), e3_sums[0], e3_sums[2], vecg_ref[...],
    ] + [jnp.concatenate([uplg_ref[2 * j], uplg_ref[2 * j + 1]], axis=1) for j in range(FF // D)] + [
        jnp.concatenate([base_ref[...], jnp.zeros((1, D - 4 * VPAD), F32)], axis=1), jnp.zeros((1, D), F32),
    ], axis=0).astype(BF16)
    for g in range(n):
        du3[g] = dpooled[:, g * width : (g + 1) * width]
        arbuf[g, JPAD : JPAD + 16] = vectors[:, g * width : (g + 1) * width]
    merging.plane()
    patches = patches_ref[...].astype(F32)
    dpatch_ref[...] = jnp.zeros_like(dpatch_ref)
    lines = -(-JPAD // width)

    def pool_core(mask):
        return pltpu.make_async_remote_copy(
            src_ref=arbuf.at[li ^ mask ^ 1], dst_ref=arland.at[mask], send_sem=asend.at[mask ^ 1], recv_sem=arecv.at[mask],
            device_id={"lon": li ^ 1}, device_id_type=MESH,
        )

    def pool_give(mask):
        return pltpu.make_async_remote_copy(
            src_ref=arbuf.at[li ^ mask], dst_ref=arland.at[mask ^ 1], send_sem=asend.at[mask], recv_sem=arecv.at[mask ^ 1],
            device_id={"lon": li ^ mask}, device_id_type=MESH,
        )

    def group(mask):
        g = li ^ mask
        halves, extra = [], []
        patch_total = jnp.zeros((rows, 4 * VPAD), F32)
        du_all, pv_all = du3[g], pv_ref[g]
        for s in range(heads):
            h = g * heads + s
            w = w_ref[h].astype(F32)
            wide = jnp.concatenate([w] * 5, axis=1)
            blended = (wide * patches).astype(BF16)
            du = du_all[:, s * HDIM : (s + 1) * HDIM]
            dbl = contract(du, pv_all[:, s * HDIM : (s + 1) * HDIM], ((1,), (1,)))
            halves.append(jnp.transpose(contract(du, blended, ((0,), (0,)))))
            x = dbl * patches
            dw = x[:, :VPAD]
            for c in range(1, 5):
                dw = dw + x[:, c * VPAD : (c + 1) * VPAD]
            da = w * (dw - jnp.sum(w * dw, axis=-1, keepdims=True)) * FACTOR
            da_wide = jnp.concatenate([da] * 5, axis=1)
            line = total(da_wide * patches)
            line = jnp.concatenate([line, jnp.zeros((1, lines * width - JPAD), F32)], axis=1) if lines * width > JPAD else line
            extra += [line[:, c * width : (c + 1) * width] for c in range(lines)]
            patch_total = patch_total + (wide[:, : 4 * VPAD] * dbl[:, : 4 * VPAD] + da_wide[:, : 4 * VPAD] * qrow_ref[h][:, : 4 * VPAD])
        dpatch_ref[...] += patch_total
        arbuf[g, :JPAD] = (jnp.concatenate(halves, axis=1) if heads > 1 else halves[0]).astype(BF16)
        tail = jnp.concatenate(extra + [jnp.zeros((ARROWS - JPAD - 16 - heads * lines, width), F32)], axis=0)
        arbuf[g, JPAD + 16 :] = tail.astype(BF16)

    evens = list(range(2, n, 2)) + [0]
    for mask in evens:
        group(mask ^ 1)
        pool_core(mask).start()
    onward(wide_b, nar)
    for mask in evens:
        group(mask)
        pool_core(mask).wait_recv()
        if mask:
            g = li ^ mask
            arbuf[g] = (arbuf[g].astype(F32) + arland[mask].astype(F32)).astype(BF16)
            pool_give(mask).start()
    def wide_give(mask):
        return pltpu.make_async_remote_copy(
            src_ref=wcolbuf.at[li ^ mask], dst_ref=wcol_ref.at[li], send_sem=ws.at[mask], recv_sem=wr.at[mask],
            device_id={"lon": li ^ mask}, device_id_type=MESH,
        )

    def col_give(mask):
        return pltpu.make_async_remote_copy(
            src_ref=pcolbuf.at[li ^ mask], dst_ref=pcol_ref.at[li], send_sem=cs.at[mask], recv_sem=cr.at[mask],
            device_id={"lon": li ^ mask}, device_id_type=MESH,
        )

    chunk = arbuf[li].astype(F32) + arland[0].astype(F32)
    for mask in range(2, n, 2):
        pool_give(mask).wait_recv()
        chunk = chunk + arland[mask ^ 1].astype(F32)
    piece = ARROWS // count
    archunk[...] = chunk.astype(BF16).reshape(archunk.shape)

    def z_give(r):
        return pltpu.make_async_remote_copy(
            src_ref=archunk.at[zi ^ r], dst_ref=arz.at[r], send_sem=azs.at[r], recv_sem=azr.at[r],
            device_id={"batch": zi ^ r}, device_id_type=MESH,
        )

    def z_share(r):
        return pltpu.make_async_remote_copy(
            src_ref=ar_ref.at[li, zi], dst_ref=ar_ref.at[li, zi], send_sem=ags.at[r], recv_sem=agr.at[r],
            device_id={"batch": zi ^ r}, device_id_type=MESH,
        )

    for r in range(1, count):
        z_give(r).start()
    onward(first, second)
    pos_sum = posbuf[zi].astype(F32)
    for r in range(1, count):
        pos_give(r).wait_recv()
        pos_sum = pos_sum + posland[r].astype(F32)
    posall[zi] = pos_sum.astype(BF16)
    piece_sum = archunk[zi].astype(F32)
    for r in range(1, count):
        z_give(r).wait_recv()
        piece_sum = piece_sum + arz[r].astype(F32)
    ar_ref[li, zi] = piece_sum.astype(BF16)

    def l_share(mask, r):
        return pltpu.make_async_remote_copy(
            src_ref=ar_ref.at[li, zi ^ r], dst_ref=ar_ref.at[li, zi ^ r], send_sem=bgs.at[mask, r], recv_sem=bgr.at[mask, r],
            device_id={"lon": li ^ mask}, device_id_type=MESH,
        )

    def l_relay(mask, r):
        return pltpu.make_async_remote_copy(
            src_ref=ar_ref.at[li ^ mask, zi ^ r], dst_ref=ar_ref.at[li ^ mask, zi ^ r], send_sem=bgs.at[mask | 1, r], recv_sem=bgr.at[mask | 1, r],
            device_id={"lon": li ^ 1}, device_id_type=MESH,
        )

    def spread_out(r):
        for mask in range(2, n, 2):
            l_share(mask, r).start()
        l_relay(0, r).start()

    for r in range(1, count):
        z_share(r).start()
    spread_out(0)
    for r in range(1, count):
        pos_share(r).start()
    nar_ref[...] = nar.absorb(steps - 1)
    for k, one in enumerate((wide_a, wide_b)):
        w_total = one.absorb(steps - 1)
        for c in range(cut):
            turned = jnp.transpose(w_total[c]).astype(BF16)
            for l in range(n):
                wcolbuf[l, k * cut + c] = turned[l * rd : (l + 1) * rd]
    for mask in range(1, n):
        wide_give(mask).start()
    wcol_ref[li] = wcolbuf[li]
    for r in range(1, count):
        z_share(r).wait_recv()
        spread_out(r)
    merging.depth()
    for i in range(items):
        var = lax.broadcasted_iota(jnp.int32, (VPAD, NVAR), 0)
        choose = (var == ids_ref[i : i + 1, :]).astype(BF16)
        for w in range(wide // lat):
            parts = pieces(stacked(dpatch_ref, i, w), 2)
            pixels = contract(parts[:lat], spread, ((0,), (0,))) + contract(parts[lat:], spread, ((0,), (0,)))
            parts = pieces(pixels, 2)
            slots = contract(choose, parts[:VPAD], ((0,), (0,))) + contract(choose, parts[VPAD:], ((0,), (0,)))
            if w == 0:
                gsend[i] = slots
            else:
                grad_ref[i, :, (w - 1) * lat : w * lat] = slots
    west_g = seam(1, gsend, gland)
    west_g.start()
    west_z.wait()
    pred_ref[:, :, wide - lat :] = zland[...]

    sqo_ref[...] = squares.total()
    top, low = first.absorb(steps - 1).astype(BF16), second.absorb(steps - 1).astype(BF16)
    pcolbuf[...] = jnp.concatenate([top, low], axis=0).reshape(pcolbuf.shape)
    for mask in range(1, n):
        col_give(mask).start()
    pcol_ref[li] = pcolbuf[li]
    for r in range(count):
        for mask in range(2, n, 2):
            l_share(mask, r).wait_recv()
            l_relay(mask, r).start()
    for r in range(1, count):
        pos_share(r).wait_recv()
    pos_ref[...] = posall[...].reshape(here, D).astype(F32)
    mer_ref[...] = merging.total()
    for r in range(count):
        for mask in range(0, n, 2):
            l_relay(mask, r).wait_recv()
    for mask in range(1, n):
        col_give(mask).wait()
        wide_give(mask).wait()
        give_do(mask).wait_send()
        for i in range(items):
            give(i, mask).wait_send()
    for mask in range(0, n, 2):
        pool_core(mask).wait_send()
        if mask:
            pool_give(mask).wait_send()
        for r in range(count):
            l_relay(mask, r).wait_send()
            if mask:
                l_share(mask, r).wait_send()
    for r in range(1, count):
        z_give(r).wait_send()
        z_share(r).wait_send()
        pos_give(r).wait_send()
        pos_share(r).wait_send()
    for part in (first, second, nar, wide_a, wide_b, squares, merging):
        part.drain()
    west_g.wait()
    grad_ref[:, :, wide - lat :] = gland[...]


def rear_part(
    do, squares, second, up, wown, nown, uplown, read, qkv, lse, rows_all, projecting, merging, emb, dmid, pooled, scaling, patches, pool_w, qrow, pv,
    vec_grads, uplift_grads, base, ids, z, direct, n, count, items, here, heads,
):
    rows, width, seq = items * here, heads * HDIM, n * here
    rd, hid = D // (n * count), FF // (n * count)
    own = count * hid
    wide = here // LATP * 2 * 2 * LATP
    shape = jax.ShapeDtypeStruct
    vm, hbm = pl.BlockSpec(memory_space=pltpu.VMEM), pl.BlockSpec(memory_space=pl.ANY)
    cols = squares.shape[3]
    piece = ARROWS // count
    hz = D // count // 2
    dma = pltpu.SemaphoreType.DMA
    lsem, zsem, isem, psem = dma((n,)), dma((count,)), dma((items, n)), dma((n, count))
    low = lambda *s: pltpu.VMEM(s, BF16)
    full = lambda *s: pltpu.VMEM(s, F32)
    pos = low(count, here // count, D)
    nbuf, wbuf, pbuf = low(count, hid, 4 * VPAD), low(count, count // 2, hid, D // count), low(count, hz, 3 * width)
    one, two = RowSum.scratch(n, count, rd, cols), RowSum.scratch(n, count, rd, D)
    return pl.pallas_call(
        functools.partial(rear_kernel, n, count, items, here, heads, direct),
        in_specs=[vm, vm, hbm, hbm, hbm, hbm, vm, vm, hbm, vm, hbm, hbm, hbm, hbm, hbm, hbm, vm, hbm, hbm, vm, hbm, vm, vm, vm, vm, hbm],
        out_specs=(vm,) * 9,
        out_shape=(
            shape((hid, 4 * VPAD), F32), shape((rd, cols), F32), shape((here, D), F32), shape((rd, D), F32),
            shape((items, NOUT, wide), BF16), shape((items, NVAR, wide), F32), shape((n, count, piece, width), BF16), shape((n, count, rd, hid), BF16), shape((n, rd, 3 * width), BF16),
        ),
        scratch_shapes=[
            full(rows, 4 * VPAD), low(items, NOUT, 2 * LATP), full(items, NVAR, 2 * LATP), low(items, NOUT, 2 * LATP), full(items, NVAR, 2 * LATP), dma((4,)),
            low(D, own), low(own, D), low(n, rows, D), low(2 * D // rows, rows, D), low(n, rows, 4 * VPAD), full(own // 2, 4 * VPAD), full(own // 2, D),
            low(count, hid, 4 * VPAD), low(count, count, hid, D // count), low(n, items, here, width),
            low(items, n, here, 3 * width), low(n, items, here, 3 * width), full(heads, HDIM, seq), full(heads, HDIM, seq),
            low(D, 3 * width), low(count, n, rd, D), low(n, rows, width),
            low(n, ARROWS, width), low(n, ARROWS, width), low(count, piece, width), low(count, piece, width), pos, pos, pos,
            low(n, count, rd, hid), low(n, rd, 3 * width), full(1, own), full(n * count, 1, hid),
            low(items, seq, 3 * width), full(rows, D), full(rows, D), low(rows, D), low(rows, JPAD), low(HEADS, rows, VPAD), low(n, JPAD, width), low(rows, 4 * VPAD),
            dma((2 * count + n + items + 4 * (D // rows) + 9,)), lsem, lsem, isem, isem, nbuf, nbuf, zsem, zsem, wbuf, wbuf, zsem, zsem, wbuf, wbuf, zsem, zsem,
            pbuf, pbuf, zsem, zsem, pbuf, pbuf, zsem, zsem,
            lsem, lsem, zsem, zsem, zsem, zsem, psem, psem, zsem, zsem, zsem, zsem, lsem, lsem, lsem, lsem,
        ] + one[:5] + two[:5] + one[5:] + two[5:],
        compiler_params=pltpu.CompilerParams(collective_id=3, has_side_effects=True, vmem_limit_bytes=63 * MIB + 3 * MIB // 4),
        name="rear",
    )(do, squares, second, up, wown, nown, uplown, read, qkv, lse, rows_all, projecting, merging, emb, dmid, pooled, scaling, patches, pool_w, qrow, pv, vec_grads, uplift_grads, base, ids, z)


def finish_kernel(
    n, count, heads, sum_ref, wcol_ref, pcol_ref, nar_ref, sq_ref, mer_ref, pos_ref, pred_ref, grad_ref, read_ref, keymap_ref, embed_ref, val_ref, kk_ref, beacon_ref,
    prediction_ref, fields_ref, position_ref, patching_ref, tagging_ref, beacon_out, keying_ref, valuing_ref, lifting_ref, merging_ref, offset_ref, scaling_ref,
    centre_ref, projecting_ref, biasing_ref, mixing_ref, nudging_ref, rescaling_ref, recentre_ref, widening_ref, uplift_ref,
    narrowing_ref, settle_ref, reading_ref, baseline_ref,
):
    li, zi = lax.axis_index("lon"), lax.axis_index("batch")
    block = zi * n + li
    rd = D // (n * count)
    hid = FF // (n * count)
    width = heads * HDIM
    lines = -(-JPAD // width)
    exact = lambda a, b, dims: lax.dot_general(a, b, (dims, ((), ())), precision=HIGH, preferred_element_type=F32)

    def mine(size):
        row = lax.broadcasted_iota(jnp.int32, (D, size), 0)
        col = lax.broadcasted_iota(jnp.int32, (D, size), 1)
        return (row == ((block * size + col) & (D - 1))).astype(BF16)

    lat = 2 * LATP
    for i in range(pred_ref.shape[0]):
        for w in range(pred_ref.shape[2] // lat):
            prediction_ref[i, :, w, :] = pred_ref[i, :, w * lat : (w + 1) * lat]
            fields_ref[i, :, w, :] = grad_ref[i, :, w * lat : (w + 1) * lat]
    position_ref[...] = pos_ref[...]
    merging_ref[...] = mer_ref[...]
    mixing_ref[...] = sq_ref[:, :D]
    narrowing_ref[...] = folded(product(pieces(nar_ref[...], 2), read_ref[...]), 2)
    reading_ref[...] = exact(sq_ref[:, D:], places(4 * NOUT, 4 * VPAD, 0, 4, 2).astype(F32), ((1,), (1,)))
    for g in range(n):
        for p in range(3):
            projecting_ref[:, p * D + g * width : p * D + (g + 1) * width] = pcol_ref[g, :, p * width : (p + 1) * width].astype(F32)
        for c in range(count):
            at = (c * n + g) * hid
            widening_ref[:, at : at + hid] = wcol_ref[g, c].astype(F32)

    sums = [sum_ref[g].reshape(ARROWS, width) for g in range(n)]
    vectors = jnp.concatenate([a[JPAD : JPAD + 16] for a in sums], axis=1)
    one, two, four = mine(rd), mine(2 * rd), mine(4 * rd)
    short = product(vectors, one)
    for j, ref in ((0, lifting_ref), (1, offset_ref), (2, scaling_ref), (3, centre_ref), (6, nudging_ref), (7, rescaling_ref), (8, recentre_ref), (9, settle_ref)):
        ref[...] = short[j : j + 1].reshape(rd)

    def across(start, size, select, ref):
        found = product(vectors, select)
        row = (block * size) // D
        total = jnp.zeros((1, size), F32)
        for k in range(size // rd):
            total = total + jnp.where(row == k, found[start + k : start + k + 1], 0.0)
        ref[...] = total.reshape(size)

    across(4, 2 * rd, two, biasing_ref)
    across(10, 4 * rd, four, uplift_ref)
    baseline_ref[...] = contract(vectors[:, : 4 * VPAD], places(4 * NOUT, 4 * VPAD, 0, 4, 2), ((1,), (1,)))[14:15].reshape(4 * NOUT)

    dqz = []
    for h in range(HEADS):
        base = JPAD + 16 + (h % heads) * lines
        lined = sums[h // heads]
        dqz.append(jnp.concatenate([lined[base + c : base + c + 1].astype(F32) for c in range(lines)], axis=1)[:, :JPAD])
    dqz = jnp.concatenate(dqz, axis=0)
    embed_mine, val_mine = embed_ref[...], val_ref[...]
    dembed = exact(keymap_ref[...], dqz, ((0,), (0,)))
    for g in range(n):
        dpv = sums[g][:JPAD]
        valuing_ref[:, g * width : (g + 1) * width] = contract(embed_mine, dpv, ((0,), (0,)))
        dembed = dembed + contract(val_mine[:, g * width : (g + 1) * width], dpv, ((1,), (1,)))
    patching_ref[...] = exact(dembed, places(4 * NVAR, JPAD, 0, 4, 2).astype(F32), ((1,), (1,)))
    tagging_ref[...] = dembed[:, 4 * VPAD : 4 * VPAD + NVAR]
    dkeymap = product(dqz.astype(BF16), embed_mine)
    keying_ref[...] = exact(dkeymap, by_head(beacon_ref[...].reshape(1, -1).astype(F32)), ((0,), (0,)))
    down = exact(dqz, kk_ref[...], ((1,), (0,)))
    head = lax.broadcasted_iota(jnp.int32, (HEADS, rd), 0)
    col = block * rd + lax.broadcasted_iota(jnp.int32, (HEADS, rd), 1)
    beacon_out[...] = jnp.sum(jnp.where(col >> 6 == head, down, 0.0), axis=0, keepdims=True).reshape(rd)


def finish(summed, wcol, pcol, nar, squares, mer, pos, pred, grad, read, keymap, embed, valuing, kk, beacon, n, count, heads):
    rd, hid = D // (n * count), FF // (n * count)
    shape = lambda *s: jax.ShapeDtypeStruct(s, F32)
    vec = shape(rd)
    lat = 2 * LATP
    items, wide = pred.shape[0], pred.shape[2] // lat
    return pl.pallas_call(
        functools.partial(finish_kernel, n, count, heads),
        out_shape=(
            jax.ShapeDtypeStruct((items, NOUT, wide, lat), BF16), shape(items, NVAR, wide, lat),
            shape(*pos.shape), shape(rd, 4 * NVAR), shape(rd, NVAR), vec, shape(rd, D), shape(rd, D), vec, shape(rd, D), vec, vec, vec,
            shape(rd, 3 * D), shape(2 * rd), shape(rd, D), vec, vec, vec, shape(rd, FF), shape(4 * rd), shape(hid, D), vec,
            shape(rd, 4 * NOUT), shape(4 * NOUT),
        ),
        compiler_params=pltpu.CompilerParams(vmem_limit_bytes=60 * MIB),
        name="finish",
    )(summed, wcol, pcol, nar, squares, mer, pos, pred, grad, read, keymap, embed, valuing, kk, beacon)


def per_device(
    fields, variable_ids, variable_mask, position, patching, tagging, beacon, keying, valuing, lifting,
    merging, offset, scaling, centre, projecting, biasing, mixing, nudging, rescaling, recentre,
    widening, uplift, narrowing, settle, reading, baseline, cotangent,
):
    count, lon = lax.axis_size("batch"), lax.axis_size("lon")
    zi, li = lax.axis_index("batch"), lax.axis_index("lon")
    items, cols_dev, lat = fields.shape[0], fields.shape[2], fields.shape[3]
    upatch = cols_dev // 2
    here = upatch * LATP
    heads = HEADS // lon
    width = heads * HDIM
    rows_dev = D // (count * lon)
    hid = FF // (count * lon)
    f = lambda a: a.astype(F32)

    columns = lambda a, start, size: lax.dynamic_slice_in_dim(a, start, size, 1)
    direct_heads, direct_hidden = width % 128 == 0, hid % 128 == 0
    proj_own = projecting if direct_heads else jnp.concatenate([columns(projecting, p * D + li * width, width) for p in range(3)], axis=1)
    wide_own = widening if direct_hidden else jnp.concatenate([columns(widening, (c * lon + li) * hid, hid) for c in range(count)], axis=1)
    (
        attended, normed_all, joint, lse, dpred_all, embedded, pooled, patches, pool_w, qrow, pv, dpred, base, reading_p, keymap_mine, embed_mine, val_mine, kk_mine,
    ) = front(
        fields, cotangent, variable_ids, variable_mask, patching.T, tagging.T, reading.T, beacon, lifting, offset, scaling, centre, biasing,
        position.reshape(here, D), keying, valuing, merging, proj_own, rows_dev, direct_heads, lon, items, here, heads,
    )
    outputs, squares, dmiddle, do, vec_grads, uplift_grads, second_all = middle_part(
        attended, embedded, mixing, nudging, rescaling, recentre, settle, uplift, baseline, widening, narrowing, reading_p, dpred,
        lon, items, here, heads,
    )
    nar, squares, pos, mer, prediction, fields_gradient, summed, wide_cols, joint_cols = rear_part(
        do, squares.reshape(count, lon, rows_dev, -1), second_all, dpred_all, wide_own, narrowing, uplift, reading_p,
        joint, lse, normed_all, projecting, merging, embedded, dmiddle, pooled, scaling, patches, pool_w, qrow, pv, vec_grads, uplift_grads, base,
        variable_ids, outputs, direct_hidden, lon, count, items, here, heads,
    )
    outs = list(finish(
        summed, wide_cols, joint_cols, nar, squares, mer, pos, prediction, fields_gradient, reading_p, keymap_mine, embed_mine, val_mine, kk_mine, beacon,
        lon, count, heads,
    ))
    outs[2] = outs[2].reshape(upatch, LATP, D)
    return tuple(outs)


def solution(mesh):
    both = ("batch", "lon")
    image, matrix, vector = P("batch", None, "lon", None), P(both, None), P(both)
    return jax.shard_map(
        per_device,
        mesh=mesh,
        in_specs=(image, P("batch", None), P("batch", None), P("lon", None, None)) + (P(),) * 22 + (image,),
        out_specs=(
            image, image, P("lon", None, None), matrix, matrix, vector, matrix, matrix, vector, matrix, vector,
            vector, vector, matrix, vector, matrix, vector, vector, vector, matrix, vector, matrix, vector, matrix, P(),
        ),
        check_vma=False,
    )
```

```python
import functools

import jax
import jax.numpy as jnp
from jax import lax
from jax.experimental import pallas as pl
from jax.experimental.pallas import tpu as pltpu
from jax.sharding import PartitionSpec as P

D = 1024
HEADS = 16
HDIM = 64
FF = 4096
NVAR = 48
NOUT = 48
LATP = 32
VPAD = 64
JPAD = 5 * VPAD

HIGH = lax.Precision.HIGHEST
EPSILON = 1e-06
F32 = jnp.float32
BF16 = jnp.bfloat16
FACTOR = HDIM ** (-0.5)
MIB = 2**20
MESH = pl.DeviceIdType.MESH


def product(left, right):
    return jnp.dot(left, right, preferred_element_type=F32)


def contract(left, right, dims):
    return lax.dot_general(left, right, (dims, ((), ())), preferred_element_type=F32)


def normalize(values):
    centred = values - jnp.mean(values, axis=-1, keepdims=True)
    inverse = lax.rsqrt(jnp.mean(centred * centred, axis=-1, keepdims=True) + EPSILON)
    return centred * inverse, inverse


def norm_back(upstream, normal, inverse, scaler):
    weighted = upstream * scaler
    return inverse * (
        weighted
        - jnp.mean(weighted, axis=-1, keepdims=True)
        - normal * jnp.mean(weighted * normal, axis=-1, keepdims=True)
    )


def gelu_parts(x):
    c = 0.7978845608028654
    t = jnp.tanh(c * (x + 0.044715 * (x * x * x)))
    value = 0.5 * x * (1.0 + t)
    slope = 0.5 * (1.0 + t) + 0.5 * x * (1.0 - t * t) * (c * (1.0 + 3 * 0.044715 * x * x))
    return value, slope


def places(rows, cols, start, step, shift):
    row = lax.broadcasted_iota(jnp.int32, (rows, cols), 0)
    col = lax.broadcasted_iota(jnp.int32, (rows, cols), 1)
    return (start + (row & (step - 1)) * VPAD + (row >> shift) == col).astype(BF16)


def latitudes(lat):
    row = lax.broadcasted_iota(jnp.int32, (lat, lat), 0)
    col = lax.broadcasted_iota(jnp.int32, (lat, lat), 1)
    half = lat // 2
    return (2 * (row & (half - 1)) + (row >> (half.bit_length() - 1)) == col).astype(BF16)


def by_head(row):
    head = lax.broadcasted_iota(jnp.int32, (HEADS, D), 0)
    col = lax.broadcasted_iota(jnp.int32, (HEADS, D), 1)
    return jnp.where(col >> 6 == head, jnp.broadcast_to(row, (HEADS, D)), jnp.zeros((), row.dtype))


def pieces(a, count):
    parts = []
    for _ in range(count):
        parts.append(a.astype(BF16))
        a = a - parts[-1].astype(F32)
    return jnp.concatenate(parts, axis=0)


class Moves:
    def __init__(self, sem):
        self.sem, self.started = sem, []

    def go(self, src, dst):
        copy = pltpu.make_async_copy(src, dst, self.sem.at[len(self.started)])
        self.started.append(copy)
        copy.start()
        return copy


def folded(a, count):
    rows = a.shape[0] // count
    total = a[:rows]
    for i in range(1, count):
        total = total + a[i * rows : (i + 1) * rows]
    return total


def barrier_all(n, li):
    sem = pltpu.get_barrier_semaphore()
    for mask in range(1, n):
        pl.semaphore_signal(sem, inc=1, device_id={"lon": li ^ mask}, device_id_type=MESH)
    pl.semaphore_wait(sem, n - 1)


class Gather:
    def __init__(self, n, li, at, send, recv):
        self.n, self.li, self.at, self.send, self.recv = n, li, at, send, recv
        self.bits = [1 << i for i in range(1, n.bit_length() - 1)]

    def order(self, piece):
        return self.bits if piece % 2 == 0 else self.bits[::-1]

    def copy(self, mask, piece):
        bit = 1 if mask & 1 else [b for b in self.order(piece) if b & mask][-1]
        return pltpu.make_async_remote_copy(
            src_ref=self.at(mask ^ bit, piece),
            dst_ref=self.at(mask, piece),
            send_sem=self.send.at[mask, piece],
            recv_sem=self.recv.at[mask, piece],
            device_id={"lon": self.li ^ bit},
            device_id_type=MESH,
        )

    def forward(self, mask, piece):
        order = self.order(piece)
        used = [i for i, b in enumerate(order) if b & mask]
        for b in order[(used[-1] + 1 if used else 0):]:
            self.copy(mask | b, piece).start()
        self.copy(mask | 1, piece).start()

    def start(self, pieces):
        for piece in pieces:
            self.forward(0, piece)

    def evens(self):
        return sorted(range(2, self.n, 2), key=lambda m: bin(m).count("1"))

    def relay(self, pieces, first=True, rest=True):
        for depth in range(1, len(self.bits) + 1):
            if (first if depth == 1 else rest):
                for piece in pieces:
                    for mask in self.evens():
                        if bin(mask).count("1") == depth:
                            self.copy(mask, piece).wait_recv()
                            self.forward(mask, piece)

    def finish(self, pieces):
        for mask in range(1, self.n, 2):
            for piece in pieces:
                self.copy(mask, piece).wait_recv()

    def drain(self, pieces):
        for mask in range(1, self.n):
            for piece in pieces:
                self.copy(mask, piece).wait_send()


def front_kernel(
    n, items, here, heads, direct, fields_ref, cot_ref, ids_ref, mask_ref, patching_ref, tagging_ref, read_ref, beacon_ref, lifting_ref,
    offset_ref, scaling_ref, centre_ref, biasing_ref, place_ref, key_hbm, val_hbm, mer_hbm, proj_hbm,
    att_ref, all_out, qkv_out, lse_ref, up_out, emb_out, pooled_out, patches_out, pw_out, qrow_ref, pv_out, dpred_ref, base_ref, readp_out,
    keymap_mine, embed_mine, val_mine, kk_mine,
    keying, valuing, merging, own_w, load, seam, seam_land, seam_send, seam_recv, up_ref, usend, urecv,
    rows_ref, obuf, land, gsend, grecv, osend, orecv, keep, qkv_ref, emb_ref, pooled_ref, patches_ref, pw_ref, pv_ref, readp_ref,
):
    li = lax.axis_index("lon")
    block = lax.axis_index("batch") * n + li
    rd = val_mine.shape[0]
    width = heads * HDIM
    seq = n * here
    tile = min(seq, 512)
    rows = items * here
    lat = 2 * LATP
    wide = fields_ref.shape[2]
    loads, keeps = Moves(load), Moves(keep)
    fetch_key, fetch_val, fetch_mer = (loads.go(h, v) for h, v in ((key_hbm, keying), (val_hbm, valuing), (mer_hbm, merging)))
    if direct:
        fetch_own = [loads.go(proj_hbm.at[:, pl.ds(pl.multiple_of(p * D + li * width, width), width)], own_w.at[:, p * width : (p + 1) * width]) for p in range(3)]
    else:
        fetch_own = [loads.go(proj_hbm, own_w)]
    for i in range(items):
        seam[0, i] = fields_ref[i, :, wide - 1, :]
        seam[1, i] = cot_ref[i, :, wide - 1, :]
    barrier_all(n, li)
    east = pltpu.make_async_remote_copy(
        src_ref=seam, dst_ref=seam_land, send_sem=seam_send, recv_sem=seam_recv,
        device_id={"lon": lax.rem(li + 1, n)}, device_id_type=MESH,
    )
    east.start()

    row = lambda ref: ref[...].reshape(1, -1)
    embed = contract(places(4 * NVAR, JPAD, 0, 4, 2), patching_ref[...], ((0,), (0,)))
    embed = (embed + contract(places(NVAR, JPAD, 4 * VPAD, 1, 0), tagging_ref[...], ((0,), (0,)))).astype(BF16)
    readp_ref[...] = contract(places(4 * NOUT, 4 * VPAD, 0, 4, 2), read_ref[...], ((0,), (0,))).astype(BF16)
    keeps.go(readp_ref, readp_out)

    fetch_key.wait()
    keymap = contract(by_head(row(beacon_ref)), keying[...], ((1,), (1,)))
    qrow = folded(contract(pieces(keymap, 3), embed, ((1,), (1,))), 3)
    for h in range(HEADS):
        qrow_ref[h] = qrow[h : h + 1, :]
    fetch_val.wait()
    pv = product(embed, valuing[...]).astype(BF16)
    for g in range(n):
        pv_ref[g] = pv[:, g * width : (g + 1) * width]
    keeps.go(pv_ref, pv_out)

    spread = latitudes(lat)
    var = lax.broadcasted_iota(jnp.int32, (VPAD, NVAR), 0)
    same = (var == lax.broadcasted_iota(jnp.int32, (VPAD, NVAR), 1)).astype(BF16)
    lane = lax.broadcasted_iota(jnp.int32, (8, VPAD), 1)
    patches_ref[:, 4 * VPAD :] = jnp.ones((rows, VPAD), BF16)
    east.wait()

    def tokens(ref, which, i, choose, out):
        pixels = [seam_land[which, i]] + [ref[i, :, w, :] for w in range(wide - 1)]
        stack = jnp.concatenate([product(choose, p).astype(BF16) for p in pixels], axis=0)
        turned = contract(spread, stack, ((1,), (1,))).astype(BF16)
        for w in range(wide):
            token = turned[:, w * VPAD : (w + 1) * VPAD]
            for e in range(2):
                corner = (w % 2) * 2 + e
                at = i * here + (w // 2) * LATP
                out[at : at + LATP, corner * VPAD : (corner + 1) * VPAD] = token[e * LATP : (e + 1) * LATP]

    for i in range(items):
        tokens(cot_ref, 1, i, same, dpred_ref)
    half_rows = rows // 2
    ups = Gather(n, li, lambda slot, piece: up_ref.at[slot, pl.ds(piece * half_rows, half_rows)], usend, urecv)
    up_ref[0] = dpred_ref[...]
    ups.start([0, 1])
    base_ref[...] = jnp.sum(dpred_ref[...].astype(F32), axis=0, keepdims=True)
    cuts = 2
    share = here // cuts
    pieces_of = lambda i: list(range(cuts * i, cuts * (i + 1)))

    def at(slot, piece):
        return rows_ref.at[piece // cuts, slot, pl.ds((piece % cuts) * share, share)]

    gather = Gather(n, li, at, gsend, grecv)
    lifting = row(lifting_ref).astype(F32)
    offset, scaling, centre = (row(a).astype(F32) for a in (offset_ref, scaling_ref, centre_ref))

    for i in range(items):
        part = slice(i * here, (i + 1) * here)
        choose = (var == ids_ref[i : i + 1, :]).astype(BF16)
        tokens(fields_ref, 0, i, choose, patches_ref)
        kept = jnp.broadcast_to(mask_ref[i : i + 1, :], (8, NVAR)).astype(F32).astype(BF16)
        live = contract(kept, choose, ((1,), (1,)))
        mask = jnp.broadcast_to(jnp.where(lane < NVAR, jnp.where(live > 0.5, 0.0, -1e30), -2e30)[:1], (here, VPAD))
        patches = patches_ref[part, :].astype(F32)
        for pair in range(HEADS // 2):
            halves = []
            for h in (2 * pair, 2 * pair + 1):
                x = patches[:, : 4 * VPAD] * qrow[h : h + 1, : 4 * VPAD]
                x = x[:, : 2 * VPAD] + x[:, 2 * VPAD :]
                logits = (x[:, :VPAD] + x[:, VPAD:] + qrow[h : h + 1, 4 * VPAD :]) * FACTOR
                logits = jnp.where(mask == 0.0, logits, mask)
                grown = jnp.exp(logits - jnp.max(logits, axis=-1, keepdims=True))
                w = grown / jnp.sum(grown, axis=-1, keepdims=True)
                pw_ref[h, part, :] = w.astype(BF16)
                blended = (jnp.concatenate([w] * 5, axis=1) * patches).astype(BF16)
                halves.append(product(blended, pv[:, h * HDIM : (h + 1) * HDIM]))
            cols = slice(pair * 128, pair * 128 + 128)
            pooled_ref[part, cols] = (jnp.concatenate(halves, axis=1) + lifting[:, cols]).astype(BF16)
        if i == 0:
            fetch_mer.wait()
        emb = product(pooled_ref[part, :], merging[...]) + offset + place_ref[...].astype(F32)
        emb_ref[part, :] = emb
        normal, _ = normalize(emb)
        rows_ref[i, 0] = (normal * scaling + centre).astype(BF16)
        gather.start(pieces_of(i))
    ups.relay([0, 1])
    gather.relay(pieces_of(0))
    for src, dst in ((patches_ref, patches_out), (pw_ref, pw_out), (pooled_ref, pooled_out), (emb_ref, emb_out)):
        keeps.go(src, dst)

    one = (lax.broadcasted_iota(jnp.int32, (D, rd), 0) == block * rd + lax.broadcasted_iota(jnp.int32, (D, rd), 1)).astype(BF16)
    embed_mine[...] = product(embed, one).astype(BF16)
    val_mine[...] = contract(one, valuing[...], ((0,), (0,))).astype(BF16)
    keymap_mine[...] = jnp.dot(keymap, one.astype(F32), precision=HIGH, preferred_element_type=F32)
    kk_mine[...] = product(embed, product(keying[...], one).astype(BF16))

    def give(i, mask):
        return pltpu.make_async_remote_copy(
            src_ref=obuf.at[i, mask],
            dst_ref=land.at[li, i],
            send_sem=osend.at[i, mask],
            recv_sem=orecv.at[i, mask],
            device_id={"lon": li ^ mask},
            device_id_type=MESH,
        )

    column = lax.broadcasted_iota(jnp.int32, (D, width), 1)
    mine = (lax.broadcasted_iota(jnp.int32, (D, width), 0) == li * width + column).astype(BF16)
    biases = jnp.broadcast_to(row(biasing_ref), (8, 2 * D))
    own_bias = jnp.concatenate(
        [product(biases[:, :D], mine)[:1], jnp.zeros((1, width), F32), product(biases[:, D:], mine)[:1]], axis=1
    )
    for c in fetch_own:
        c.wait()
    for i in range(items):
        later = pieces_of(i + 1) if i + 1 < items else []
        gather.finish(pieces_of(i))
        keeps.go(rows_ref.at[i], all_out.at[i])
        joint = product(rows_ref[i].reshape(seq, D), own_w[...]) + own_bias
        qkv_ref[i] = joint.astype(BF16)
        keeps.go(qkv_ref.at[i], qkv_out.at[i])
        for t in range(seq // tile):
            outs = []
            for h in range(heads):
                q = qkv_ref[i, t * tile : (t + 1) * tile, h * HDIM : (h + 1) * HDIM] * FACTOR
                k = qkv_ref[i, :, width + h * HDIM : width + (h + 1) * HDIM]
                v = qkv_ref[i, :, 2 * width + h * HDIM : 2 * width + (h + 1) * HDIM]
                scores = contract(q, k, ((1,), (1,)))
                top = jnp.max(scores, axis=1, keepdims=True)
                grown = jnp.exp(scores - top)
                total = jnp.sum(grown, axis=1, keepdims=True)
                outs.append(product(grown.astype(BF16), v) / total)
                lse = top + jnp.log(total)
                lse_ref[i, h : h + 1, t * tile : (t + 1) * tile] = jnp.transpose(lse)
                if t == 0 and h == 0:
                    gather.relay(later)
            out = jnp.concatenate(outs, axis=1) if heads > 1 else outs[0]
            slots = range(t * (tile // here), (t + 1) * (tile // here))
            obuf[i, t * (tile // here) : (t + 1) * (tile // here)] = out.astype(BF16).reshape(tile // here, here, width)
            for mask in slots:
                if mask:
                    give(i, mask).start()
        land[li, i] = obuf[i, 0]
    ups.finish([0, 1])
    keeps.go(up_ref, up_out)
    for i in range(items):
        for mask in range(1, n):
            give(i, mask).wait_recv()
        att_ref[i * here : (i + 1) * here, :] = jnp.concatenate([land[g, i] for g in range(n)], axis=1)
    ups.drain([0, 1])
    for i in range(items):
        gather.drain(pieces_of(i))
        for mask in range(1, n):
            give(i, mask).wait_send()
    for c in keeps.started:
        c.wait()


def front(fields, cot, ids, mask, patching, tagging, reading, beacon, lifting, offset, scaling, centre, biasing, place, keying, valuing, merging, proj, rd, direct, n, items, here, heads):
    width = heads * HDIM
    seq = n * here
    rows = items * here
    vm, hbm = pl.BlockSpec(memory_space=pltpu.VMEM), pl.BlockSpec(memory_space=pl.ANY)
    shape = jax.ShapeDtypeStruct
    dma = pltpu.SemaphoreType.DMA
    low = lambda *a: pltpu.VMEM(a, BF16)
    edge = low(2, items, NVAR, 2 * LATP)
    return pl.pallas_call(
        functools.partial(front_kernel, n, items, here, heads, direct),
        in_specs=[vm] * 14 + [hbm] * 4,
        out_specs=(vm, hbm, hbm, vm, hbm, hbm, hbm, hbm, hbm, vm, hbm, vm, vm, hbm, vm, vm, vm, vm),
        out_shape=(
            shape((rows, D), BF16), shape((items, n, here, D), BF16), shape((items, seq, 3 * width), BF16), shape((items, heads, seq), F32),
            shape((n, rows, 4 * VPAD), BF16), shape((rows, D), F32), shape((rows, D), BF16), shape((rows, JPAD), BF16),
            shape((HEADS, rows, VPAD), BF16), shape((HEADS, 1, JPAD), F32), shape((n, JPAD, width), BF16), shape((rows, 4 * VPAD), BF16),
            shape((1, 4 * VPAD), F32), shape((4 * VPAD, D), BF16), shape((HEADS, rd), F32), shape((JPAD, rd), BF16), shape((rd, D), BF16), shape((JPAD, rd), F32),
        ),
        scratch_shapes=[
            low(D, D), low(D, D), low(D, D), low(D, 3 * width), dma((8,)), edge, edge, dma, dma,
            low(n, rows, 4 * VPAD), dma((n, 2)), dma((n, 2)),
            low(items, n, here, D), low(items, n, here, width), low(n, items, here, width),
            dma((n, 2 * items)), dma((n, 2 * items)), dma((items, n)), dma((items, n)), dma((2 * items + 9,)),
            low(items, seq, 3 * width), pltpu.VMEM((rows, D), F32), low(rows, D), low(rows, JPAD), low(HEADS, rows, VPAD),
            low(n, JPAD, width), low(4 * VPAD, D),
        ],
        compiler_params=pltpu.CompilerParams(collective_id=1, has_side_effects=True, vmem_limit_bytes=60 * MIB),
        name="front",
    )(fields, cot, ids, mask, patching, tagging, reading, beacon, lifting, offset, scaling, centre, biasing, place, keying, valuing, merging, proj)


def middle_kernel(
    n, items, here, heads, block,
    att_ref, emb_ref, mix_hbm, nudging_ref, rescaling_ref, recentre_ref, settle_ref, uplift_ref, baseline_ref, w1_hbm, w2_hbm, read_ref, dpred_ref,
    z_ref, sq_out, dmid_ref, do_ref, vecg_ref, uplg_ref, rows_out,
    w1, w2, mix, rows_ref, normal_ref, acc, slope_ref, upl_ref, sq_ref, gsend, grecv, load, keep,
):
    li = lax.axis_index("lon")
    rows = items * here
    width = heads * HDIM
    blocks = FF // block

    def fetch1(b):
        return pltpu.make_async_copy(w1_hbm.at[:, pl.ds(pl.multiple_of(b * block, block), block)], w1.at[b], load.at[b])

    def fetch2(b):
        return pltpu.make_async_copy(w2_hbm.at[pl.ds(pl.multiple_of(b * block, block), block)], w2.at[b], load.at[blocks + b])

    fetch_mix = pltpu.make_async_copy(mix_hbm, mix, load.at[2 * blocks])
    fetch_mix.start()
    for b in range(blocks):
        fetch1(b).start()
        fetch2(b).start()
    barrier_all(n, li)

    row = lambda ref: ref[...].reshape(1, -1).astype(F32)
    nudging, rescaling, recentre, settle = (row(a) for a in (nudging_ref, rescaling_ref, recentre_ref, settle_ref))
    uplift = row(uplift_ref)
    for b in range(blocks):
        upl_ref[b] = uplift[:, b * block : (b + 1) * block]
    quarter = rows // 4
    keeps = Moves(keep)
    every = list(range(4))
    gather = Gather(n, li, lambda slot, piece: rows_ref.at[slot, pl.ds(piece * quarter, quarter)], gsend, grecv)
    fetch_mix.wait()
    mid = emb_ref[...] + (product(att_ref[...], mix[...]) + nudging)
    dmid_ref[...] = mid
    normal, inverse = normalize(mid)
    normal_ref[...] = normal
    rows_ref[0] = (normal * rescaling + recentre).astype(BF16)
    gather.start(every)
    acc[...] = jnp.zeros_like(acc)

    def ahead(b, _):
        fetch1(b).wait()
        hidden = product(rows_ref[0], w1[b]) + upl_ref[b]
        value, slope = gelu_parts(hidden)
        slope_ref[b] = slope
        fetch2(b).wait()
        acc[...] += product(value.astype(BF16), w2[b])
        return 0

    lax.fori_loop(0, blocks, ahead, 0)
    final = (dmid_ref[...] + (acc[...] + settle)).astype(BF16)
    baseline = jnp.broadcast_to(baseline_ref[...].reshape(1, -1), (8, 4 * NOUT))
    baseline = product(baseline, places(4 * NOUT, 4 * VPAD, 0, 4, 2))[:1]
    z_ref[...] = (contract(final, read_ref[...], ((1,), (1,))) + baseline).astype(BF16)
    dpred = dpred_ref[...]
    sq_ref[:, D:] = contract(final, dpred, ((0,), (0,))).astype(BF16)
    keeps.go(sq_ref.at[:, pl.ds(D, 4 * VPAD)], sq_out.at[:, pl.ds(D, 4 * VPAD)])
    dfinal = product(dpred, read_ref[...])
    dfinal_low = dfinal.astype(BF16)
    acc[...] = jnp.zeros_like(acc)

    def back(b, _):
        dhidden = (contract(dfinal_low, w2[b], ((1,), (1,))) * slope_ref[b]).astype(BF16)
        uplg_ref[b] = jnp.sum(dhidden.astype(F32), axis=0, keepdims=True)
        acc[...] += contract(dhidden, w1[b], ((1,), (1,)))
        return 0

    gather.relay(every[:2], rest=False)
    lax.fori_loop(0, blocks // 2, back, 0)
    gather.relay(every[2:], rest=False)
    lax.fori_loop(blocks // 2, blocks, back, 0)
    gather.relay(every, first=False)
    for mask in range(0, n, 2):
        keeps.go(rows_ref.at[mask], rows_out.at[mask])
    dsecond = acc[...]
    normal = normal_ref[...]
    dmid = dfinal + norm_back(dsecond, normal, inverse, rescaling)
    dmid_ref[...] = dmid
    dmid_low = dmid.astype(BF16)
    vecg_ref[...] = jnp.concatenate([
        jnp.sum(dmid_low.astype(F32), axis=0, keepdims=True),
        jnp.sum(dsecond * normal, axis=0, keepdims=True),
        jnp.sum(dsecond, axis=0, keepdims=True),
        jnp.sum(dfinal_low.astype(F32), axis=0, keepdims=True),
    ], axis=0)
    dout = contract(dmid_low, mix[...], ((1,), (1,))).astype(BF16)
    for g in range(n):
        do_ref[g] = dout[:, g * width : (g + 1) * width].reshape(items, here, width)
    sq_ref[:, :D] = contract(att_ref[...], dmid_low, ((0,), (0,))).astype(BF16)
    keeps.go(sq_ref.at[:, pl.ds(0, D)], sq_out.at[:, pl.ds(0, D)])
    for mask in range(1, n, 2):
        for piece in every:
            gather.copy(mask, piece).wait_recv()
        keeps.go(rows_ref.at[mask], rows_out.at[mask])
    gather.drain(every)
    for c in keeps.started:
        c.wait()


def middle_part(att, emb, mixing, nudging, rescaling, recentre, settle, uplift, baseline, widening, narrowing, read, dpred, n, items, here, heads):
    rows = items * here
    width = heads * HDIM
    block = 512
    blocks = FF // block
    vm = pl.BlockSpec(memory_space=pltpu.VMEM)
    hbm = pl.BlockSpec(memory_space=pl.ANY)
    shape = jax.ShapeDtypeStruct
    return pl.pallas_call(
        functools.partial(middle_kernel, n, items, here, heads, block),
        in_specs=[vm, vm, hbm, vm, vm, vm, vm, vm, vm, hbm, hbm, vm, vm],
        out_specs=(vm, hbm, vm, vm, vm, vm, hbm),
        out_shape=(
            shape((rows, 4 * VPAD), BF16), shape((D, D + 4 * VPAD), BF16), shape((rows, D), F32),
            shape((n, items, here, width), BF16), shape((4, D), F32), shape((blocks, 1, block), F32), shape((n, rows, D), BF16),
        ),
        scratch_shapes=[
            pltpu.VMEM((blocks, D, block), BF16), pltpu.VMEM((blocks, block, D), BF16), pltpu.VMEM((D, D), BF16),
            pltpu.VMEM((n, rows, D), BF16), pltpu.VMEM((rows, D), F32), pltpu.VMEM((rows, D), F32),
            pltpu.VMEM((blocks, rows, block), F32), pltpu.VMEM((blocks, 1, block), F32), pltpu.VMEM((D, D + 4 * VPAD), BF16),
            pltpu.SemaphoreType.DMA((n, 4)), pltpu.SemaphoreType.DMA((n, 4)),
            pltpu.SemaphoreType.DMA((2 * blocks + 1,)), pltpu.SemaphoreType.DMA((n + 2,)),
        ],
        compiler_params=pltpu.CompilerParams(collective_id=2, has_side_effects=True, vmem_limit_bytes=60 * MIB),
        name="middle",
    )(att, emb, mixing, nudging, rescaling, recentre, settle, uplift, baseline, widening, narrowing, read, dpred)


def greet(n, li, count, zi):
    sem = pltpu.get_barrier_semaphore()
    for mask in range(1, n):
        pl.semaphore_signal(sem, inc=1, device_id={"lon": li ^ mask}, device_id_type=MESH)
    for mask in range(1, count):
        pl.semaphore_signal(sem, inc=1, device_id={"batch": zi ^ mask}, device_id_type=MESH)
    pl.semaphore_wait(sem, n + count - 2)


class Halving:
    def __init__(self, count, zi, flip, own, stage, land, send, recv):
        self.count, self.zi, self.own, self.stage, self.land = count, zi, own, stage, land
        self.send_sem, self.recv_sem = send, recv
        self.bits = [1 << i for i in range(count.bit_length() - 1)]
        if flip:
            self.bits = self.bits[::-1]

    def at_step(self, step):
        return [r for r in range(1, self.count) if min(i for i, b in enumerate(self.bits) if b & r) == step]

    def copy(self, r, step):
        return pltpu.make_async_remote_copy(
            src_ref=self.own(self.zi ^ r) if step == 0 else self.stage.at[r],
            dst_ref=self.land.at[r],
            send_sem=self.send_sem.at[r],
            recv_sem=self.recv_sem.at[r],
            device_id={"batch": self.zi ^ self.bits[step]},
            device_id_type=MESH,
        )

    def send(self, step):
        for r in self.at_step(step):
            self.copy(r, step).start()

    def absorb(self, step):
        for r in self.at_step(step):
            self.copy(r, step).wait_recv()
            to = r ^ self.bits[step]
            base = self.own(self.zi ^ to)[...] if step == 0 else self.stage[to]
            total = base.astype(F32) + self.land[r].astype(F32)
            if step == len(self.bits) - 1:
                return total
            self.stage[to] = total.astype(BF16)

    def drain(self):
        for step in range(len(self.bits)):
            for r in self.at_step(step):
                self.copy(r, step).wait_send()


class RowSum:
    def __init__(self, n, li, count, zi, own, land1, stage1, land2, stage2, land3, sems):
        self.n, self.li, self.count, self.zi, self.own = n, li, count, zi, own
        self.land1, self.stage1, self.land2, self.stage2, self.land3 = land1, stage1, land2, stage2, land3
        self.s1, self.r1, self.s2, self.r2, self.s3, self.r3 = sems
        self.half = n // 2

    @staticmethod
    def scratch(n, count, rows, cols):
        half = pltpu.VMEM((n // 2, count, rows, cols), BF16)
        one = pltpu.VMEM((count, rows, cols), BF16)
        lon_sem, z_sem = pltpu.SemaphoreType.DMA((n // 2,)), pltpu.SemaphoreType.DMA((count,))
        return [half, half, half, one, one, lon_sem, lon_sem, lon_sem, lon_sem, z_sem, z_sem]

    def copy1(self, j):
        return pltpu.make_async_remote_copy(
            src_ref=self.own(self.li ^ (2 * j + 1)), dst_ref=self.land1.at[j], send_sem=self.s1.at[j],
            recv_sem=self.r1.at[j], device_id={"lon": self.li ^ 1}, device_id_type=MESH,
        )

    def copy2(self, j):
        return pltpu.make_async_remote_copy(
            src_ref=self.stage1.at[j], dst_ref=self.land2.at[j], send_sem=self.s2.at[j],
            recv_sem=self.r2.at[j], device_id={"lon": self.li ^ (2 * j)}, device_id_type=MESH,
        )

    def copy3(self, r):
        return pltpu.make_async_remote_copy(
            src_ref=self.stage2.at[self.zi ^ r], dst_ref=self.land3.at[r], send_sem=self.s3.at[r],
            recv_sem=self.r3.at[r], device_id={"batch": self.zi ^ r}, device_id_type=MESH,
        )

    def core(self):
        for j in range(self.half):
            self.copy1(j).start()

    def plane(self):
        for j in list(range(1, self.half)) + [0]:
            self.copy1(j).wait_recv()
            self.stage1[j] = (self.own(self.li ^ (2 * j))[...].astype(F32) + self.land1[j].astype(F32)).astype(BF16)
            if j:
                self.copy2(j).start()

    def depth(self):
        total = self.stage1[0].astype(F32)
        for j in range(1, self.half):
            self.copy2(j).wait_recv()
            total = total + self.land2[j].astype(F32)
        self.stage2[...] = total.astype(BF16)
        for r in range(1, self.count):
            self.copy3(r).start()

    def total(self):
        total = self.stage2[self.zi].astype(F32)
        for r in range(1, self.count):
            self.copy3(r).wait_recv()
            total = total + self.land3[r].astype(F32)
        return total

    def drain(self):
        for j in range(self.half):
            self.copy1(j).wait_send()
            if j:
                self.copy2(j).wait_send()
        for r in range(1, self.count):
            self.copy3(r).wait_send()


KEPT = 5 * NVAR


def arrows(count):
    unit = 16 * count
    return -(-(KEPT + 24) // unit) * unit


def rear_kernel(
    n, count, items, here, heads, direct,
    do_ref, sq_ref, second_hbm, up_hbm, wown_hbm, nown_hbm, uplift_ref, read_ref, qkv_hbm, lse_ref, rows_hbm,
    proj_hbm, merge_hbm, emb_hbm, dmid_hbm, pooled_hbm, scaling_ref, patches_hbm, w_hbm, qrow_ref, pv_hbm, vecg_ref, uplg_ref, base_ref,
    ids_ref, z_hbm,
    nar_ref, sqo_ref, pos_ref, mer_ref, pred_ref, grad_ref, ar_ref, wcol_ref, pcol_ref,
    dpatch_ref, zsend, gsend, zland, gland, seams, wown, nown, bufa, bufb, dz, accn, accw, narg, widg, do_land, ebuf, eland, dk_acc, dv_acc, projg,
    mbuf, du3, arbuf, arland, arz, archunk, posbuf, posland, posall, wcolbuf, pcolbuf, upl, upall,
    qkv_ref, emb_ref, dmid_ref, pooled_ref, patches_ref, w_ref, pv_ref, z_ref,
    load, osend, orecv, esend, erecv, nstage, nland, nsend, nrecv, wstage, wland, wsend, wrecv, xstage, xland, xsend, xrecv,
    pstage, pland, psend, precv, qstage, qland, qsend, qrecv,
    asend, arecv, azs, azr, ags, agr, bgs, bgr, pss, psr, pgs, pgr, ws, wr, cs, cr, *sums,
):
    li, zi = lax.axis_index("lon"), lax.axis_index("batch")
    rows = items * here
    width = heads * HDIM
    seq = n * here
    rd = D // (n * count)
    hid = FF // (n * count)
    tile = 512 if seq <= 1024 else 256
    total = lambda a: jnp.sum(a, axis=0, keepdims=True)

    loads = Moves(load)
    starts = [pl.multiple_of((c * n + li) * hid, hid) for c in range(count)]
    fetch_own = [loads.go(nown_hbm.at[pl.ds(at, hid)], nown.at[pl.ds(c * hid, hid)]) for c, at in enumerate(starts)]
    if direct:
        fetch_own += [loads.go(wown_hbm.at[:, pl.ds(at, hid)], wown.at[:, c * hid : (c + 1) * hid]) for c, at in enumerate(starts)]
    else:
        fetch_own.append(loads.go(wown_hbm, wown))
    fetch_own.append(loads.go(up_hbm, dz))
    fetch_rows = [loads.go(second_hbm.at[m], bufa.at[m]) for m in range(n)]
    fetch_z = loads.go(z_hbm, z_ref)
    fetch_qkv = loads.go(qkv_hbm, qkv_ref)
    per = D // rows
    roomy = n <= 2 * per
    buf_rows, buf_proj = (bufb, bufa) if roomy else (bufa, bufb)

    def fetch_normed():
        return [loads.go(rows_hbm.at[i], buf_rows.at[pl.ds(0, n), pl.ds(i * here, here)]) for i in range(items)]

    def fetch_square(hbm, first, buf, at):
        return [loads.go(hbm.at[pl.ds(j * rows, rows), first : first + D], buf.at[at + j]) for j in range(per)]

    def fetch_joint():
        return fetch_square(proj_hbm, 0, buf_proj, 0) + fetch_square(proj_hbm, D, buf_proj, per)

    fetch_early = fetch_normed() if roomy else fetch_joint()
    fetch_late = [
        loads.go(h, v)
        for h, v in ((emb_hbm, emb_ref), (dmid_hbm, dmid_ref), (pooled_hbm, pooled_ref), (patches_hbm, patches_ref), (w_hbm, w_ref), (pv_hbm, pv_ref))
    ]
    greet(n, li, count, zi)
    nar = Halving(count, zi, False, lambda b: narg.at[b], nstage, nland, nsend, nrecv)
    cut = count // 2
    wide_a = Halving(count, zi, False, lambda b: widg.at[b, pl.ds(0, cut)], wstage, wland, wsend, wrecv)
    wide_b = Halving(count, zi, True, lambda b: widg.at[b, pl.ds(cut, cut)], xstage, xland, xsend, xrecv)
    squares = RowSum(n, li, count, zi, lambda l: sq_ref.at[:, l], *sums[:5], sums[10:16])
    merging = RowSum(n, li, count, zi, lambda l: mbuf.at[:, l], *sums[5:10], sums[16:22])
    hz = D // count // 2
    first = Halving(count, zi, False, lambda b: projg.at[pl.ds(b * 2 * hz, hz)], pstage, pland, psend, precv)
    second = Halving(count, zi, True, lambda b: projg.at[pl.ds(b * 2 * hz + hz, hz)], qstage, qland, qsend, qrecv)
    steps = len(nar.bits)

    def onward(*sums):
        for step in range(steps - 1):
            for one in sums:
                one.absorb(step)
                one.send(step + 1)

    def give_do(mask):
        return pltpu.make_async_remote_copy(
            src_ref=do_ref.at[li ^ mask], dst_ref=do_land.at[mask], send_sem=osend.at[mask], recv_sem=orecv.at[mask],
            device_id={"lon": li ^ mask}, device_id_type=MESH,
        )

    for mask in range(1, n):
        give_do(mask).start()
    do_land[0] = do_ref[li]
    squares.core()

    for c in fetch_own:
        c.wait()
    slopes = contract(nown[...], read_ref[...], ((1,), (1,))).astype(BF16)
    uplift = uplift_ref[...].reshape(1, FF).astype(F32)
    for j in range(n * count):
        upall[j] = uplift[:, j * hid : (j + 1) * hid]
    upl[...] = jnp.concatenate([upall[c * n + li] for c in range(count)], axis=1)
    for c in fetch_rows:
        c.wait()
    group_of = D // rows
    half = count * hid // 2

    def own_units(part):
        cols = slice(part * half, (part + 1) * half)
        accn[...] = jnp.zeros_like(accn)
        accw[...] = jnp.zeros_like(accw)

        def own(m, _):
            take = pl.ds(m * group_of, group_of)
            normed, upstream = bufa[take].reshape(D, D), dz[take].reshape(D, 4 * VPAD)
            value, slope = gelu_parts(product(normed, wown[:, cols]) + upl[:, cols])
            dhidden = (contract(upstream, slopes[cols], ((1,), (1,))) * slope).astype(BF16)
            accn[...] += contract(value.astype(BF16), upstream, ((0,), (0,)))
            accw[...] += contract(dhidden, normed, ((0,), (0,)))
            return 0

        lax.fori_loop(0, n // group_of, own, 0)
        for j in range(cut):
            narg[part * cut + j] = accn[j * hid : (j + 1) * hid, :].astype(BF16)
            for b in range(count):
                widg[b, part * cut + j] = accw[j * hid : (j + 1) * hid, b * (D // count) : (b + 1) * (D // count)].astype(BF16)

    squares.plane()
    own_units(0)
    wide_a.send(0)

    def give(i, mask):
        return pltpu.make_async_remote_copy(
            src_ref=ebuf.at[i, mask], dst_ref=eland.at[li, i], send_sem=esend.at[i, mask], recv_sem=erecv.at[i, mask],
            device_id={"lon": li ^ mask}, device_id_type=MESH,
        )

    fetch_qkv.wait()
    for mask in range(1, n):
        give_do(mask).wait_recv()
    for i in range(items):
        dk_acc[...] = jnp.zeros_like(dk_acc)
        dv_acc[...] = jnp.zeros_like(dv_acc)
        for t in range(seq // tile):
            part = slice(t * tile, (t + 1) * tile)
            outs = []
            do_rows = do_land[t * (tile // here) : (t + 1) * (tile // here), i].reshape(tile, width)
            for h in range(heads):
                cols = slice(h * HDIM, (h + 1) * HDIM)
                q = qkv_ref[i, part, h * HDIM : (h + 1) * HDIM] * FACTOR
                k = qkv_ref[i, :, width + h * HDIM : width + (h + 1) * HDIM]
                v = qkv_ref[i, :, 2 * width + h * HDIM : 2 * width + (h + 1) * HDIM]
                do = do_rows[:, cols]
                probs = jnp.exp(contract(q, k, ((1,), (1,))) - jnp.transpose(lse_ref[i, h : h + 1, part]))
                dprobs = contract(do, v, ((1,), (1,)))
                delta = jnp.sum(probs * dprobs, axis=1, keepdims=True)
                dscores = (probs * (dprobs - delta)).astype(BF16)
                dv_acc[h] += contract(do, probs.astype(BF16), ((0,), (0,)))
                dk_acc[h] += contract(q, dscores, ((0,), (0,)))
                outs.append(product(dscores, k) * FACTOR)
            out = jnp.concatenate(outs, axis=1) if heads > 1 else outs[0]
            ebuf[i, t * (tile // here) : (t + 1) * (tile // here), :, :width] = out.astype(BF16).reshape(tile // here, here, width)
        for h in range(heads):
            ebuf[i, :, :, width + h * HDIM : width + (h + 1) * HDIM] = jnp.transpose(dk_acc[h]).astype(BF16).reshape(n, here, HDIM)
            ebuf[i, :, :, 2 * width + h * HDIM : 2 * width + (h + 1) * HDIM] = jnp.transpose(dv_acc[h]).astype(BF16).reshape(n, here, HDIM)
        for mask in range(1, n):
            give(i, mask).start()
        eland[li, i] = ebuf[i, 0]
        if i == 0:
            onward(wide_a)
    squares.depth()
    own_units(1)
    wide_b.send(0)
    nar.send(0)
    fetch_next = fetch_joint() if roomy else fetch_normed()
    for c in fetch_early if roomy else fetch_next:
        c.wait()
    joint = jnp.zeros((D, 3 * width), F32)
    for i in range(items):
        joint = joint + contract(buf_rows[:n, i * here : (i + 1) * here].reshape(seq, D), ebuf[i].reshape(seq, 3 * width), ((0,), (0,)))
    projg[...] = joint.astype(BF16)
    fetch_third = fetch_square(proj_hbm, 2 * D, buf_rows, 0)
    fetch_m = fetch_square(merge_hbm, 0, buf_rows, per)
    first.send(0)
    second.send(0)
    for c in (fetch_next if roomy else fetch_early) + fetch_late:
        c.wait()

    normal, inverse = normalize(emb_ref[...])
    lat = 2 * LATP
    wide = pred_ref.shape[2]
    spread = latitudes(lat)

    def seam(j, src, dst):
        return pltpu.make_async_remote_copy(
            src_ref=src, dst_ref=dst, send_sem=seams.at[2 * j], recv_sem=seams.at[2 * j + 1],
            device_id={"lon": lax.rem(li + n - 1, n)}, device_id_type=MESH,
        )

    def stacked(ref, i, w):
        at = i * here + (w // 2) * LATP
        corner = (w % 2) * 2
        return jnp.concatenate([ref[at : at + LATP, (corner + e) * VPAD : (corner + e + 1) * VPAD] for e in range(2)], axis=0)

    fetch_z.wait()
    for i in range(items):
        for w in range(wide // lat):
            pixels = contract(stacked(z_ref, i, w), spread, ((0,), (0,)))[:NOUT].astype(BF16)
            if w == 0:
                zsend[i] = pixels
            else:
                pred_ref[i, :, (w - 1) * lat : w * lat] = pixels
    west_z = seam(0, zsend, zland)
    west_z.start()

    for i in range(items):
        for mask in range(1, n):
            give(i, mask).wait_recv()
    scaling = scaling_ref[...].reshape(1, -1).astype(F32)
    dnormed = jnp.zeros((rows, D), F32)
    e3_sums = []
    for p, buf, at in ((0, buf_proj, 0), (1, buf_proj, per), (2, buf_rows, 0)):
        if p == 2:
            for c in fetch_third:
                c.wait()
        e3 = jnp.concatenate(
            [eland[g, :, :, p * width : (p + 1) * width].reshape(rows, width) for g in range(n)], axis=1
        )
        e3_sums.append(total(e3.astype(F32)))
        dnormed = dnormed + contract(e3, buf[at : at + per].reshape(D, D), ((1,), (1,)))
    demb = dmid_ref[...] + norm_back(dnormed, normal, inverse, scaling)
    demb_low = demb.astype(BF16)
    summed = demb[:here]
    for i in range(1, items):
        summed = summed + demb[i * here : (i + 1) * here]
    posbuf[...] = summed.astype(BF16).reshape(count, here // count, D)

    def pos_give(r):
        return pltpu.make_async_remote_copy(
            src_ref=posbuf.at[zi ^ r], dst_ref=posland.at[r], send_sem=pss.at[r], recv_sem=psr.at[r],
            device_id={"batch": zi ^ r}, device_id_type=MESH,
        )

    def pos_share(r):
        return pltpu.make_async_remote_copy(
            src_ref=posall.at[zi], dst_ref=posall.at[zi], send_sem=pgs.at[r], recv_sem=pgr.at[r],
            device_id={"batch": zi ^ r}, device_id_type=MESH,
        )

    for r in range(1, count):
        pos_give(r).start()
    mbuf[...] = contract(pooled_ref[...], demb_low, ((0,), (0,))).astype(BF16).reshape(mbuf.shape)
    merging.core()
    for c in fetch_m:
        c.wait()
    dpooled = contract(demb_low, buf_rows[per : 2 * per].reshape(D, D), ((1,), (1,))).astype(BF16)
    vectors = jnp.concatenate([
        total(dpooled.astype(F32)), total(demb_low.astype(F32)), total(dnormed * normal), total(dnormed), e3_sums[0], e3_sums[2], vecg_ref[...],
    ] + [jnp.concatenate([uplg_ref[2 * j], uplg_ref[2 * j + 1]], axis=1) for j in range(FF // D)] + [
        jnp.concatenate([base_ref[...], jnp.zeros((1, D - 4 * VPAD), F32)], axis=1), jnp.zeros((1, D), F32),
    ], axis=0).astype(BF16)
    for g in range(n):
        du3[g] = dpooled[:, g * width : (g + 1) * width]
        arbuf[g, KEPT : KEPT + 16] = vectors[:, g * width : (g + 1) * width]
    merging.plane()
    patches = patches_ref[...].astype(F32)
    dpatch_ref[...] = jnp.zeros_like(dpatch_ref)
    lines = -(-JPAD // width)

    def pool_core(mask):
        return pltpu.make_async_remote_copy(
            src_ref=arbuf.at[li ^ mask ^ 1], dst_ref=arland.at[mask], send_sem=asend.at[mask ^ 1], recv_sem=arecv.at[mask],
            device_id={"lon": li ^ 1}, device_id_type=MESH,
        )

    def pool_give(mask):
        return pltpu.make_async_remote_copy(
            src_ref=arbuf.at[li ^ mask], dst_ref=arland.at[mask ^ 1], send_sem=asend.at[mask], recv_sem=arecv.at[mask ^ 1],
            device_id={"lon": li ^ mask}, device_id_type=MESH,
        )

    def group(mask):
        g = li ^ mask
        halves, extra = [], []
        patch_total = jnp.zeros((rows, 4 * VPAD), F32)
        du_all, pv_all = du3[g], pv_ref[g]
        for s in range(heads):
            h = g * heads + s
            w = w_ref[h].astype(F32)
            wide = jnp.concatenate([w] * 5, axis=1)
            blended = (wide * patches).astype(BF16)
            du = du_all[:, s * HDIM : (s + 1) * HDIM]
            dbl = contract(du, pv_all[:, s * HDIM : (s + 1) * HDIM], ((1,), (1,)))
            halves.append(jnp.transpose(contract(du, blended, ((0,), (0,)))))
            x = dbl * patches
            dw = x[:, :VPAD]
            for c in range(1, 5):
                dw = dw + x[:, c * VPAD : (c + 1) * VPAD]
            da = w * (dw - jnp.sum(w * dw, axis=-1, keepdims=True)) * FACTOR
            da_wide = jnp.concatenate([da] * 5, axis=1)
            line = total(da_wide * patches)
            line = jnp.concatenate([line, jnp.zeros((1, lines * width - JPAD), F32)], axis=1) if lines * width > JPAD else line
            extra += [line[:, c * width : (c + 1) * width] for c in range(lines)]
            patch_total = patch_total + (wide[:, : 4 * VPAD] * dbl[:, : 4 * VPAD] + da_wide[:, : 4 * VPAD] * qrow_ref[h][:, : 4 * VPAD])
        dpatch_ref[...] += patch_total
        both = (jnp.concatenate(halves, axis=1) if heads > 1 else halves[0]).astype(BF16)
        arbuf[g, :KEPT] = jnp.concatenate([both[c * VPAD : c * VPAD + NVAR] for c in range(5)], axis=0)
        tail = jnp.concatenate(extra + [jnp.zeros((arrows(count) - KEPT - 16 - heads * lines, width), F32)], axis=0)
        arbuf[g, KEPT + 16 :] = tail.astype(BF16)

    evens = list(range(2, n, 2)) + [0]
    for mask in evens:
        group(mask ^ 1)
        pool_core(mask).start()
    onward(wide_b, nar)
    for mask in evens:
        group(mask)
        pool_core(mask).wait_recv()
        if mask:
            g = li ^ mask
            arbuf[g] = (arbuf[g].astype(F32) + arland[mask].astype(F32)).astype(BF16)
            pool_give(mask).start()
    def wide_give(mask):
        return pltpu.make_async_remote_copy(
            src_ref=wcolbuf.at[li ^ mask], dst_ref=wcol_ref.at[li], send_sem=ws.at[mask], recv_sem=wr.at[mask],
            device_id={"lon": li ^ mask}, device_id_type=MESH,
        )

    def col_give(mask):
        return pltpu.make_async_remote_copy(
            src_ref=pcolbuf.at[li ^ mask], dst_ref=pcol_ref.at[li], send_sem=cs.at[mask], recv_sem=cr.at[mask],
            device_id={"lon": li ^ mask}, device_id_type=MESH,
        )

    chunk = arbuf[li].astype(F32) + arland[0].astype(F32)
    for mask in range(2, n, 2):
        pool_give(mask).wait_recv()
        chunk = chunk + arland[mask ^ 1].astype(F32)
    piece = arrows(count) // count
    archunk[...] = chunk.astype(BF16).reshape(archunk.shape)

    def z_give(r):
        return pltpu.make_async_remote_copy(
            src_ref=archunk.at[zi ^ r], dst_ref=arz.at[r], send_sem=azs.at[r], recv_sem=azr.at[r],
            device_id={"batch": zi ^ r}, device_id_type=MESH,
        )

    def z_share(r):
        return pltpu.make_async_remote_copy(
            src_ref=ar_ref.at[li, zi], dst_ref=ar_ref.at[li, zi], send_sem=ags.at[r], recv_sem=agr.at[r],
            device_id={"batch": zi ^ r}, device_id_type=MESH,
        )

    for r in range(1, count):
        z_give(r).start()
    onward(first, second)
    pos_sum = posbuf[zi].astype(F32)
    for r in range(1, count):
        pos_give(r).wait_recv()
        pos_sum = pos_sum + posland[r].astype(F32)
    posall[zi] = pos_sum.astype(BF16)
    piece_sum = archunk[zi].astype(F32)
    for r in range(1, count):
        z_give(r).wait_recv()
        piece_sum = piece_sum + arz[r].astype(F32)
    ar_ref[li, zi] = piece_sum.astype(BF16)

    def l_share(mask, r):
        return pltpu.make_async_remote_copy(
            src_ref=ar_ref.at[li, zi ^ r], dst_ref=ar_ref.at[li, zi ^ r], send_sem=bgs.at[mask, r], recv_sem=bgr.at[mask, r],
            device_id={"lon": li ^ mask}, device_id_type=MESH,
        )

    def l_relay(mask, r):
        return pltpu.make_async_remote_copy(
            src_ref=ar_ref.at[li ^ mask, zi ^ r], dst_ref=ar_ref.at[li ^ mask, zi ^ r], send_sem=bgs.at[mask | 1, r], recv_sem=bgr.at[mask | 1, r],
            device_id={"lon": li ^ 1}, device_id_type=MESH,
        )

    def spread_out(r):
        for mask in range(2, n, 2):
            l_share(mask, r).start()
        l_relay(0, r).start()

    for r in range(1, count):
        z_share(r).start()
    spread_out(0)
    for r in range(1, count):
        pos_share(r).start()
    nar_ref[...] = nar.absorb(steps - 1)
    for k, one in enumerate((wide_a, wide_b)):
        w_total = one.absorb(steps - 1)
        for c in range(cut):
            turned = jnp.transpose(w_total[c]).astype(BF16)
            for l in range(n):
                wcolbuf[l, k * cut + c] = turned[l * rd : (l + 1) * rd]
    for mask in range(1, n):
        wide_give(mask).start()
    wcol_ref[li] = wcolbuf[li]
    for r in range(1, count):
        z_share(r).wait_recv()
        spread_out(r)
    merging.depth()
    for i in range(items):
        var = lax.broadcasted_iota(jnp.int32, (VPAD, NVAR), 0)
        choose = (var == ids_ref[i : i + 1, :]).astype(BF16)
        for w in range(wide // lat):
            parts = pieces(stacked(dpatch_ref, i, w), 2)
            pixels = contract(parts[:lat], spread, ((0,), (0,))) + contract(parts[lat:], spread, ((0,), (0,)))
            parts = pieces(pixels, 2)
            slots = contract(choose, parts[:VPAD], ((0,), (0,))) + contract(choose, parts[VPAD:], ((0,), (0,)))
            if w == 0:
                gsend[i] = slots
            else:
                grad_ref[i, :, (w - 1) * lat : w * lat] = slots
    west_g = seam(1, gsend, gland)
    west_g.start()
    west_z.wait()
    pred_ref[:, :, wide - lat :] = zland[...]

    sqo_ref[...] = squares.total()
    top, low = first.absorb(steps - 1).astype(BF16), second.absorb(steps - 1).astype(BF16)
    pcolbuf[...] = jnp.concatenate([top, low], axis=0).reshape(pcolbuf.shape)
    for mask in range(1, n):
        col_give(mask).start()
    pcol_ref[li] = pcolbuf[li]
    for r in range(count):
        for mask in range(2, n, 2):
            l_share(mask, r).wait_recv()
            l_relay(mask, r).start()
    for r in range(1, count):
        pos_share(r).wait_recv()
    pos_ref[...] = posall[...].reshape(here, D).astype(F32)
    mer_ref[...] = merging.total()
    for r in range(count):
        for mask in range(0, n, 2):
            l_relay(mask, r).wait_recv()
    for mask in range(1, n):
        col_give(mask).wait()
        wide_give(mask).wait()
        give_do(mask).wait_send()
        for i in range(items):
            give(i, mask).wait_send()
    for mask in range(0, n, 2):
        pool_core(mask).wait_send()
        if mask:
            pool_give(mask).wait_send()
        for r in range(count):
            l_relay(mask, r).wait_send()
            if mask:
                l_share(mask, r).wait_send()
    for r in range(1, count):
        z_give(r).wait_send()
        z_share(r).wait_send()
        pos_give(r).wait_send()
        pos_share(r).wait_send()
    for part in (first, second, nar, wide_a, wide_b, squares, merging):
        part.drain()
    west_g.wait()
    grad_ref[:, :, wide - lat :] = gland[...]


def rear_part(
    do, squares, second, up, wown, nown, uplown, read, qkv, lse, rows_all, projecting, merging, emb, dmid, pooled, scaling, patches, pool_w, qrow, pv,
    vec_grads, uplift_grads, base, ids, z, direct, n, count, items, here, heads,
):
    rows, width, seq = items * here, heads * HDIM, n * here
    rd, hid = D // (n * count), FF // (n * count)
    own = count * hid
    wide = here // LATP * 2 * 2 * LATP
    shape = jax.ShapeDtypeStruct
    vm, hbm = pl.BlockSpec(memory_space=pltpu.VMEM), pl.BlockSpec(memory_space=pl.ANY)
    cols = squares.shape[3]
    piece = arrows(count) // count
    hz = D // count // 2
    dma = pltpu.SemaphoreType.DMA
    lsem, zsem, isem, psem = dma((n,)), dma((count,)), dma((items, n)), dma((n, count))
    low = lambda *s: pltpu.VMEM(s, BF16)
    full = lambda *s: pltpu.VMEM(s, F32)
    pos = low(count, here // count, D)
    nbuf, wbuf, pbuf = low(count, hid, 4 * VPAD), low(count, count // 2, hid, D // count), low(count, hz, 3 * width)
    one, two = RowSum.scratch(n, count, rd, cols), RowSum.scratch(n, count, rd, D)
    return pl.pallas_call(
        functools.partial(rear_kernel, n, count, items, here, heads, direct),
        in_specs=[vm, vm, hbm, hbm, hbm, hbm, vm, vm, hbm, vm, hbm, hbm, hbm, hbm, hbm, hbm, vm, hbm, hbm, vm, hbm, vm, vm, vm, vm, hbm],
        out_specs=(vm,) * 9,
        out_shape=(
            shape((hid, 4 * VPAD), F32), shape((rd, cols), F32), shape((here, D), F32), shape((rd, D), F32),
            shape((items, NOUT, wide), BF16), shape((items, NVAR, wide), F32), shape((n, count, piece, width), BF16), shape((n, count, rd, hid), BF16), shape((n, rd, 3 * width), BF16),
        ),
        scratch_shapes=[
            full(rows, 4 * VPAD), low(items, NOUT, 2 * LATP), full(items, NVAR, 2 * LATP), low(items, NOUT, 2 * LATP), full(items, NVAR, 2 * LATP), dma((4,)),
            low(D, own), low(own, D), low(n, rows, D), low(2 * D // rows, rows, D), low(n, rows, 4 * VPAD), full(own // 2, 4 * VPAD), full(own // 2, D),
            low(count, hid, 4 * VPAD), low(count, count, hid, D // count), low(n, items, here, width),
            low(items, n, here, 3 * width), low(n, items, here, 3 * width), full(heads, HDIM, seq), full(heads, HDIM, seq),
            low(D, 3 * width), low(count, n, rd, D), low(n, rows, width),
            low(n, arrows(count), width), low(n, arrows(count), width), low(count, piece, width), low(count, piece, width), pos, pos, pos,
            low(n, count, rd, hid), low(n, rd, 3 * width), full(1, own), full(n * count, 1, hid),
            low(items, seq, 3 * width), full(rows, D), full(rows, D), low(rows, D), low(rows, JPAD), low(HEADS, rows, VPAD), low(n, JPAD, width), low(rows, 4 * VPAD),
            dma((2 * count + n + items + 4 * (D // rows) + 9,)), lsem, lsem, isem, isem, nbuf, nbuf, zsem, zsem, wbuf, wbuf, zsem, zsem, wbuf, wbuf, zsem, zsem,
            pbuf, pbuf, zsem, zsem, pbuf, pbuf, zsem, zsem,
            lsem, lsem, zsem, zsem, zsem, zsem, psem, psem, zsem, zsem, zsem, zsem, lsem, lsem, lsem, lsem,
        ] + one[:5] + two[:5] + one[5:] + two[5:],
        compiler_params=pltpu.CompilerParams(collective_id=3, has_side_effects=True, vmem_limit_bytes=63 * MIB + 3 * MIB // 4),
        name="rear",
    )(do, squares, second, up, wown, nown, uplown, read, qkv, lse, rows_all, projecting, merging, emb, dmid, pooled, scaling, patches, pool_w, qrow, pv, vec_grads, uplift_grads, base, ids, z)


def finish_kernel(
    n, count, heads, sum_ref, wcol_ref, pcol_ref, nar_ref, sq_ref, mer_ref, pos_ref, pred_ref, grad_ref, read_ref, keymap_ref, embed_ref, val_ref, kk_ref, beacon_ref,
    prediction_ref, fields_ref, position_ref, patching_ref, tagging_ref, beacon_out, keying_ref, valuing_ref, lifting_ref, merging_ref, offset_ref, scaling_ref,
    centre_ref, projecting_ref, biasing_ref, mixing_ref, nudging_ref, rescaling_ref, recentre_ref, widening_ref, uplift_ref,
    narrowing_ref, settle_ref, reading_ref, baseline_ref,
):
    li, zi = lax.axis_index("lon"), lax.axis_index("batch")
    block = zi * n + li
    rd = D // (n * count)
    hid = FF // (n * count)
    width = heads * HDIM
    lines = -(-JPAD // width)
    exact = lambda a, b, dims: lax.dot_general(a, b, (dims, ((), ())), precision=HIGH, preferred_element_type=F32)

    def mine(size):
        row = lax.broadcasted_iota(jnp.int32, (D, size), 0)
        col = lax.broadcasted_iota(jnp.int32, (D, size), 1)
        return (row == ((block * size + col) & (D - 1))).astype(BF16)

    lat = 2 * LATP
    for i in range(pred_ref.shape[0]):
        for w in range(pred_ref.shape[2] // lat):
            prediction_ref[i, :, w, :] = pred_ref[i, :, w * lat : (w + 1) * lat]
            fields_ref[i, :, w, :] = grad_ref[i, :, w * lat : (w + 1) * lat]
    position_ref[...] = pos_ref[...]
    merging_ref[...] = mer_ref[...]
    mixing_ref[...] = sq_ref[:, :D]
    narrowing_ref[...] = folded(product(pieces(nar_ref[...], 2), read_ref[...]), 2)
    reading_ref[...] = exact(sq_ref[:, D:], places(4 * NOUT, 4 * VPAD, 0, 4, 2).astype(F32), ((1,), (1,)))
    for g in range(n):
        for p in range(3):
            projecting_ref[:, p * D + g * width : p * D + (g + 1) * width] = pcol_ref[g, :, p * width : (p + 1) * width].astype(F32)
        for c in range(count):
            at = (c * n + g) * hid
            widening_ref[:, at : at + hid] = wcol_ref[g, c].astype(F32)

    sums = [sum_ref[g].reshape(arrows(count), width) for g in range(n)]
    vectors = jnp.concatenate([a[KEPT : KEPT + 16] for a in sums], axis=1)
    one, two, four = mine(rd), mine(2 * rd), mine(4 * rd)
    short = product(vectors, one)
    for j, ref in ((0, lifting_ref), (1, offset_ref), (2, scaling_ref), (3, centre_ref), (6, nudging_ref), (7, rescaling_ref), (8, recentre_ref), (9, settle_ref)):
        ref[...] = short[j : j + 1].reshape(rd)

    def across(start, size, select, ref):
        found = product(vectors, select)
        row = (block * size) // D
        total = jnp.zeros((1, size), F32)
        for k in range(size // rd):
            total = total + jnp.where(row == k, found[start + k : start + k + 1], 0.0)
        ref[...] = total.reshape(size)

    across(4, 2 * rd, two, biasing_ref)
    across(10, 4 * rd, four, uplift_ref)
    baseline_ref[...] = contract(vectors[:, : 4 * VPAD], places(4 * NOUT, 4 * VPAD, 0, 4, 2), ((1,), (1,)))[14:15].reshape(4 * NOUT)

    dqz = []
    for h in range(HEADS):
        base = KEPT + 16 + (h % heads) * lines
        lined = sums[h // heads]
        dqz.append(jnp.concatenate([lined[base + c : base + c + 1].astype(F32) for c in range(lines)], axis=1)[:, :JPAD])
    dqz = jnp.concatenate(dqz, axis=0)
    embed_mine, val_mine = embed_ref[...], val_ref[...]
    dembed = exact(keymap_ref[...], dqz, ((0,), (0,)))
    for g in range(n):
        blank = jnp.zeros((VPAD - NVAR, width), BF16)
        dpv = jnp.concatenate([a for c in range(5) for a in (sums[g][c * NVAR : (c + 1) * NVAR], blank)], axis=0)
        valuing_ref[:, g * width : (g + 1) * width] = contract(embed_mine, dpv, ((0,), (0,)))
        dembed = dembed + contract(val_mine[:, g * width : (g + 1) * width], dpv, ((1,), (1,)))
    patching_ref[...] = exact(dembed, places(4 * NVAR, JPAD, 0, 4, 2).astype(F32), ((1,), (1,)))
    tagging_ref[...] = dembed[:, 4 * VPAD : 4 * VPAD + NVAR]
    dkeymap = product(dqz.astype(BF16), embed_mine)
    keying_ref[...] = exact(dkeymap, by_head(beacon_ref[...].reshape(1, -1).astype(F32)), ((0,), (0,)))
    down = exact(dqz, kk_ref[...], ((1,), (0,)))
    head = lax.broadcasted_iota(jnp.int32, (HEADS, rd), 0)
    col = block * rd + lax.broadcasted_iota(jnp.int32, (HEADS, rd), 1)
    beacon_out[...] = jnp.sum(jnp.where(col >> 6 == head, down, 0.0), axis=0, keepdims=True).reshape(rd)


def finish(summed, wcol, pcol, nar, squares, mer, pos, pred, grad, read, keymap, embed, valuing, kk, beacon, n, count, heads):
    rd, hid = D // (n * count), FF // (n * count)
    shape = lambda *s: jax.ShapeDtypeStruct(s, F32)
    vec = shape(rd)
    lat = 2 * LATP
    items, wide = pred.shape[0], pred.shape[2] // lat
    return pl.pallas_call(
        functools.partial(finish_kernel, n, count, heads),
        out_shape=(
            jax.ShapeDtypeStruct((items, NOUT, wide, lat), BF16), shape(items, NVAR, wide, lat),
            shape(*pos.shape), shape(rd, 4 * NVAR), shape(rd, NVAR), vec, shape(rd, D), shape(rd, D), vec, shape(rd, D), vec, vec, vec,
            shape(rd, 3 * D), shape(2 * rd), shape(rd, D), vec, vec, vec, shape(rd, FF), shape(4 * rd), shape(hid, D), vec,
            shape(rd, 4 * NOUT), shape(4 * NOUT),
        ),
        compiler_params=pltpu.CompilerParams(vmem_limit_bytes=60 * MIB),
        name="finish",
    )(summed, wcol, pcol, nar, squares, mer, pos, pred, grad, read, keymap, embed, valuing, kk, beacon)


def per_device(
    fields, variable_ids, variable_mask, position, patching, tagging, beacon, keying, valuing, lifting,
    merging, offset, scaling, centre, projecting, biasing, mixing, nudging, rescaling, recentre,
    widening, uplift, narrowing, settle, reading, baseline, cotangent,
):
    count, lon = lax.axis_size("batch"), lax.axis_size("lon")
    zi, li = lax.axis_index("batch"), lax.axis_index("lon")
    items, cols_dev, lat = fields.shape[0], fields.shape[2], fields.shape[3]
    upatch = cols_dev // 2
    here = upatch * LATP
    heads = HEADS // lon
    width = heads * HDIM
    rows_dev = D // (count * lon)
    hid = FF // (count * lon)
    f = lambda a: a.astype(F32)

    columns = lambda a, start, size: lax.dynamic_slice_in_dim(a, start, size, 1)
    direct_heads, direct_hidden = width % 128 == 0, hid % 128 == 0
    proj_own = projecting if direct_heads else jnp.concatenate([columns(projecting, p * D + li * width, width) for p in range(3)], axis=1)
    wide_own = widening if direct_hidden else jnp.concatenate([columns(widening, (c * lon + li) * hid, hid) for c in range(count)], axis=1)
    (
        attended, normed_all, joint, lse, dpred_all, embedded, pooled, patches, pool_w, qrow, pv, dpred, base, reading_p, keymap_mine, embed_mine, val_mine, kk_mine,
    ) = front(
        fields, cotangent, variable_ids, variable_mask, patching.T, tagging.T, reading.T, beacon, lifting, offset, scaling, centre, biasing,
        position.reshape(here, D), keying, valuing, merging, proj_own, rows_dev, direct_heads, lon, items, here, heads,
    )
    outputs, squares, dmiddle, do, vec_grads, uplift_grads, second_all = middle_part(
        attended, embedded, mixing, nudging, rescaling, recentre, settle, uplift, baseline, widening, narrowing, reading_p, dpred,
        lon, items, here, heads,
    )
    nar, squares, pos, mer, prediction, fields_gradient, summed, wide_cols, joint_cols = rear_part(
        do, squares.reshape(count, lon, rows_dev, -1), second_all, dpred_all, wide_own, narrowing, uplift, reading_p,
        joint, lse, normed_all, projecting, merging, embedded, dmiddle, pooled, scaling, patches, pool_w, qrow, pv, vec_grads, uplift_grads, base,
        variable_ids, outputs, direct_hidden, lon, count, items, here, heads,
    )
    outs = list(finish(
        summed, wide_cols, joint_cols, nar, squares, mer, pos, prediction, fields_gradient, reading_p, keymap_mine, embed_mine, val_mine, kk_mine, beacon,
        lon, count, heads,
    ))
    outs[2] = outs[2].reshape(upatch, LATP, D)
    return tuple(outs)


def solution(mesh):
    both = ("batch", "lon")
    image, matrix, vector = P("batch", None, "lon", None), P(both, None), P(both)
    return jax.shard_map(
        per_device,
        mesh=mesh,
        in_specs=(image, P("batch", None), P("batch", None), P("lon", None, None)) + (P(),) * 22 + (image,),
        out_specs=(
            image, image, P("lon", None, None), matrix, matrix, vector, matrix, matrix, vector, matrix, vector,
            vector, vector, matrix, vector, matrix, vector, vector, vector, matrix, vector, matrix, vector, matrix, P(),
        ),
        check_vma=False,
    )
```

```python
import functools

import jax
import jax.numpy as jnp
from jax import lax
from jax.experimental import pallas as pl
from jax.experimental.pallas import tpu as pltpu
from jax.sharding import PartitionSpec as P

D = 1024
HEADS = 16
HDIM = 64
FF = 4096
NVAR = 48
NOUT = 48
LATP = 32
VPAD = 64
JPAD = 5 * VPAD

HIGH = lax.Precision.HIGHEST
EPSILON = 1e-06
F32 = jnp.float32
BF16 = jnp.bfloat16
FACTOR = HDIM ** (-0.5)
MIB = 2**20
MESH = pl.DeviceIdType.MESH


def product(left, right):
    return jnp.dot(left, right, preferred_element_type=F32)


def contract(left, right, dims):
    return lax.dot_general(left, right, (dims, ((), ())), preferred_element_type=F32)


def normalize(values):
    centred = values - jnp.mean(values, axis=-1, keepdims=True)
    inverse = lax.rsqrt(jnp.mean(centred * centred, axis=-1, keepdims=True) + EPSILON)
    return centred * inverse, inverse


def norm_back(upstream, normal, inverse, scaler):
    weighted = upstream * scaler
    return inverse * (
        weighted
        - jnp.mean(weighted, axis=-1, keepdims=True)
        - normal * jnp.mean(weighted * normal, axis=-1, keepdims=True)
    )


def gelu_parts(x):
    c = 0.7978845608028654
    t = jnp.tanh(c * (x + 0.044715 * (x * x * x)))
    value = 0.5 * x * (1.0 + t)
    slope = 0.5 * (1.0 + t) + 0.5 * x * (1.0 - t * t) * (c * (1.0 + 3 * 0.044715 * x * x))
    return value, slope


def places(rows, cols, start, step, shift):
    row = lax.broadcasted_iota(jnp.int32, (rows, cols), 0)
    col = lax.broadcasted_iota(jnp.int32, (rows, cols), 1)
    return (start + (row & (step - 1)) * VPAD + (row >> shift) == col).astype(BF16)


def latitudes(lat):
    row = lax.broadcasted_iota(jnp.int32, (lat, lat), 0)
    col = lax.broadcasted_iota(jnp.int32, (lat, lat), 1)
    half = lat // 2
    return (2 * (row & (half - 1)) + (row >> (half.bit_length() - 1)) == col).astype(BF16)


def by_head(row):
    head = lax.broadcasted_iota(jnp.int32, (HEADS, D), 0)
    col = lax.broadcasted_iota(jnp.int32, (HEADS, D), 1)
    return jnp.where(col >> 6 == head, jnp.broadcast_to(row, (HEADS, D)), jnp.zeros((), row.dtype))


def pieces(a, count):
    parts = []
    for _ in range(count):
        parts.append(a.astype(BF16))
        a = a - parts[-1].astype(F32)
    return jnp.concatenate(parts, axis=0)


class Moves:
    def __init__(self, sem):
        self.sem, self.started = sem, []

    def go(self, src, dst):
        copy = pltpu.make_async_copy(src, dst, self.sem.at[len(self.started)])
        self.started.append(copy)
        copy.start()
        return copy


def folded(a, count):
    rows = a.shape[0] // count
    total = a[:rows]
    for i in range(1, count):
        total = total + a[i * rows : (i + 1) * rows]
    return total


def barrier_all(n, li):
    sem = pltpu.get_barrier_semaphore()
    for mask in range(1, n):
        pl.semaphore_signal(sem, inc=1, device_id={"lon": li ^ mask}, device_id_type=MESH)
    pl.semaphore_wait(sem, n - 1)


class Gather:
    def __init__(self, n, li, at, send, recv):
        self.n, self.li, self.at, self.send, self.recv = n, li, at, send, recv
        self.bits = [1 << i for i in range(1, n.bit_length() - 1)]

    def order(self, piece):
        return self.bits if piece % 2 == 0 else self.bits[::-1]

    def copy(self, mask, piece):
        bit = 1 if mask & 1 else [b for b in self.order(piece) if b & mask][-1]
        return pltpu.make_async_remote_copy(
            src_ref=self.at(mask ^ bit, piece),
            dst_ref=self.at(mask, piece),
            send_sem=self.send.at[mask, piece],
            recv_sem=self.recv.at[mask, piece],
            device_id={"lon": self.li ^ bit},
            device_id_type=MESH,
        )

    def forward(self, mask, piece):
        order = self.order(piece)
        used = [i for i, b in enumerate(order) if b & mask]
        for b in order[(used[-1] + 1 if used else 0):]:
            self.copy(mask | b, piece).start()
        self.copy(mask | 1, piece).start()

    def start(self, pieces):
        for piece in pieces:
            self.forward(0, piece)

    def evens(self):
        return sorted(range(2, self.n, 2), key=lambda m: bin(m).count("1"))

    def relay(self, pieces, first=True, rest=True):
        for depth in range(1, len(self.bits) + 1):
            if (first if depth == 1 else rest):
                for piece in pieces:
                    for mask in self.evens():
                        if bin(mask).count("1") == depth:
                            self.copy(mask, piece).wait_recv()
                            self.forward(mask, piece)

    def finish(self, pieces):
        for mask in range(1, self.n, 2):
            for piece in pieces:
                self.copy(mask, piece).wait_recv()

    def drain(self, pieces):
        for mask in range(1, self.n):
            for piece in pieces:
                self.copy(mask, piece).wait_send()


def front_kernel(
    n, items, here, heads, direct, fields_ref, cot_ref, ids_ref, mask_ref, patching_ref, tagging_ref, read_ref, beacon_ref, lifting_ref,
    offset_ref, scaling_ref, centre_ref, biasing_ref, place_ref, key_hbm, val_hbm, mer_hbm, proj_hbm,
    att_ref, all_out, qkv_out, lse_ref, up_out, emb_out, pooled_out, patches_out, pw_out, qrow_ref, pv_out, dpred_ref, base_ref, readp_out,
    keymap_mine, embed_mine, val_mine, kk_mine,
    keying, valuing, merging, own_w, load, seam, seam_land, seam_send, seam_recv, up_ref, usend, urecv,
    rows_ref, obuf, land, gsend, grecv, osend, orecv, keep, qkv_ref, emb_ref, pooled_ref, patches_ref, pw_ref, pv_ref, readp_ref,
):
    li = lax.axis_index("lon")
    block = lax.axis_index("batch") * n + li
    rd = val_mine.shape[0]
    width = heads * HDIM
    seq = n * here
    tile = min(seq, 512)
    rows = items * here
    lat = 2 * LATP
    wide = fields_ref.shape[2]
    loads, keeps = Moves(load), Moves(keep)
    fetch_key, fetch_val, fetch_mer = (loads.go(h, v) for h, v in ((key_hbm, keying), (val_hbm, valuing), (mer_hbm, merging)))
    if direct:
        fetch_own = [loads.go(proj_hbm.at[:, pl.ds(pl.multiple_of(p * D + li * width, width), width)], own_w.at[:, p * width : (p + 1) * width]) for p in range(3)]
    else:
        fetch_own = [loads.go(proj_hbm, own_w)]
    for i in range(items):
        seam[0, i] = fields_ref[i, :, wide - 1, :]
        seam[1, i] = cot_ref[i, :, wide - 1, :]
    barrier_all(n, li)
    east = pltpu.make_async_remote_copy(
        src_ref=seam, dst_ref=seam_land, send_sem=seam_send, recv_sem=seam_recv,
        device_id={"lon": lax.rem(li + 1, n)}, device_id_type=MESH,
    )
    east.start()

    row = lambda ref: ref[...].reshape(1, -1)
    embed = contract(places(4 * NVAR, JPAD, 0, 4, 2), patching_ref[...], ((0,), (0,)))
    embed = (embed + contract(places(NVAR, JPAD, 4 * VPAD, 1, 0), tagging_ref[...], ((0,), (0,)))).astype(BF16)
    readp_ref[...] = contract(places(4 * NOUT, 4 * VPAD, 0, 4, 2), read_ref[...], ((0,), (0,))).astype(BF16)
    keeps.go(readp_ref, readp_out)

    fetch_key.wait()
    keymap = contract(by_head(row(beacon_ref)), keying[...], ((1,), (1,)))
    qrow = folded(contract(pieces(keymap, 3), embed, ((1,), (1,))), 3)
    for h in range(HEADS):
        qrow_ref[h] = qrow[h : h + 1, :]
    fetch_val.wait()
    pv = product(embed, valuing[...]).astype(BF16)
    for g in range(n):
        pv_ref[g] = pv[:, g * width : (g + 1) * width]
    keeps.go(pv_ref, pv_out)

    spread = latitudes(lat)
    var = lax.broadcasted_iota(jnp.int32, (VPAD, NVAR), 0)
    same = (var == lax.broadcasted_iota(jnp.int32, (VPAD, NVAR), 1)).astype(BF16)
    lane = lax.broadcasted_iota(jnp.int32, (8, VPAD), 1)
    patches_ref[:, 4 * VPAD :] = jnp.ones((rows, VPAD), BF16)
    east.wait()

    def tokens(ref, which, i, choose, out):
        pixels = [seam_land[which, i]] + [ref[i, :, w, :] for w in range(wide - 1)]
        stack = jnp.concatenate([product(choose, p).astype(BF16) for p in pixels], axis=0)
        turned = contract(spread, stack, ((1,), (1,))).astype(BF16)
        for w in range(wide):
            token = turned[:, w * VPAD : (w + 1) * VPAD]
            for e in range(2):
                corner = (w % 2) * 2 + e
                at = i * here + (w // 2) * LATP
                out[at : at + LATP, corner * VPAD : (corner + 1) * VPAD] = token[e * LATP : (e + 1) * LATP]

    for i in range(items):
        tokens(cot_ref, 1, i, same, dpred_ref)
    half_rows = rows // 2
    ups = Gather(n, li, lambda slot, piece: up_ref.at[slot, pl.ds(piece * half_rows, half_rows)], usend, urecv)
    up_ref[0] = dpred_ref[...]
    ups.start([0, 1])
    base_ref[...] = jnp.sum(dpred_ref[...].astype(F32), axis=0, keepdims=True)
    cuts = 2
    share = here // cuts
    pieces_of = lambda i: list(range(cuts * i, cuts * (i + 1)))

    def at(slot, piece):
        return rows_ref.at[piece // cuts, slot, pl.ds((piece % cuts) * share, share)]

    gather = Gather(n, li, at, gsend, grecv)
    lifting = row(lifting_ref).astype(F32)
    offset, scaling, centre = (row(a).astype(F32) for a in (offset_ref, scaling_ref, centre_ref))

    for i in range(items):
        part = slice(i * here, (i + 1) * here)
        choose = (var == ids_ref[i : i + 1, :]).astype(BF16)
        tokens(fields_ref, 0, i, choose, patches_ref)
        kept = jnp.broadcast_to(mask_ref[i : i + 1, :], (8, NVAR)).astype(F32).astype(BF16)
        live = contract(kept, choose, ((1,), (1,)))
        mask = jnp.broadcast_to(jnp.where(lane < NVAR, jnp.where(live > 0.5, 0.0, -1e30), -2e30)[:1], (here, VPAD))
        patches = patches_ref[part, :].astype(F32)
        for pair in range(HEADS // 2):
            halves = []
            for h in (2 * pair, 2 * pair + 1):
                x = patches[:, : 4 * VPAD] * qrow[h : h + 1, : 4 * VPAD]
                x = x[:, : 2 * VPAD] + x[:, 2 * VPAD :]
                logits = (x[:, :VPAD] + x[:, VPAD:] + qrow[h : h + 1, 4 * VPAD :]) * FACTOR
                logits = jnp.where(mask == 0.0, logits, mask)
                grown = jnp.exp(logits - jnp.max(logits, axis=-1, keepdims=True))
                w = grown / jnp.sum(grown, axis=-1, keepdims=True)
                pw_ref[h, part, :] = w.astype(BF16)
                blended = (jnp.concatenate([w] * 5, axis=1) * patches).astype(BF16)
                halves.append(product(blended, pv[:, h * HDIM : (h + 1) * HDIM]))
            cols = slice(pair * 128, pair * 128 + 128)
            pooled_ref[part, cols] = (jnp.concatenate(halves, axis=1) + lifting[:, cols]).astype(BF16)
        if i == 0:
            fetch_mer.wait()
        emb = product(pooled_ref[part, :], merging[...]) + offset + place_ref[...].astype(F32)
        emb_ref[part, :] = emb
        normal, _ = normalize(emb)
        rows_ref[i, 0] = (normal * scaling + centre).astype(BF16)
        gather.start(pieces_of(i))
    ups.relay([0, 1])
    gather.relay(pieces_of(0))
    for src, dst in ((patches_ref, patches_out), (pw_ref, pw_out), (pooled_ref, pooled_out), (emb_ref, emb_out)):
        keeps.go(src, dst)

    one = (lax.broadcasted_iota(jnp.int32, (D, rd), 0) == block * rd + lax.broadcasted_iota(jnp.int32, (D, rd), 1)).astype(BF16)
    embed_mine[...] = product(embed, one).astype(BF16)
    val_mine[...] = contract(one, valuing[...], ((0,), (0,))).astype(BF16)
    keymap_mine[...] = jnp.dot(keymap, one.astype(F32), precision=HIGH, preferred_element_type=F32)
    kk_mine[...] = product(embed, product(keying[...], one).astype(BF16))

    def give(i, mask):
        return pltpu.make_async_remote_copy(
            src_ref=obuf.at[i, mask],
            dst_ref=land.at[li, i],
            send_sem=osend.at[i, mask],
            recv_sem=orecv.at[i, mask],
            device_id={"lon": li ^ mask},
            device_id_type=MESH,
        )

    column = lax.broadcasted_iota(jnp.int32, (D, width), 1)
    mine = (lax.broadcasted_iota(jnp.int32, (D, width), 0) == li * width + column).astype(BF16)
    biases = jnp.broadcast_to(row(biasing_ref), (8, 2 * D))
    own_bias = jnp.concatenate(
        [product(biases[:, :D], mine)[:1], jnp.zeros((1, width), F32), product(biases[:, D:], mine)[:1]], axis=1
    )
    for c in fetch_own:
        c.wait()
    for i in range(items):
        later = pieces_of(i + 1) if i + 1 < items else []
        gather.finish(pieces_of(i))
        keeps.go(rows_ref.at[i], all_out.at[i])
        joint = product(rows_ref[i].reshape(seq, D), own_w[...]) + own_bias
        qkv_ref[i] = joint.astype(BF16)
        keeps.go(qkv_ref.at[i], qkv_out.at[i])
        for t in range(seq // tile):
            outs = []
            for h in range(heads):
                q = qkv_ref[i, t * tile : (t + 1) * tile, h * HDIM : (h + 1) * HDIM] * FACTOR
                k = qkv_ref[i, :, width + h * HDIM : width + (h + 1) * HDIM]
                v = qkv_ref[i, :, 2 * width + h * HDIM : 2 * width + (h + 1) * HDIM]
                scores = contract(q, k, ((1,), (1,)))
                top = jnp.max(scores, axis=1, keepdims=True)
                grown = jnp.exp(scores - top)
                total = jnp.sum(grown, axis=1, keepdims=True)
                outs.append(product(grown.astype(BF16), v) / total)
                lse = top + jnp.log(total)
                lse_ref[i, h : h + 1, t * tile : (t + 1) * tile] = jnp.transpose(lse)
                if t == 0 and h == 0:
                    gather.relay(later)
            out = jnp.concatenate(outs, axis=1) if heads > 1 else outs[0]
            slots = range(t * (tile // here), (t + 1) * (tile // here))
            obuf[i, t * (tile // here) : (t + 1) * (tile // here)] = out.astype(BF16).reshape(tile // here, here, width)
            for mask in slots:
                if mask:
                    give(i, mask).start()
        land[li, i] = obuf[i, 0]
    ups.finish([0, 1])
    keeps.go(up_ref, up_out)
    for i in range(items):
        for mask in range(1, n):
            give(i, mask).wait_recv()
        att_ref[i * here : (i + 1) * here, :] = jnp.concatenate([land[g, i] for g in range(n)], axis=1)
    ups.drain([0, 1])
    for i in range(items):
        gather.drain(pieces_of(i))
        for mask in range(1, n):
            give(i, mask).wait_send()
    for c in keeps.started:
        c.wait()


def front(fields, cot, ids, mask, patching, tagging, reading, beacon, lifting, offset, scaling, centre, biasing, place, keying, valuing, merging, proj, rd, direct, n, items, here, heads):
    width = heads * HDIM
    seq = n * here
    rows = items * here
    vm, hbm = pl.BlockSpec(memory_space=pltpu.VMEM), pl.BlockSpec(memory_space=pl.ANY)
    shape = jax.ShapeDtypeStruct
    dma = pltpu.SemaphoreType.DMA
    low = lambda *a: pltpu.VMEM(a, BF16)
    edge = low(2, items, NVAR, 2 * LATP)
    return pl.pallas_call(
        functools.partial(front_kernel, n, items, here, heads, direct),
        in_specs=[vm] * 14 + [hbm] * 4,
        out_specs=(vm, hbm, hbm, vm, hbm, hbm, hbm, hbm, hbm, vm, hbm, vm, vm, hbm, vm, vm, vm, vm),
        out_shape=(
            shape((rows, D), BF16), shape((items, n, here, D), BF16), shape((items, seq, 3 * width), BF16), shape((items, heads, seq), F32),
            shape((n, rows, 4 * VPAD), BF16), shape((rows, D), F32), shape((rows, D), BF16), shape((rows, JPAD), BF16),
            shape((HEADS, rows, VPAD), BF16), shape((HEADS, 1, JPAD), F32), shape((n, JPAD, width), BF16), shape((rows, 4 * VPAD), BF16),
            shape((1, 4 * VPAD), F32), shape((4 * VPAD, D), BF16), shape((HEADS, rd), F32), shape((JPAD, rd), BF16), shape((rd, D), BF16), shape((JPAD, rd), F32),
        ),
        scratch_shapes=[
            low(D, D), low(D, D), low(D, D), low(D, 3 * width), dma((8,)), edge, edge, dma, dma,
            low(n, rows, 4 * VPAD), dma((n, 2)), dma((n, 2)),
            low(items, n, here, D), low(items, n, here, width), low(n, items, here, width),
            dma((n, 2 * items)), dma((n, 2 * items)), dma((items, n)), dma((items, n)), dma((2 * items + 9,)),
            low(items, seq, 3 * width), pltpu.VMEM((rows, D), F32), low(rows, D), low(rows, JPAD), low(HEADS, rows, VPAD),
            low(n, JPAD, width), low(4 * VPAD, D),
        ],
        compiler_params=pltpu.CompilerParams(collective_id=1, has_side_effects=True, vmem_limit_bytes=60 * MIB),
        name="front",
    )(fields, cot, ids, mask, patching, tagging, reading, beacon, lifting, offset, scaling, centre, biasing, place, keying, valuing, merging, proj)


def middle_kernel(
    n, items, here, heads, block,
    att_ref, emb_ref, mix_hbm, nudging_ref, rescaling_ref, recentre_ref, settle_ref, uplift_ref, baseline_ref, w1_hbm, w2_hbm, read_ref, dpred_ref,
    z_ref, sq_out, dmid_ref, do_ref, vecg_ref, uplg_ref, rows_out,
    w1, w2, mix, rows_ref, normal_ref, acc, slope_ref, upl_ref, sq_ref, gsend, grecv, load, keep,
):
    li = lax.axis_index("lon")
    rows = items * here
    width = heads * HDIM
    blocks = FF // block

    def fetch1(b):
        return pltpu.make_async_copy(w1_hbm.at[:, pl.ds(pl.multiple_of(b * block, block), block)], w1.at[b], load.at[b])

    def fetch2(b):
        return pltpu.make_async_copy(w2_hbm.at[pl.ds(pl.multiple_of(b * block, block), block)], w2.at[b], load.at[blocks + b])

    fetch_mix = pltpu.make_async_copy(mix_hbm, mix, load.at[2 * blocks])
    fetch_mix.start()
    for b in range(blocks):
        fetch1(b).start()
        fetch2(b).start()
    barrier_all(n, li)

    row = lambda ref: ref[...].reshape(1, -1).astype(F32)
    nudging, rescaling, recentre, settle = (row(a) for a in (nudging_ref, rescaling_ref, recentre_ref, settle_ref))
    uplift = row(uplift_ref)
    for b in range(blocks):
        upl_ref[b] = uplift[:, b * block : (b + 1) * block]
    quarter = rows // 4
    keeps = Moves(keep)
    every = list(range(4))
    gather = Gather(n, li, lambda slot, piece: rows_ref.at[slot, pl.ds(piece * quarter, quarter)], gsend, grecv)
    fetch_mix.wait()
    mid = emb_ref[...] + (product(att_ref[...], mix[...]) + nudging)
    dmid_ref[...] = mid
    normal, inverse = normalize(mid)
    normal_ref[...] = normal
    rows_ref[0] = (normal * rescaling + recentre).astype(BF16)
    gather.start(every)
    acc[...] = jnp.zeros_like(acc)

    def ahead(b, _):
        fetch1(b).wait()
        hidden = product(rows_ref[0], w1[b]) + upl_ref[b]
        value, slope = gelu_parts(hidden)
        slope_ref[b] = slope
        fetch2(b).wait()
        acc[...] += product(value.astype(BF16), w2[b])
        return 0

    lax.fori_loop(0, blocks, ahead, 0)
    final = (dmid_ref[...] + (acc[...] + settle)).astype(BF16)
    baseline = jnp.broadcast_to(baseline_ref[...].reshape(1, -1), (8, 4 * NOUT))
    baseline = product(baseline, places(4 * NOUT, 4 * VPAD, 0, 4, 2))[:1]
    z_ref[...] = (contract(final, read_ref[...], ((1,), (1,))) + baseline).astype(BF16)
    dpred = dpred_ref[...]
    sq_ref[:, D:] = contract(final, dpred, ((0,), (0,))).astype(BF16)
    keeps.go(sq_ref.at[:, pl.ds(D, 4 * VPAD)], sq_out.at[:, pl.ds(D, 4 * VPAD)])
    dfinal = product(dpred, read_ref[...])
    dfinal_low = dfinal.astype(BF16)
    acc[...] = jnp.zeros_like(acc)

    def back(b, _):
        dhidden = (contract(dfinal_low, w2[b], ((1,), (1,))) * slope_ref[b]).astype(BF16)
        uplg_ref[b] = jnp.sum(dhidden.astype(F32), axis=0, keepdims=True)
        acc[...] += contract(dhidden, w1[b], ((1,), (1,)))
        return 0

    gather.relay(every[:2], rest=False)
    lax.fori_loop(0, blocks // 2, back, 0)
    gather.relay(every[2:], rest=False)
    lax.fori_loop(blocks // 2, blocks, back, 0)
    gather.relay(every, first=False)
    for mask in range(0, n, 2):
        keeps.go(rows_ref.at[mask], rows_out.at[mask])
    dsecond = acc[...]
    normal = normal_ref[...]
    dmid = dfinal + norm_back(dsecond, normal, inverse, rescaling)
    dmid_ref[...] = dmid
    dmid_low = dmid.astype(BF16)
    vecg_ref[...] = jnp.concatenate([
        jnp.sum(dmid_low.astype(F32), axis=0, keepdims=True),
        jnp.sum(dsecond * normal, axis=0, keepdims=True),
        jnp.sum(dsecond, axis=0, keepdims=True),
        jnp.sum(dfinal_low.astype(F32), axis=0, keepdims=True),
    ], axis=0)
    dout = contract(dmid_low, mix[...], ((1,), (1,))).astype(BF16)
    for g in range(n):
        do_ref[g] = dout[:, g * width : (g + 1) * width].reshape(items, here, width)
    sq_ref[:, :D] = contract(att_ref[...], dmid_low, ((0,), (0,))).astype(BF16)
    keeps.go(sq_ref.at[:, pl.ds(0, D)], sq_out.at[:, pl.ds(0, D)])
    for mask in range(1, n, 2):
        for piece in every:
            gather.copy(mask, piece).wait_recv()
        keeps.go(rows_ref.at[mask], rows_out.at[mask])
    gather.drain(every)
    for c in keeps.started:
        c.wait()


def middle_part(att, emb, mixing, nudging, rescaling, recentre, settle, uplift, baseline, widening, narrowing, read, dpred, n, items, here, heads):
    rows = items * here
    width = heads * HDIM
    block = 512
    blocks = FF // block
    vm = pl.BlockSpec(memory_space=pltpu.VMEM)
    hbm = pl.BlockSpec(memory_space=pl.ANY)
    shape = jax.ShapeDtypeStruct
    return pl.pallas_call(
        functools.partial(middle_kernel, n, items, here, heads, block),
        in_specs=[vm, vm, hbm, vm, vm, vm, vm, vm, vm, hbm, hbm, vm, vm],
        out_specs=(vm, hbm, vm, vm, vm, vm, hbm),
        out_shape=(
            shape((rows, 4 * VPAD), BF16), shape((D, D + 4 * VPAD), BF16), shape((rows, D), F32),
            shape((n, items, here, width), BF16), shape((4, D), F32), shape((blocks, 1, block), F32), shape((n, rows, D), BF16),
        ),
        scratch_shapes=[
            pltpu.VMEM((blocks, D, block), BF16), pltpu.VMEM((blocks, block, D), BF16), pltpu.VMEM((D, D), BF16),
            pltpu.VMEM((n, rows, D), BF16), pltpu.VMEM((rows, D), F32), pltpu.VMEM((rows, D), F32),
            pltpu.VMEM((blocks, rows, block), F32), pltpu.VMEM((blocks, 1, block), F32), pltpu.VMEM((D, D + 4 * VPAD), BF16),
            pltpu.SemaphoreType.DMA((n, 4)), pltpu.SemaphoreType.DMA((n, 4)),
            pltpu.SemaphoreType.DMA((2 * blocks + 1,)), pltpu.SemaphoreType.DMA((n + 2,)),
        ],
        compiler_params=pltpu.CompilerParams(collective_id=2, has_side_effects=True, vmem_limit_bytes=60 * MIB),
        name="middle",
    )(att, emb, mixing, nudging, rescaling, recentre, settle, uplift, baseline, widening, narrowing, read, dpred)


def greet(n, li, count, zi):
    sem = pltpu.get_barrier_semaphore()
    for mask in range(1, n):
        pl.semaphore_signal(sem, inc=1, device_id={"lon": li ^ mask}, device_id_type=MESH)
    for mask in range(1, count):
        pl.semaphore_signal(sem, inc=1, device_id={"batch": zi ^ mask}, device_id_type=MESH)
    pl.semaphore_wait(sem, n + count - 2)


class Halving:
    def __init__(self, count, zi, flip, own, stage, land, send, recv):
        self.count, self.zi, self.own, self.stage, self.land = count, zi, own, stage, land
        self.send_sem, self.recv_sem = send, recv
        self.bits = [1 << i for i in range(count.bit_length() - 1)]
        if flip:
            self.bits = self.bits[::-1]

    def at_step(self, step):
        return [r for r in range(1, self.count) if min(i for i, b in enumerate(self.bits) if b & r) == step]

    def copy(self, r, step):
        return pltpu.make_async_remote_copy(
            src_ref=self.own(self.zi ^ r) if step == 0 else self.stage.at[r],
            dst_ref=self.land.at[r],
            send_sem=self.send_sem.at[r],
            recv_sem=self.recv_sem.at[r],
            device_id={"batch": self.zi ^ self.bits[step]},
            device_id_type=MESH,
        )

    def send(self, step):
        for r in self.at_step(step):
            self.copy(r, step).start()

    def absorb(self, step):
        for r in self.at_step(step):
            self.copy(r, step).wait_recv()
            to = r ^ self.bits[step]
            base = self.own(self.zi ^ to)[...] if step == 0 else self.stage[to]
            total = base.astype(F32) + self.land[r].astype(F32)
            if step == len(self.bits) - 1:
                return total
            self.stage[to] = total.astype(BF16)

    def drain(self):
        for step in range(len(self.bits)):
            for r in self.at_step(step):
                self.copy(r, step).wait_send()


class RowSum:
    def __init__(self, n, li, count, zi, own, land1, stage1, land2, stage2, land3, sems):
        self.n, self.li, self.count, self.zi, self.own = n, li, count, zi, own
        self.land1, self.stage1, self.land2, self.stage2, self.land3 = land1, stage1, land2, stage2, land3
        self.s1, self.r1, self.s2, self.r2, self.s3, self.r3 = sems
        self.half = n // 2

    @staticmethod
    def scratch(n, count, rows, cols):
        half = pltpu.VMEM((n // 2, count, rows, cols), BF16)
        one = pltpu.VMEM((count, rows, cols), BF16)
        lon_sem, z_sem = pltpu.SemaphoreType.DMA((n // 2,)), pltpu.SemaphoreType.DMA((count,))
        return [half, half, half, one, one, lon_sem, lon_sem, lon_sem, lon_sem, z_sem, z_sem]

    def copy1(self, j):
        return pltpu.make_async_remote_copy(
            src_ref=self.own(self.li ^ (2 * j + 1)), dst_ref=self.land1.at[j], send_sem=self.s1.at[j],
            recv_sem=self.r1.at[j], device_id={"lon": self.li ^ 1}, device_id_type=MESH,
        )

    def copy2(self, j):
        return pltpu.make_async_remote_copy(
            src_ref=self.stage1.at[j], dst_ref=self.land2.at[j], send_sem=self.s2.at[j],
            recv_sem=self.r2.at[j], device_id={"lon": self.li ^ (2 * j)}, device_id_type=MESH,
        )

    def copy3(self, r):
        return pltpu.make_async_remote_copy(
            src_ref=self.stage2.at[self.zi ^ r], dst_ref=self.land3.at[r], send_sem=self.s3.at[r],
            recv_sem=self.r3.at[r], device_id={"batch": self.zi ^ r}, device_id_type=MESH,
        )

    def core(self):
        for j in range(self.half):
            self.copy1(j).start()

    def plane(self):
        for j in list(range(1, self.half)) + [0]:
            self.copy1(j).wait_recv()
            self.stage1[j] = (self.own(self.li ^ (2 * j))[...].astype(F32) + self.land1[j].astype(F32)).astype(BF16)
            if j:
                self.copy2(j).start()

    def depth(self):
        total = self.stage1[0].astype(F32)
        for j in range(1, self.half):
            self.copy2(j).wait_recv()
            total = total + self.land2[j].astype(F32)
        self.stage2[...] = total.astype(BF16)
        for r in range(1, self.count):
            self.copy3(r).start()

    def total(self):
        total = self.stage2[self.zi].astype(F32)
        for r in range(1, self.count):
            self.copy3(r).wait_recv()
            total = total + self.land3[r].astype(F32)
        return total

    def drain(self):
        for j in range(self.half):
            self.copy1(j).wait_send()
            if j:
                self.copy2(j).wait_send()
        for r in range(1, self.count):
            self.copy3(r).wait_send()


KEPT = 5 * NVAR


def arrows(count):
    unit = 16 * count
    return -(-(KEPT + 24) // unit) * unit


def rear_kernel(
    n, count, items, here, heads, direct,
    do_ref, sq_ref, second_hbm, up_hbm, wown_hbm, nown_hbm, uplift_ref, read_ref, qkv_hbm, lse_ref, rows_hbm,
    proj_hbm, merge_hbm, emb_hbm, dmid_hbm, pooled_hbm, scaling_ref, patches_hbm, w_hbm, qrow_ref, pv_hbm, vecg_ref, uplg_ref, base_ref,
    ids_ref, z_hbm,
    nar_ref, sqo_ref, pos_ref, mer_ref, pred_ref, grad_ref, ar_ref, wcol_ref, pcol_ref,
    dpatch_ref, zsend, gsend, zland, gland, seams, wown, nown, bufa, bufb, dz, accn, accw, narg, widg, do_land, ebuf, eland, dk_acc, dv_acc, projg,
    mbuf, du3, arbuf, arland, arz, archunk, posbuf, posland, posall, wcolbuf, pcolbuf, upl, upall,
    qkv_ref, emb_ref, dmid_ref, pooled_ref, patches_ref, w_ref, pv_ref, z_ref,
    load, osend, orecv, esend, erecv, nstage, nland, nsend, nrecv, wstage, wland, wsend, wrecv, xstage, xland, xsend, xrecv,
    pstage, pland, psend, precv, qstage, qland, qsend, qrecv,
    asend, arecv, azs, azr, ags, agr, bgs, bgr, pss, psr, pgs, pgr, ws, wr, cs, cr, *sums,
):
    li, zi = lax.axis_index("lon"), lax.axis_index("batch")
    rows = items * here
    width = heads * HDIM
    seq = n * here
    rd = D // (n * count)
    hid = FF // (n * count)
    tile = 512 if seq <= 1024 else 256
    total = lambda a: jnp.sum(a, axis=0, keepdims=True)

    loads = Moves(load)
    starts = [pl.multiple_of((c * n + li) * hid, hid) for c in range(count)]
    fetch_own = [loads.go(nown_hbm.at[pl.ds(at, hid)], nown.at[pl.ds(c * hid, hid)]) for c, at in enumerate(starts)]
    if direct:
        fetch_own += [loads.go(wown_hbm.at[:, pl.ds(at, hid)], wown.at[:, c * hid : (c + 1) * hid]) for c, at in enumerate(starts)]
    else:
        fetch_own.append(loads.go(wown_hbm, wown))
    fetch_own.append(loads.go(up_hbm, dz))
    fetch_rows = [loads.go(second_hbm.at[m], bufa.at[m]) for m in range(n)]
    fetch_z = loads.go(z_hbm, z_ref)
    fetch_qkv = loads.go(qkv_hbm, qkv_ref)
    per = D // rows
    roomy = n <= 2 * per
    buf_rows, buf_proj = (bufb, bufa) if roomy else (bufa, bufb)

    def fetch_normed():
        return [loads.go(rows_hbm.at[i], buf_rows.at[pl.ds(0, n), pl.ds(i * here, here)]) for i in range(items)]

    def fetch_square(hbm, first, buf, at):
        return [loads.go(hbm.at[pl.ds(j * rows, rows), first : first + D], buf.at[at + j]) for j in range(per)]

    def fetch_joint():
        return fetch_square(proj_hbm, 0, buf_proj, 0) + fetch_square(proj_hbm, D, buf_proj, per)

    fetch_early = fetch_normed() if roomy else fetch_joint()
    fetch_late = [
        loads.go(h, v)
        for h, v in ((emb_hbm, emb_ref), (dmid_hbm, dmid_ref), (pooled_hbm, pooled_ref), (patches_hbm, patches_ref), (w_hbm, w_ref), (pv_hbm, pv_ref))
    ]
    greet(n, li, count, zi)
    nar = Halving(count, zi, False, lambda b: narg.at[b], nstage, nland, nsend, nrecv)
    cut = count // 2
    wide_a = Halving(count, zi, False, lambda b: widg.at[b, pl.ds(0, cut)], wstage, wland, wsend, wrecv)
    wide_b = Halving(count, zi, True, lambda b: widg.at[b, pl.ds(cut, cut)], xstage, xland, xsend, xrecv)
    squares = RowSum(n, li, count, zi, lambda l: sq_ref.at[:, l], *sums[:5], sums[10:16])
    merging = RowSum(n, li, count, zi, lambda l: mbuf.at[:, l], *sums[5:10], sums[16:22])
    hz = D // count // 2
    first = Halving(count, zi, False, lambda b: projg.at[pl.ds(b * 2 * hz, hz)], pstage, pland, psend, precv)
    second = Halving(count, zi, True, lambda b: projg.at[pl.ds(b * 2 * hz + hz, hz)], qstage, qland, qsend, qrecv)
    steps = len(nar.bits)

    def onward(*sums):
        for step in range(steps - 1):
            for one in sums:
                one.absorb(step)
                one.send(step + 1)

    def give_do(mask):
        return pltpu.make_async_remote_copy(
            src_ref=do_ref.at[li ^ mask], dst_ref=do_land.at[mask], send_sem=osend.at[mask], recv_sem=orecv.at[mask],
            device_id={"lon": li ^ mask}, device_id_type=MESH,
        )

    for mask in range(1, n):
        give_do(mask).start()
    do_land[0] = do_ref[li]
    squares.core()

    for c in fetch_own:
        c.wait()
    slopes = contract(nown[...], read_ref[...], ((1,), (1,))).astype(BF16)
    uplift = uplift_ref[...].reshape(1, FF).astype(F32)
    for j in range(n * count):
        upall[j] = uplift[:, j * hid : (j + 1) * hid]
    upl[...] = jnp.concatenate([upall[c * n + li] for c in range(count)], axis=1)
    for c in fetch_rows:
        c.wait()
    group_of = D // rows
    half = count * hid // 2

    def own_units(part):
        cols = slice(part * half, (part + 1) * half)
        accn[...] = jnp.zeros_like(accn)
        accw[...] = jnp.zeros_like(accw)

        def own(m, _):
            take = pl.ds(m * group_of, group_of)
            normed, upstream = bufa[take].reshape(D, D), dz[take].reshape(D, 4 * VPAD)
            value, slope = gelu_parts(product(normed, wown[:, cols]) + upl[:, cols])
            dhidden = (contract(upstream, slopes[cols], ((1,), (1,))) * slope).astype(BF16)
            accn[...] += contract(value.astype(BF16), upstream, ((0,), (0,)))
            accw[...] += contract(dhidden, normed, ((0,), (0,)))
            return 0

        lax.fori_loop(0, n // group_of, own, 0)
        for j in range(cut):
            narg[part * cut + j] = accn[j * hid : (j + 1) * hid, :].astype(BF16)
            for b in range(count):
                widg[b, part * cut + j] = accw[j * hid : (j + 1) * hid, b * (D // count) : (b + 1) * (D // count)].astype(BF16)

    squares.plane()
    own_units(0)
    wide_a.send(0)

    def give(i, mask):
        return pltpu.make_async_remote_copy(
            src_ref=ebuf.at[i, mask], dst_ref=eland.at[li, i], send_sem=esend.at[i, mask], recv_sem=erecv.at[i, mask],
            device_id={"lon": li ^ mask}, device_id_type=MESH,
        )

    fetch_qkv.wait()
    for mask in range(1, n):
        give_do(mask).wait_recv()
    for i in range(items):
        dk_acc[...] = jnp.zeros_like(dk_acc)
        dv_acc[...] = jnp.zeros_like(dv_acc)
        for t in range(seq // tile):
            part = slice(t * tile, (t + 1) * tile)
            outs = []
            do_rows = do_land[t * (tile // here) : (t + 1) * (tile // here), i].reshape(tile, width)
            for h in range(heads):
                cols = slice(h * HDIM, (h + 1) * HDIM)
                q = qkv_ref[i, part, h * HDIM : (h + 1) * HDIM] * FACTOR
                k = qkv_ref[i, :, width + h * HDIM : width + (h + 1) * HDIM]
                v = qkv_ref[i, :, 2 * width + h * HDIM : 2 * width + (h + 1) * HDIM]
                do = do_rows[:, cols]
                probs = jnp.exp(contract(q, k, ((1,), (1,))) - jnp.transpose(lse_ref[i, h : h + 1, part]))
                dprobs = contract(do, v, ((1,), (1,)))
                delta = jnp.sum(probs * dprobs, axis=1, keepdims=True)
                dscores = (probs * (dprobs - delta)).astype(BF16)
                dv_acc[h] += contract(do, probs.astype(BF16), ((0,), (0,)))
                dk_acc[h] += contract(q, dscores, ((0,), (0,)))
                outs.append(product(dscores, k) * FACTOR)
            out = jnp.concatenate(outs, axis=1) if heads > 1 else outs[0]
            ebuf[i, t * (tile // here) : (t + 1) * (tile // here), :, :width] = out.astype(BF16).reshape(tile // here, here, width)
        for h in range(heads):
            ebuf[i, :, :, width + h * HDIM : width + (h + 1) * HDIM] = jnp.transpose(dk_acc[h]).astype(BF16).reshape(n, here, HDIM)
            ebuf[i, :, :, 2 * width + h * HDIM : 2 * width + (h + 1) * HDIM] = jnp.transpose(dv_acc[h]).astype(BF16).reshape(n, here, HDIM)
        for mask in range(1, n):
            give(i, mask).start()
        eland[li, i] = ebuf[i, 0]
        if i == 0:
            onward(wide_a)
    squares.depth()
    own_units(1)
    wide_b.send(0)
    nar.send(0)
    fetch_next = fetch_joint() if roomy else fetch_normed()
    for c in fetch_early if roomy else fetch_next:
        c.wait()
    joint = jnp.zeros((D, 3 * width), F32)
    for i in range(items):
        joint = joint + contract(buf_rows[:n, i * here : (i + 1) * here].reshape(seq, D), ebuf[i].reshape(seq, 3 * width), ((0,), (0,)))
    projg[...] = joint.astype(BF16)
    fetch_third = fetch_square(proj_hbm, 2 * D, buf_rows, 0)
    fetch_m = fetch_square(merge_hbm, 0, buf_rows, per)
    first.send(0)
    second.send(0)
    for c in (fetch_next if roomy else fetch_early) + fetch_late:
        c.wait()

    normal, inverse = normalize(emb_ref[...])
    lat = 2 * LATP
    wide = pred_ref.shape[2]
    spread = latitudes(lat)

    def seam(j, src, dst):
        return pltpu.make_async_remote_copy(
            src_ref=src, dst_ref=dst, send_sem=seams.at[2 * j], recv_sem=seams.at[2 * j + 1],
            device_id={"lon": lax.rem(li + n - 1, n)}, device_id_type=MESH,
        )

    def stacked(ref, i, w):
        at = i * here + (w // 2) * LATP
        corner = (w % 2) * 2
        return jnp.concatenate([ref[at : at + LATP, (corner + e) * VPAD : (corner + e + 1) * VPAD] for e in range(2)], axis=0)

    fetch_z.wait()
    for i in range(items):
        for w in range(wide // lat):
            pixels = contract(stacked(z_ref, i, w), spread, ((0,), (0,)))[:NOUT].astype(BF16)
            if w == 0:
                zsend[i] = pixels
            else:
                pred_ref[i, :, (w - 1) * lat : w * lat] = pixels
    west_z = seam(0, zsend, zland)
    west_z.start()

    for i in range(items):
        for mask in range(1, n):
            give(i, mask).wait_recv()
    scaling = scaling_ref[...].reshape(1, -1).astype(F32)
    dnormed = jnp.zeros((rows, D), F32)
    e3_sums = []
    for p, buf, at in ((0, buf_proj, 0), (1, buf_proj, per), (2, buf_rows, 0)):
        if p == 2:
            for c in fetch_third:
                c.wait()
        e3 = jnp.concatenate(
            [eland[g, :, :, p * width : (p + 1) * width].reshape(rows, width) for g in range(n)], axis=1
        )
        e3_sums.append(total(e3.astype(F32)))
        dnormed = dnormed + contract(e3, buf[at : at + per].reshape(D, D), ((1,), (1,)))
    demb = dmid_ref[...] + norm_back(dnormed, normal, inverse, scaling)
    demb_low = demb.astype(BF16)
    summed = demb[:here]
    for i in range(1, items):
        summed = summed + demb[i * here : (i + 1) * here]
    posbuf[...] = summed.astype(BF16).reshape(count, here // count, D)

    def pos_give(r):
        return pltpu.make_async_remote_copy(
            src_ref=posbuf.at[zi ^ r], dst_ref=posland.at[r], send_sem=pss.at[r], recv_sem=psr.at[r],
            device_id={"batch": zi ^ r}, device_id_type=MESH,
        )

    def pos_share(r):
        return pltpu.make_async_remote_copy(
            src_ref=posall.at[zi], dst_ref=posall.at[zi], send_sem=pgs.at[r], recv_sem=pgr.at[r],
            device_id={"batch": zi ^ r}, device_id_type=MESH,
        )

    for r in range(1, count):
        pos_give(r).start()
    mbuf[...] = contract(pooled_ref[...], demb_low, ((0,), (0,))).astype(BF16).reshape(mbuf.shape)
    merging.core()
    for c in fetch_m:
        c.wait()
    dpooled = contract(demb_low, buf_rows[per : 2 * per].reshape(D, D), ((1,), (1,))).astype(BF16)
    vectors = jnp.concatenate([
        total(dpooled.astype(F32)), total(demb_low.astype(F32)), total(dnormed * normal), total(dnormed), e3_sums[0], e3_sums[2], vecg_ref[...],
    ] + [jnp.concatenate([uplg_ref[2 * j], uplg_ref[2 * j + 1]], axis=1) for j in range(FF // D)] + [
        jnp.concatenate([base_ref[...], jnp.zeros((1, D - 4 * VPAD), F32)], axis=1), jnp.zeros((1, D), F32),
    ], axis=0).astype(BF16)
    for g in range(n):
        du3[g] = dpooled[:, g * width : (g + 1) * width]
        arbuf[g, KEPT : KEPT + 16] = vectors[:, g * width : (g + 1) * width]
    merging.plane()
    patches = patches_ref[...].astype(F32)
    dpatch_ref[...] = jnp.zeros_like(dpatch_ref)
    lines = -(-JPAD // width)

    def pool_core(mask):
        return pltpu.make_async_remote_copy(
            src_ref=arbuf.at[li ^ mask ^ 1], dst_ref=arland.at[mask], send_sem=asend.at[mask ^ 1], recv_sem=arecv.at[mask],
            device_id={"lon": li ^ 1}, device_id_type=MESH,
        )

    def pool_give(mask):
        return pltpu.make_async_remote_copy(
            src_ref=arbuf.at[li ^ mask], dst_ref=arland.at[mask ^ 1], send_sem=asend.at[mask], recv_sem=arecv.at[mask ^ 1],
            device_id={"lon": li ^ mask}, device_id_type=MESH,
        )

    def group(mask):
        g = li ^ mask
        halves, extra = [], []
        patch_total = jnp.zeros((rows, 4 * VPAD), F32)
        du_all, pv_all = du3[g], pv_ref[g]
        for s in range(heads):
            h = g * heads + s
            w = w_ref[h].astype(F32)
            wide = jnp.concatenate([w] * 5, axis=1)
            blended = (wide * patches).astype(BF16)
            du = du_all[:, s * HDIM : (s + 1) * HDIM]
            dbl = contract(du, pv_all[:, s * HDIM : (s + 1) * HDIM], ((1,), (1,)))
            halves.append(jnp.transpose(contract(du, blended, ((0,), (0,)))))
            x = dbl * patches
            dw = x[:, :VPAD]
            for c in range(1, 5):
                dw = dw + x[:, c * VPAD : (c + 1) * VPAD]
            da = w * (dw - jnp.sum(w * dw, axis=-1, keepdims=True)) * FACTOR
            da_wide = jnp.concatenate([da] * 5, axis=1)
            line = total(da_wide * patches)
            line = jnp.concatenate([line, jnp.zeros((1, lines * width - JPAD), F32)], axis=1) if lines * width > JPAD else line
            extra += [line[:, c * width : (c + 1) * width] for c in range(lines)]
            patch_total = patch_total + (wide[:, : 4 * VPAD] * dbl[:, : 4 * VPAD] + da_wide[:, : 4 * VPAD] * qrow_ref[h][:, : 4 * VPAD])
        dpatch_ref[...] += patch_total
        both = (jnp.concatenate(halves, axis=1) if heads > 1 else halves[0]).astype(BF16)
        arbuf[g, :KEPT] = jnp.concatenate([both[c * VPAD : c * VPAD + NVAR] for c in range(5)], axis=0)
        tail = jnp.concatenate(extra + [jnp.zeros((arrows(count) - KEPT - 16 - heads * lines, width), F32)], axis=0)
        arbuf[g, KEPT + 16 :] = tail.astype(BF16)

    evens = list(range(2, n, 2)) + [0]
    for mask in evens:
        group(mask ^ 1)
        pool_core(mask).start()
    onward(wide_b, nar)
    for mask in evens:
        group(mask)
        if mask == evens[-1]:
            onward(first, second)
        pool_core(mask).wait_recv()
        if mask:
            g = li ^ mask
            arbuf[g] = (arbuf[g].astype(F32) + arland[mask].astype(F32)).astype(BF16)
            pool_give(mask).start()
    def wide_give(mask):
        return pltpu.make_async_remote_copy(
            src_ref=wcolbuf.at[li ^ mask], dst_ref=wcol_ref.at[li], send_sem=ws.at[mask], recv_sem=wr.at[mask],
            device_id={"lon": li ^ mask}, device_id_type=MESH,
        )

    def col_give(mask):
        return pltpu.make_async_remote_copy(
            src_ref=pcolbuf.at[li ^ mask], dst_ref=pcol_ref.at[li], send_sem=cs.at[mask], recv_sem=cr.at[mask],
            device_id={"lon": li ^ mask}, device_id_type=MESH,
        )

    chunk = arbuf[li].astype(F32) + arland[0].astype(F32)
    for mask in range(2, n, 2):
        pool_give(mask).wait_recv()
        chunk = chunk + arland[mask ^ 1].astype(F32)
    piece = arrows(count) // count
    archunk[...] = chunk.astype(BF16).reshape(archunk.shape)

    def z_give(r):
        return pltpu.make_async_remote_copy(
            src_ref=archunk.at[zi ^ r], dst_ref=arz.at[r], send_sem=azs.at[r], recv_sem=azr.at[r],
            device_id={"batch": zi ^ r}, device_id_type=MESH,
        )

    def z_share(r):
        return pltpu.make_async_remote_copy(
            src_ref=ar_ref.at[li, zi], dst_ref=ar_ref.at[li, zi], send_sem=ags.at[r], recv_sem=agr.at[r],
            device_id={"batch": zi ^ r}, device_id_type=MESH,
        )

    for r in range(1, count):
        z_give(r).start()
    pos_sum = posbuf[zi].astype(F32)
    for r in range(1, count):
        pos_give(r).wait_recv()
        pos_sum = pos_sum + posland[r].astype(F32)
    posall[zi] = pos_sum.astype(BF16)
    piece_sum = archunk[zi].astype(F32)
    for r in range(1, count):
        z_give(r).wait_recv()
        piece_sum = piece_sum + arz[r].astype(F32)
    ar_ref[li, zi] = piece_sum.astype(BF16)

    def l_share(mask, r):
        return pltpu.make_async_remote_copy(
            src_ref=ar_ref.at[li, zi ^ r], dst_ref=ar_ref.at[li, zi ^ r], send_sem=bgs.at[mask, r], recv_sem=bgr.at[mask, r],
            device_id={"lon": li ^ mask}, device_id_type=MESH,
        )

    def l_relay(mask, r):
        return pltpu.make_async_remote_copy(
            src_ref=ar_ref.at[li ^ mask, zi ^ r], dst_ref=ar_ref.at[li ^ mask, zi ^ r], send_sem=bgs.at[mask | 1, r], recv_sem=bgr.at[mask | 1, r],
            device_id={"lon": li ^ 1}, device_id_type=MESH,
        )

    def spread_out(r):
        for mask in range(2, n, 2):
            l_share(mask, r).start()
        l_relay(0, r).start()

    for r in range(1, count):
        z_share(r).start()
    spread_out(0)
    for r in range(1, count):
        pos_share(r).start()
    nar_ref[...] = nar.absorb(steps - 1)
    for k, one in enumerate((wide_a, wide_b)):
        w_total = one.absorb(steps - 1)
        for c in range(cut):
            turned = jnp.transpose(w_total[c]).astype(BF16)
            for l in range(n):
                wcolbuf[l, k * cut + c] = turned[l * rd : (l + 1) * rd]
    for mask in range(1, n):
        wide_give(mask).start()
    wcol_ref[li] = wcolbuf[li]
    for r in range(1, count):
        z_share(r).wait_recv()
        spread_out(r)
    merging.depth()
    for i in range(items):
        var = lax.broadcasted_iota(jnp.int32, (VPAD, NVAR), 0)
        choose = (var == ids_ref[i : i + 1, :]).astype(BF16)
        for w in range(wide // lat):
            parts = pieces(stacked(dpatch_ref, i, w), 2)
            pixels = contract(parts[:lat], spread, ((0,), (0,))) + contract(parts[lat:], spread, ((0,), (0,)))
            parts = pieces(pixels, 2)
            slots = contract(choose, parts[:VPAD], ((0,), (0,))) + contract(choose, parts[VPAD:], ((0,), (0,)))
            if w == 0:
                gsend[i] = slots
            else:
                grad_ref[i, :, (w - 1) * lat : w * lat] = slots
    west_g = seam(1, gsend, gland)
    west_g.start()
    west_z.wait()
    pred_ref[:, :, wide - lat :] = zland[...]

    sqo_ref[...] = squares.total()
    top, low = first.absorb(steps - 1).astype(BF16), second.absorb(steps - 1).astype(BF16)
    pcolbuf[...] = jnp.concatenate([top, low], axis=0).reshape(pcolbuf.shape)
    for mask in range(1, n):
        col_give(mask).start()
    pcol_ref[li] = pcolbuf[li]
    for r in range(count):
        for mask in range(2, n, 2):
            l_share(mask, r).wait_recv()
            l_relay(mask, r).start()
    for r in range(1, count):
        pos_share(r).wait_recv()
    pos_ref[...] = posall[...].reshape(here, D).astype(F32)
    mer_ref[...] = merging.total()
    for r in range(count):
        for mask in range(0, n, 2):
            l_relay(mask, r).wait_recv()
    for mask in range(1, n):
        col_give(mask).wait()
        wide_give(mask).wait()
        give_do(mask).wait_send()
        for i in range(items):
            give(i, mask).wait_send()
    for mask in range(0, n, 2):
        pool_core(mask).wait_send()
        if mask:
            pool_give(mask).wait_send()
        for r in range(count):
            l_relay(mask, r).wait_send()
            if mask:
                l_share(mask, r).wait_send()
    for r in range(1, count):
        z_give(r).wait_send()
        z_share(r).wait_send()
        pos_give(r).wait_send()
        pos_share(r).wait_send()
    for part in (first, second, nar, wide_a, wide_b, squares, merging):
        part.drain()
    west_g.wait()
    grad_ref[:, :, wide - lat :] = gland[...]


def rear_part(
    do, squares, second, up, wown, nown, uplown, read, qkv, lse, rows_all, projecting, merging, emb, dmid, pooled, scaling, patches, pool_w, qrow, pv,
    vec_grads, uplift_grads, base, ids, z, direct, n, count, items, here, heads,
):
    rows, width, seq = items * here, heads * HDIM, n * here
    rd, hid = D // (n * count), FF // (n * count)
    own = count * hid
    wide = here // LATP * 2 * 2 * LATP
    shape = jax.ShapeDtypeStruct
    vm, hbm = pl.BlockSpec(memory_space=pltpu.VMEM), pl.BlockSpec(memory_space=pl.ANY)
    cols = squares.shape[3]
    piece = arrows(count) // count
    hz = D // count // 2
    dma = pltpu.SemaphoreType.DMA
    lsem, zsem, isem, psem = dma((n,)), dma((count,)), dma((items, n)), dma((n, count))
    low = lambda *s: pltpu.VMEM(s, BF16)
    full = lambda *s: pltpu.VMEM(s, F32)
    pos = low(count, here // count, D)
    nbuf, wbuf, pbuf = low(count, hid, 4 * VPAD), low(count, count // 2, hid, D // count), low(count, hz, 3 * width)
    one, two = RowSum.scratch(n, count, rd, cols), RowSum.scratch(n, count, rd, D)
    return pl.pallas_call(
        functools.partial(rear_kernel, n, count, items, here, heads, direct),
        in_specs=[vm, vm, hbm, hbm, hbm, hbm, vm, vm, hbm, vm, hbm, hbm, hbm, hbm, hbm, hbm, vm, hbm, hbm, vm, hbm, vm, vm, vm, vm, hbm],
        out_specs=(vm,) * 9,
        out_shape=(
            shape((hid, 4 * VPAD), F32), shape((rd, cols), F32), shape((here, D), F32), shape((rd, D), F32),
            shape((items, NOUT, wide), BF16), shape((items, NVAR, wide), F32), shape((n, count, piece, width), BF16), shape((n, count, rd, hid), BF16), shape((n, rd, 3 * width), BF16),
        ),
        scratch_shapes=[
            full(rows, 4 * VPAD), low(items, NOUT, 2 * LATP), full(items, NVAR, 2 * LATP), low(items, NOUT, 2 * LATP), full(items, NVAR, 2 * LATP), dma((4,)),
            low(D, own), low(own, D), low(n, rows, D), low(2 * D // rows, rows, D), low(n, rows, 4 * VPAD), full(own // 2, 4 * VPAD), full(own // 2, D),
            low(count, hid, 4 * VPAD), low(count, count, hid, D // count), low(n, items, here, width),
            low(items, n, here, 3 * width), low(n, items, here, 3 * width), full(heads, HDIM, seq), full(heads, HDIM, seq),
            low(D, 3 * width), low(count, n, rd, D), low(n, rows, width),
            low(n, arrows(count), width), low(n, arrows(count), width), low(count, piece, width), low(count, piece, width), pos, pos, pos,
            low(n, count, rd, hid), low(n, rd, 3 * width), full(1, own), full(n * count, 1, hid),
            low(items, seq, 3 * width), full(rows, D), full(rows, D), low(rows, D), low(rows, JPAD), low(HEADS, rows, VPAD), low(n, JPAD, width), low(rows, 4 * VPAD),
            dma((2 * count + n + items + 4 * (D // rows) + 9,)), lsem, lsem, isem, isem, nbuf, nbuf, zsem, zsem, wbuf, wbuf, zsem, zsem, wbuf, wbuf, zsem, zsem,
            pbuf, pbuf, zsem, zsem, pbuf, pbuf, zsem, zsem,
            lsem, lsem, zsem, zsem, zsem, zsem, psem, psem, zsem, zsem, zsem, zsem, lsem, lsem, lsem, lsem,
        ] + one[:5] + two[:5] + one[5:] + two[5:],
        compiler_params=pltpu.CompilerParams(collective_id=3, has_side_effects=True, vmem_limit_bytes=63 * MIB + 3 * MIB // 4),
        name="rear",
    )(do, squares, second, up, wown, nown, uplown, read, qkv, lse, rows_all, projecting, merging, emb, dmid, pooled, scaling, patches, pool_w, qrow, pv, vec_grads, uplift_grads, base, ids, z)


def finish_kernel(
    n, count, heads, sum_ref, wcol_ref, pcol_ref, nar_ref, sq_ref, mer_ref, pos_ref, pred_ref, grad_ref, read_ref, keymap_ref, embed_ref, val_ref, kk_ref, beacon_ref,
    prediction_ref, fields_ref, position_ref, patching_ref, tagging_ref, beacon_out, keying_ref, valuing_ref, lifting_ref, merging_ref, offset_ref, scaling_ref,
    centre_ref, projecting_ref, biasing_ref, mixing_ref, nudging_ref, rescaling_ref, recentre_ref, widening_ref, uplift_ref,
    narrowing_ref, settle_ref, reading_ref, baseline_ref,
):
    li, zi = lax.axis_index("lon"), lax.axis_index("batch")
    block = zi * n + li
    rd = D // (n * count)
    hid = FF // (n * count)
    width = heads * HDIM
    lines = -(-JPAD // width)
    exact = lambda a, b, dims: lax.dot_general(a, b, (dims, ((), ())), precision=HIGH, preferred_element_type=F32)

    def mine(size):
        row = lax.broadcasted_iota(jnp.int32, (D, size), 0)
        col = lax.broadcasted_iota(jnp.int32, (D, size), 1)
        return (row == ((block * size + col) & (D - 1))).astype(BF16)

    lat = 2 * LATP
    for i in range(pred_ref.shape[0]):
        for w in range(pred_ref.shape[2] // lat):
            prediction_ref[i, :, w, :] = pred_ref[i, :, w * lat : (w + 1) * lat]
            fields_ref[i, :, w, :] = grad_ref[i, :, w * lat : (w + 1) * lat]
    position_ref[...] = pos_ref[...]
    merging_ref[...] = mer_ref[...]
    mixing_ref[...] = sq_ref[:, :D]
    narrowing_ref[...] = folded(product(pieces(nar_ref[...], 2), read_ref[...]), 2)
    reading_ref[...] = exact(sq_ref[:, D:], places(4 * NOUT, 4 * VPAD, 0, 4, 2).astype(F32), ((1,), (1,)))
    for g in range(n):
        for p in range(3):
            projecting_ref[:, p * D + g * width : p * D + (g + 1) * width] = pcol_ref[g, :, p * width : (p + 1) * width].astype(F32)
        for c in range(count):
            at = (c * n + g) * hid
            widening_ref[:, at : at + hid] = wcol_ref[g, c].astype(F32)

    sums = [sum_ref[g].reshape(arrows(count), width) for g in range(n)]
    vectors = jnp.concatenate([a[KEPT : KEPT + 16] for a in sums], axis=1)
    one, two, four = mine(rd), mine(2 * rd), mine(4 * rd)
    short = product(vectors, one)
    for j, ref in ((0, lifting_ref), (1, offset_ref), (2, scaling_ref), (3, centre_ref), (6, nudging_ref), (7, rescaling_ref), (8, recentre_ref), (9, settle_ref)):
        ref[...] = short[j : j + 1].reshape(rd)

    def across(start, size, select, ref):
        found = product(vectors, select)
        row = (block * size) // D
        total = jnp.zeros((1, size), F32)
        for k in range(size // rd):
            total = total + jnp.where(row == k, found[start + k : start + k + 1], 0.0)
        ref[...] = total.reshape(size)

    across(4, 2 * rd, two, biasing_ref)
    across(10, 4 * rd, four, uplift_ref)
    baseline_ref[...] = contract(vectors[:, : 4 * VPAD], places(4 * NOUT, 4 * VPAD, 0, 4, 2), ((1,), (1,)))[14:15].reshape(4 * NOUT)

    dqz = []
    for h in range(HEADS):
        base = KEPT + 16 + (h % heads) * lines
        lined = sums[h // heads]
        dqz.append(jnp.concatenate([lined[base + c : base + c + 1].astype(F32) for c in range(lines)], axis=1)[:, :JPAD])
    dqz = jnp.concatenate(dqz, axis=0)
    embed_mine, val_mine = embed_ref[...], val_ref[...]
    dembed = exact(keymap_ref[...], dqz, ((0,), (0,)))
    for g in range(n):
        blank = jnp.zeros((VPAD - NVAR, width), BF16)
        dpv = jnp.concatenate([a for c in range(5) for a in (sums[g][c * NVAR : (c + 1) * NVAR], blank)], axis=0)
        valuing_ref[:, g * width : (g + 1) * width] = contract(embed_mine, dpv, ((0,), (0,)))
        dembed = dembed + contract(val_mine[:, g * width : (g + 1) * width], dpv, ((1,), (1,)))
    patching_ref[...] = exact(dembed, places(4 * NVAR, JPAD, 0, 4, 2).astype(F32), ((1,), (1,)))
    tagging_ref[...] = dembed[:, 4 * VPAD : 4 * VPAD + NVAR]
    dkeymap = product(dqz.astype(BF16), embed_mine)
    keying_ref[...] = exact(dkeymap, by_head(beacon_ref[...].reshape(1, -1).astype(F32)), ((0,), (0,)))
    down = exact(dqz, kk_ref[...], ((1,), (0,)))
    head = lax.broadcasted_iota(jnp.int32, (HEADS, rd), 0)
    col = block * rd + lax.broadcasted_iota(jnp.int32, (HEADS, rd), 1)
    beacon_out[...] = jnp.sum(jnp.where(col >> 6 == head, down, 0.0), axis=0, keepdims=True).reshape(rd)


def finish(summed, wcol, pcol, nar, squares, mer, pos, pred, grad, read, keymap, embed, valuing, kk, beacon, n, count, heads):
    rd, hid = D // (n * count), FF // (n * count)
    shape = lambda *s: jax.ShapeDtypeStruct(s, F32)
    vec = shape(rd)
    lat = 2 * LATP
    items, wide = pred.shape[0], pred.shape[2] // lat
    return pl.pallas_call(
        functools.partial(finish_kernel, n, count, heads),
        out_shape=(
            jax.ShapeDtypeStruct((items, NOUT, wide, lat), BF16), shape(items, NVAR, wide, lat),
            shape(*pos.shape), shape(rd, 4 * NVAR), shape(rd, NVAR), vec, shape(rd, D), shape(rd, D), vec, shape(rd, D), vec, vec, vec,
            shape(rd, 3 * D), shape(2 * rd), shape(rd, D), vec, vec, vec, shape(rd, FF), shape(4 * rd), shape(hid, D), vec,
            shape(rd, 4 * NOUT), shape(4 * NOUT),
        ),
        compiler_params=pltpu.CompilerParams(vmem_limit_bytes=60 * MIB),
        name="finish",
    )(summed, wcol, pcol, nar, squares, mer, pos, pred, grad, read, keymap, embed, valuing, kk, beacon)


def per_device(
    fields, variable_ids, variable_mask, position, patching, tagging, beacon, keying, valuing, lifting,
    merging, offset, scaling, centre, projecting, biasing, mixing, nudging, rescaling, recentre,
    widening, uplift, narrowing, settle, reading, baseline, cotangent,
):
    count, lon = lax.axis_size("batch"), lax.axis_size("lon")
    zi, li = lax.axis_index("batch"), lax.axis_index("lon")
    items, cols_dev, lat = fields.shape[0], fields.shape[2], fields.shape[3]
    upatch = cols_dev // 2
    here = upatch * LATP
    heads = HEADS // lon
    width = heads * HDIM
    rows_dev = D // (count * lon)
    hid = FF // (count * lon)
    f = lambda a: a.astype(F32)

    columns = lambda a, start, size: lax.dynamic_slice_in_dim(a, start, size, 1)
    direct_heads, direct_hidden = width % 128 == 0, hid % 128 == 0
    proj_own = projecting if direct_heads else jnp.concatenate([columns(projecting, p * D + li * width, width) for p in range(3)], axis=1)
    wide_own = widening if direct_hidden else jnp.concatenate([columns(widening, (c * lon + li) * hid, hid) for c in range(count)], axis=1)
    (
        attended, normed_all, joint, lse, dpred_all, embedded, pooled, patches, pool_w, qrow, pv, dpred, base, reading_p, keymap_mine, embed_mine, val_mine, kk_mine,
    ) = front(
        fields, cotangent, variable_ids, variable_mask, patching.T, tagging.T, reading.T, beacon, lifting, offset, scaling, centre, biasing,
        position.reshape(here, D), keying, valuing, merging, proj_own, rows_dev, direct_heads, lon, items, here, heads,
    )
    outputs, squares, dmiddle, do, vec_grads, uplift_grads, second_all = middle_part(
        attended, embedded, mixing, nudging, rescaling, recentre, settle, uplift, baseline, widening, narrowing, reading_p, dpred,
        lon, items, here, heads,
    )
    nar, squares, pos, mer, prediction, fields_gradient, summed, wide_cols, joint_cols = rear_part(
        do, squares.reshape(count, lon, rows_dev, -1), second_all, dpred_all, wide_own, narrowing, uplift, reading_p,
        joint, lse, normed_all, projecting, merging, embedded, dmiddle, pooled, scaling, patches, pool_w, qrow, pv, vec_grads, uplift_grads, base,
        variable_ids, outputs, direct_hidden, lon, count, items, here, heads,
    )
    outs = list(finish(
        summed, wide_cols, joint_cols, nar, squares, mer, pos, prediction, fields_gradient, reading_p, keymap_mine, embed_mine, val_mine, kk_mine, beacon,
        lon, count, heads,
    ))
    outs[2] = outs[2].reshape(upatch, LATP, D)
    return tuple(outs)


def solution(mesh):
    both = ("batch", "lon")
    image, matrix, vector = P("batch", None, "lon", None), P(both, None), P(both)
    return jax.shard_map(
        per_device,
        mesh=mesh,
        in_specs=(image, P("batch", None), P("batch", None), P("lon", None, None)) + (P(),) * 22 + (image,),
        out_specs=(
            image, image, P("lon", None, None), matrix, matrix, vector, matrix, matrix, vector, matrix, vector,
            vector, vector, matrix, vector, matrix, vector, vector, vector, matrix, vector, matrix, vector, matrix, P(),
        ),
        check_vma=False,
    )
```
